128 devices in a mesh: dp: 16 (over y, z_hi, core), tensor: 8 (over z_lo, x).
Axes of the slice: x: 4, y: 4, z: 4 (z_hi: 2, z_lo: 2; z = z_hi * 2 + z_lo), core: 2. Of those that a mesh axis runs over, the one named last changes fastest.
Arguments:
- tokens: bfloat16 [16384, 2048], P(('dp', 'tensor')), may hold values from -6 to 6
- segment: int32 [16384], P('dp'), may hold values from -1024 to 2, as said below
- ln_gain: bfloat16 [2048], replicated, may hold values from 0.099609375 to 1.8984375
- ln_bias: bfloat16 [2048], replicated, may hold values from -3 to 3
- w_qkv: bfloat16 [2048, 3, 2048], P(None, None, 'tensor'), may hold values from -0.125 to 0.125
- b_qkv: bfloat16 [3, 2048], P(None, 'tensor'), may hold values from -3 to 3
- w_out: bfloat16 [2048, 2048], P('tensor'), may hold values from -0.5 to 0.5
- b_out: bfloat16 [2048], replicated, may hold values from -1.75 to 1.75
- w_up: bfloat16 [2048, 8192], P(None, 'tensor'), may hold values from -0.125 to 0.125
- b_up: bfloat16 [8192], P('tensor'), may hold values from -3 to 3
- w_down: bfloat16 [8192, 2048], P('tensor'), may hold values from -0.0625 to 0.0625
- b_down: bfloat16 [2048], replicated, may hold values from -1.75 to 1.75
- cotangent: bfloat16 [16384, 2048], P(('dp', 'tensor')), may hold values from -6 to 6
Outputs:
- output: bfloat16 [16384, 2048], P(('dp', 'tensor'))
- input_grad: bfloat16 [16384, 2048], P(('dp', 'tensor'))
- grad_ln_gain: float32 [2048], replicated
- grad_ln_bias: float32 [2048], replicated
- grad_w_qkv: float32 [2048, 3, 2048], P(None, None, 'tensor')
- grad_b_qkv: float32 [3, 2048], P(None, 'tensor')
- grad_w_out: float32 [2048, 2048], P('tensor')
- grad_b_out: float32 [2048], replicated
- grad_w_up: float32 [2048, 8192], P(None, 'tensor')
- grad_b_up: float32 [8192], P('tensor')
- grad_w_down: float32 [8192, 2048], P('tensor')
- grad_b_down: float32 [2048], replicated
The draws below stay inside these ranges and needn't reach their ends.
Inputs may be any that keep to these rules, and one draw needn't show every extreme that they name: `segment`: within each group the slots of each device that hold tokens come first and the rest of its 128 slots are padding, with distinct negative ids, the slot at index k of the group having id -(k + 1); the last slot of every group is padding; the tokens of a group form three whole sequences with ids 0, 1, 2 in order, the first lying within the group's first device and the last within its last device.
All inputs are finite; a program needn't handle non-finite values.
Results may differ from the reference program's by a relative error of at most 0.012.
The reference program's roundings to bfloat16 on the way count: a program that leaves them out, or rounds other values in their place, can miss the bound.
Values may be sent and summed in bfloat16 or wider, within the bound.
A program may use at most 192 MiB of HBM per device.

```python
import jax
import jax.numpy as jnp
from jax import lax

D = 2048
FF = 8192
HEAD_DIM = 64
ROT = 32
HEADS = 32
TOK_DEV = 128
GRP_TOK = 1024
TOKENS = 16384


def draw_segment(key, part):
    key = jax.random.fold_in(key, 7)
    key_pad, key_head, key_tail = jax.random.split(key, 3)
    groups = TOKENS // GRP_TOK
    devices_group = GRP_TOK // TOK_DEV
    pad_counts = jax.random.randint(key_pad, (groups, devices_group), 0, TOK_DEV // 8 + 1)
    pad_counts = jnp.concatenate([pad_counts[:, :-1], jnp.maximum(pad_counts[:, -1:], 1)], axis=1).astype(jnp.int32)
    slot_index = jnp.arange(GRP_TOK, dtype=jnp.int32) % TOK_DEV
    device_index = jnp.arange(GRP_TOK, dtype=jnp.int32) // TOK_DEV
    is_valid = slot_index[None, :] < TOK_DEV - pad_counts[:, device_index]
    valid_rank = jnp.cumsum(is_valid.astype(jnp.int32), axis=1).astype(jnp.int32) - 1
    valid_count = jnp.sum(is_valid.astype(jnp.int32), axis=1, keepdims=True).astype(jnp.int32)
    head_length = jax.random.randint(key_head, (groups, 1), TOK_DEV // 8, TOK_DEV // 4 + 1)
    tail_length = jax.random.randint(key_tail, (groups, 1), TOK_DEV // 8, TOK_DEV // 4 + 1)
    segment_id = (valid_rank >= head_length).astype(jnp.int32) + (valid_rank >= valid_count - tail_length).astype(jnp.int32)
    pad_ids = -(jnp.arange(GRP_TOK, dtype=jnp.int32) + 1)
    return jnp.where(is_valid, segment_id, pad_ids[None, :]).reshape(TOKENS).astype(jnp.int32)


def shard_levels(stream_key, extent, shards, least, largest):
    factor_of = 1.0
    for dim, shards_of in shards:
        draws = jax.random.uniform(jax.random.fold_in(jax.random.fold_in(stream_key, 6), dim), (shards_of,), jnp.float32, least / len(shards), largest / len(shards))
        factor_of = factor_of * jnp.repeat(jnp.exp(draws), extent[dim] // shards_of).reshape((-1,) + (1,) * (len(extent) - 1 - dim))
    return factor_of


def normal_values(own_key, shape, deviation, most, shards=(), held_as=jnp.bfloat16):
    values = deviation * jax.random.normal(own_key, shape, jnp.float32)
    if shards:
        values = values * shard_levels(own_key, shape, shards, -0.22, 0.18)
    return jnp.clip(values, -most, most).astype(held_as)


def setup_inputs(seed: int = 0) -> dict:
    key_list = jax.random.split(jax.random.key(seed), 14)
    tokens = normal_values(key_list[0], (TOKENS, D), 1.0, 6.0, ((0, 128),))
    segment = draw_segment(jax.random.fold_in(key_list[13], 71), 0)
    ln_gain = jnp.clip(1.0 + 0.18 * jax.random.normal(key_list[2], (D,), jnp.float32), 0.099609375, 1.8984375).astype(jnp.bfloat16)
    ln_bias = normal_values(key_list[3], (D,), 0.5, 3.0)
    w_qkv = normal_values(key_list[4], (D, 3, D), D ** -0.5, 0.125, ((2, 8),))
    b_qkv = normal_values(key_list[5], (3, D), 0.5, 3.0, ((1, 8),))
    w_out = normal_values(key_list[6], (D, D), (max(D // 16, 2)) ** -0.5, 0.5, ((0, 8),))
    b_out = normal_values(key_list[7], (D,), 0.3, 1.75)
    w_up = normal_values(key_list[8], (D, FF), D ** -0.5, 0.125, ((1, 8),))
    b_up = normal_values(key_list[9], (FF,), 0.5, 3.0, ((0, 8),))
    w_down = normal_values(key_list[10], (FF, D), FF ** -0.5, 0.0625, ((0, 8),))
    b_down = normal_values(key_list[11], (D,), 0.3, 1.75)
    cotangent = normal_values(key_list[12], (TOKENS, D), 1.0, 6.0, ((0, 128),))
    return {"tokens": tokens, "segment": segment, "ln_gain": ln_gain, "ln_bias": ln_bias, "w_qkv": w_qkv, "b_qkv": b_qkv, "w_out": w_out, "b_out": b_out, "w_up": w_up, "b_up": b_up, "w_down": w_down, "b_down": b_down, "cotangent": cotangent}


EPSILON = 1e-05
HIGHEST = lax.Precision.HIGHEST

@jax.custom_vjp
def low(v):
    return lax.optimization_barrier(v.astype(jnp.bfloat16)).astype(jnp.float32)

@jax.custom_vjp
def low_back(v):
    return v

def low_keep(v):
    return (low(v), None)

def low_pass(kept, grad):
    return (grad,)

def back_keep(v):
    return (v, None)

def back_low(kept, grad):
    return (low(grad),)
low.defvjp(low_keep, low_pass)
low_back.defvjp(back_keep, back_low)

def positions_of(segment):
    is_valid = segment >= 0
    valid_rank = jnp.cumsum(is_valid.astype(jnp.int32)).astype(jnp.int32) - 1
    seen = lax.cummax(jnp.where(is_valid, segment, -1).astype(jnp.int32), axis=0)
    before = jnp.concatenate([jnp.full((1,), -1, jnp.int32), seen[:-1]])
    starts = is_valid & (segment > before)
    start_rank = lax.cummax(jnp.where(starts, valid_rank, -1).astype(jnp.int32), axis=0)
    return jnp.where(is_valid, valid_rank - start_rank, 0).astype(jnp.int32)

def rotary_tables(position):
    exponent = jnp.arange(ROT // 2, dtype=jnp.float32) * (2.0 / ROT)
    inverse = jnp.power(10000.0, -exponent)
    angle = position.astype(jnp.float32)[:, None] * inverse[None, :]
    return (jnp.cos(angle)[:, None, :], jnp.sin(angle)[:, None, :])

def rotate(vectors, cosine_table, sine_table):
    half_rot = ROT // 2
    first_part = vectors[..., :half_rot]
    second_part = vectors[..., half_rot:ROT]
    return jnp.concatenate([first_part * cosine_table - second_part * sine_table, second_part * cosine_table + first_part * sine_table, vectors[..., ROT:]], axis=-1)

def attend(packed):
    queries, key_rows, value_rows, segment = packed
    scores = jnp.einsum('ihd,jhd->hij', queries, key_rows, precision=HIGHEST) * HEAD_DIM ** (-0.5)
    scores = low_back(scores)
    position = jnp.arange(segment.shape[0], dtype=jnp.int32)
    allowed = (segment[:, None] == segment[None, :]) & (position[:, None] >= position[None, :])
    scores = jnp.where(allowed[None], scores, -1e+30)
    row_max = lax.optimization_barrier(jnp.max(scores, axis=2, keepdims=True))
    exponent = jnp.exp(scores - row_max)
    probs = low(exponent / lax.optimization_barrier(jnp.sum(exponent, axis=2, keepdims=True)))
    return jnp.einsum('hij,jhd->ihd', probs, value_rows, precision=HIGHEST)

def layer(tokens, ln_gain, ln_bias, w_qkv, b_qkv, w_out, b_out, w_up, b_up, w_down, b_down, segment):
    groups = TOKENS // GRP_TOK
    centered = tokens - lax.optimization_barrier(jnp.mean(tokens, axis=1, keepdims=True))
    unit_rows = centered * lax.rsqrt(lax.optimization_barrier(jnp.mean(centered * centered, axis=1, keepdims=True)) + EPSILON)
    normed = low(unit_rows * ln_gain + ln_bias)
    qkv_pre = low_back(jnp.einsum('td,dcf->tcf', normed, w_qkv, precision=HIGHEST) + b_qkv)
    shaped = qkv_pre.reshape(TOKENS, 3, HEADS, HEAD_DIM)
    position = jax.vmap(positions_of)(segment.reshape(groups, GRP_TOK)).reshape(TOKENS)
    cosine_table, sine_table = rotary_tables(position)
    queries = low(rotate(shaped[:, 0], cosine_table, sine_table))
    key_rows = low(rotate(shaped[:, 1], cosine_table, sine_table))
    value_rows = low(shaped[:, 2])
    grouped = (queries.reshape(groups, GRP_TOK, HEADS, HEAD_DIM), key_rows.reshape(groups, GRP_TOK, HEADS, HEAD_DIM), value_rows.reshape(groups, GRP_TOK, HEADS, HEAD_DIM), segment.reshape(groups, GRP_TOK))
    attended = lax.map(jax.checkpoint(attend), grouped)
    heads_out = low(low_back(attended.reshape(TOKENS, D)))
    up_pre = low_back(jnp.dot(normed, w_up, precision=HIGHEST) + b_up)
    activated = low(jax.nn.gelu(up_pre, approximate=True))
    attn_branch = jnp.dot(heads_out, w_out, precision=HIGHEST) + b_out
    mlp_branch = jnp.dot(activated, w_down, precision=HIGHEST) + b_down
    return tokens + attn_branch + mlp_branch

def reference(tokens, segment, ln_gain, ln_bias, w_qkv, b_qkv, w_out, b_out, w_up, b_up, w_down, b_down, cotangent):
    floats = tuple((array_in.astype(jnp.float32) for array_in in (tokens, ln_gain, ln_bias, w_qkv, b_qkv, w_out, b_out, w_up, b_up, w_down, b_down)))

    def forward(*params):
        return layer(*params, segment)
    result, pullback = jax.vjp(forward, *floats)
    grads = pullback(cotangent.astype(jnp.float32))
    return (result.astype(jnp.bfloat16), grads[0].astype(jnp.bfloat16), grads[1], grads[2], grads[3], grads[4], grads[5], grads[6], grads[7], grads[8], grads[9], grads[10])
```

```python
import jax
import jax.numpy as jnp
from jax import lax
from jax.experimental import pallas as pl
from jax.experimental.pallas import tpu as pltpu
from jax.sharding import PartitionSpec as P

HEAD_DIM = 64
ROT = 32
EPSILON = 1e-05
MESH = pl.DeviceIdType.MESH
BF = jnp.bfloat16
F32 = jnp.float32
NP = 24
DP_STAGES = 8


def neighbours():
    dp = lax.axis_index("dp")
    tensor = lax.axis_index("tensor")
    y, zh, core = dp // 4, (dp // 2) % 2, dp % 2
    zl, x = tensor // 4, tensor % 4
    yl, yr, yo = (y + 3) % 4, (y + 1) % 4, (y + 2) % 4
    xl, xr, xo = (x + 3) % 4, (x + 1) % 4, (x + 2) % 4
    where = dict(y=y, core=core, zl=zl, x=x, yl=yl, yr=yr, yo=yo, xl=xl, xr=xr, xo=xo)
    where["dev_yl"] = (yl * 4 + zh * 2 + core, tensor)
    where["dev_yr"] = (yr * 4 + zh * 2 + core, tensor)
    where["dev_zh"] = (y * 4 + (1 - zh) * 2 + core, tensor)
    where["dev_core"] = (y * 4 + zh * 2 + 1 - core, tensor)
    where["dev_xl"] = (dp, zl * 4 + xl)
    where["dev_xr"] = (dp, zl * 4 + xr)
    where["dev_zl"] = (dp, (1 - zl) * 4 + x)
    return where


def greet(devices):
    barrier = pltpu.get_barrier_semaphore()
    for device in devices:
        pl.semaphore_signal(barrier, inc=1, device_id=device, device_id_type=MESH)
    pl.semaphore_wait(barrier, len(devices))


def rcopy(src, dst, send, recv, device):
    return pltpu.make_async_remote_copy(
        src_ref=src, dst_ref=dst, send_sem=send, recv_sem=recv, device_id=device, device_id_type=MESH
    )


def rows_at(index, size, count=None):
    return pl.ds(pl.multiple_of(index * size, size), size if count is None else count)


class GradSum:
    def scratch():
        return [
            pltpu.VMEM((2, 1024, 256), BF),
            pltpu.VMEM((4, 512, 256), BF),
            pltpu.VMEM((4, 512, 256), BF),
            pltpu.VMEM((4, 2, 64, 256), BF),
            pltpu.VMEM((4, 2, 128, 256), BF),
            pltpu.VMEM((4, 128, 256), BF),
            pltpu.VMEM((4, 128, 256), BF),
            pltpu.VMEM((4, 128, 256), BF),
            pltpu.SemaphoreType.DMA((11, 4)),
            pltpu.SemaphoreType.DMA((11, 4)),
            pltpu.SemaphoreType.DMA((4,)),
        ]

    def __init__(self, at, out, scratch):
        self.at, self.out = at, out
        (self.own, self.other, self.half, self.r1, self.r2, self.zs, self.zr, self.full,
         self.send, self.recv, self.local) = scratch

    def core_copy(self, p):
        s, at = p % 4, self.at
        return rcopy(self.own.at[p % 2, rows_at(1 - at["core"], 512)], self.other.at[s],
                     self.send.at[0, s], self.recv.at[0, s], at["dev_core"])

    def first_copies(self, p):
        s, at = p % 4, self.at
        top = self.half.at[s, rows_at(at["yo"], 128, 64)]
        low = self.half.at[s, pl.ds(pl.multiple_of(at["yo"] * 128 + 64, 64), 64)]
        return (rcopy(top, self.r1.at[s, 0], self.send.at[1, s], self.recv.at[1, s], at["dev_yr"]),
                rcopy(low, self.r1.at[s, 1], self.send.at[2, s], self.recv.at[2, s], at["dev_yl"]))

    def second_copies(self, p):
        s, at = p % 4, self.at
        return (rcopy(self.half.at[s, rows_at(at["yr"], 128)], self.r2.at[s, 0],
                      self.send.at[3, s], self.recv.at[3, s], at["dev_yr"]),
                rcopy(self.half.at[s, rows_at(at["yl"], 128)], self.r2.at[s, 1],
                      self.send.at[4, s], self.recv.at[4, s], at["dev_yl"]))

    def z_copy(self, p):
        s = p % 4
        return rcopy(self.zs.at[s], self.zr.at[s], self.send.at[5, s], self.recv.at[5, s],
                     self.at["dev_zh"])

    def back_first(self, p):
        s, at = p % 4, self.at
        mine = self.out.at[p, rows_at(at["core"] * 4 + at["y"], 128)]
        return (rcopy(self.full.at[s], mine, self.send.at[6, s], self.recv.at[6, s], at["dev_yr"]),
                rcopy(self.full.at[s], mine, self.send.at[7, s], self.recv.at[7, s], at["dev_yl"]),
                pltpu.make_async_copy(self.full.at[s], mine, self.local.at[s]))

    def back_second(self, p):
        s, at = p % 4, self.at
        top = self.out.at[p, rows_at(at["core"] * 4 + at["yl"], 128, 64)]
        low = self.out.at[p, pl.ds(pl.multiple_of((at["core"] * 4 + at["yr"]) * 128 + 64, 64), 64)]
        return (rcopy(top, top, self.send.at[9, s], self.recv.at[9, s], at["dev_yr"]),
                rcopy(low, low, self.send.at[10, s], self.recv.at[10, s], at["dev_yl"]))

    def back_core(self, p):
        s, at = p % 4, self.at
        mine = self.out.at[p, rows_at(at["core"], 512)]
        return rcopy(mine, mine, self.send.at[8, s], self.recv.at[8, s], at["dev_core"])

    def send_piece(self, p):
        self.core_copy(p).start()

    def add_core(self, p):
        s = p % 4
        self.core_copy(p).wait()

        @pl.loop(0, 4)
        def _(j):
            rows = rows_at(j, 128)
            mine = self.own[p % 2, pl.ds(pl.multiple_of(self.at["core"] * 512 + j * 128, 128), 128)]
            self.half[s, rows] = (mine.astype(F32) + self.other[s, rows].astype(F32)).astype(BF)

        for copy in self.first_copies(p):
            copy.start()

    def add_first(self, p):
        s, at = p % 4, self.at
        for copy in self.first_copies(p):
            copy.wait()
        top = rows_at(at["yr"], 128, 64)
        low = pl.ds(pl.multiple_of(at["yl"] * 128 + 64, 64), 64)
        self.half[s, top] = (self.half[s, top].astype(F32) + self.r1[s, 0].astype(F32)).astype(BF)
        self.half[s, low] = (self.half[s, low].astype(F32) + self.r1[s, 1].astype(F32)).astype(BF)
        for copy in self.second_copies(p):
            copy.start()

    def add_second(self, p):
        s = p % 4
        for copy in self.second_copies(p):
            copy.wait()
        mine = self.half[s, rows_at(self.at["y"], 128)].astype(F32)
        self.zs[s] = (mine + self.r2[s, 0].astype(F32) + self.r2[s, 1].astype(F32)).astype(BF)
        self.z_copy(p).start()

    def add_z(self, p):
        s = p % 4
        self.z_copy(p).wait()
        self.full[s] = (self.zs[s].astype(F32) + self.zr[s].astype(F32)).astype(BF)
        for copy in self.back_first(p):
            copy.start()

    def forward_y(self, p):
        for copy in self.back_first(p):
            copy.wait()
        for copy in self.back_second(p):
            copy.start()

    def forward_core(self, p):
        for copy in self.back_second(p):
            copy.wait()
        self.back_core(p).start()

    def finish(self, p):
        self.back_core(p).wait()

    def steps(self, t, begin=0):
        for lag, step in enumerate((self.add_core, self.add_first, self.add_second, self.add_z,
                                    self.forward_y, self.forward_core, self.finish), 1):
            p = t - lag
            pl.when((p >= 0) & (p < NP))(lambda step=step, p=p: step(p))


def sum_kernel(pieces, out, copied, *scratch):
    at = neighbours()
    greet([at["dev_yl"], at["dev_yr"], at["dev_zh"], at["dev_core"]])
    engine = GradSum(at, out, scratch)

    @pl.loop(0, NP + DP_STAGES - 1)
    def _(t):
        engine.steps(t)

        @pl.when(t < NP)
        def _():
            copy = pltpu.make_async_copy(pieces.at[t], engine.own.at[t % 2], copied)
            copy.start()
            copy.wait()
            engine.send_piece(t)


def sum_pieces(pieces):
    return pl.pallas_call(
        sum_kernel,
        out_shape=jax.ShapeDtypeStruct((NP, 1024, 256), BF),
        in_specs=[pl.BlockSpec(memory_space=pl.ANY)],
        out_specs=pl.BlockSpec(memory_space=pl.ANY),
        scratch_shapes=[pltpu.SemaphoreType.DMA] + GradSum.scratch(),
        compiler_params=pltpu.CompilerParams(
            collective_id=0, has_side_effects=True, vmem_limit_bytes=32 << 20),
        cost_estimate=pl.CostEstimate(flops=0, bytes_accessed=2 * NP * 1024 * 512, transcendentals=0),
    )(pieces)


def to_pieces(grad_w_down, grad_w_out, grad_w_up, grad_w_qkv):
    parts = [
        grad_w_down.astype(BF).reshape(1024, 8, 256).transpose(1, 0, 2),
        grad_w_out.astype(BF).reshape(256, 8, 256).transpose(1, 0, 2).reshape(2, 1024, 256),
        grad_w_up.astype(BF).reshape(2, 1024, 4, 256).transpose(2, 0, 1, 3).reshape(8, 1024, 256),
        grad_w_qkv.astype(BF).reshape(2, 1024, 3, 256).transpose(2, 0, 1, 3).reshape(6, 1024, 256),
    ]
    return jnp.concatenate(parts, axis=0)


def from_pieces(total):
    down = total[:8].transpose(1, 0, 2).reshape(1024, 2048).astype(F32)
    out = total[8:10].reshape(8, 256, 256).transpose(1, 0, 2).reshape(256, 2048).astype(F32)
    up = total[10:18].reshape(4, 2048, 256).transpose(1, 0, 2).reshape(2048, 1024).astype(F32)
    qkv = total[18:].reshape(3, 2048, 256).transpose(1, 0, 2).astype(F32)
    return down, out, up, qkv


def positions_of(segment):
    is_valid = segment >= 0
    valid_rank = jnp.cumsum(is_valid.astype(jnp.int32)) - 1
    seen = lax.cummax(jnp.where(is_valid, segment, -1), axis=0)
    before = jnp.concatenate([jnp.full((1,), -1, jnp.int32), seen[:-1]])
    starts = is_valid & (segment > before)
    start_rank = lax.cummax(jnp.where(starts, valid_rank, -1), axis=0)
    return jnp.where(is_valid, valid_rank - start_rank, 0)


def rotary_tables(position):
    exponent = jnp.arange(ROT // 2, dtype=jnp.float32) * (2.0 / ROT)
    inverse = jnp.power(10000.0, -exponent)
    angle = position.astype(jnp.float32)[:, None] * inverse[None, :]
    return (jnp.cos(angle)[:, None, :], jnp.sin(angle)[:, None, :])


def rotate(vectors, cosine_table, sine_table):
    half_rot = ROT // 2
    first_part = vectors[..., :half_rot]
    second_part = vectors[..., half_rot:ROT]
    return jnp.concatenate(
        [
            first_part * cosine_table - second_part * sine_table,
            second_part * cosine_table + first_part * sine_table,
            vectors[..., ROT:],
        ],
        axis=-1,
    )


def unrotate(grads_in, cosine_table, sine_table):
    half_rot = ROT // 2
    first_part = grads_in[..., :half_rot]
    second_part = grads_in[..., half_rot:ROT]
    return jnp.concatenate(
        [
            first_part * cosine_table + second_part * sine_table,
            second_part * cosine_table - first_part * sine_table,
            grads_in[..., ROT:],
        ],
        axis=-1,
    )


def block_scores(queries, key_rows, segment, begin_row, end_row):
    scale = HEAD_DIM ** (-0.5)
    scores = (
        jnp.einsum(
            "ihd,jhd->hij",
            queries[begin_row:end_row],
            key_rows[:end_row],
            preferred_element_type=jnp.float32,
        )
        * scale
    )
    position = jnp.arange(end_row, dtype=jnp.int32)
    allowed = (segment[begin_row:end_row, None] == segment[None, :end_row]) & (
        position[begin_row:end_row, None] >= position[None, :]
    )
    return (scores, allowed[None])


def attend_forward(queries, key_rows, value_rows, segment):
    group_rows = queries.shape[0]
    block_rows = min(512, group_rows)
    out_blocks = []
    lse_blocks = []
    for begin_row in range(0, group_rows, block_rows):
        end_row = begin_row + block_rows
        scores, allowed = block_scores(queries, key_rows, segment, begin_row, end_row)
        scores = jnp.where(allowed, scores, -1e30)
        row_max = jnp.max(scores, axis=2, keepdims=True)
        exponent = jnp.exp(scores - row_max)
        row_total = jnp.sum(exponent, axis=2, keepdims=True)
        probs = (exponent / row_total).astype(jnp.bfloat16)
        out_blocks.append(
            jnp.einsum(
                "hij,jhd->ihd", probs, value_rows[:end_row], preferred_element_type=jnp.float32
            )
        )
        lse_blocks.append(row_max + jnp.log(row_total))
    return (jnp.concatenate(out_blocks, axis=0), jnp.concatenate(lse_blocks, axis=1))


def attend_backward(queries, key_rows, value_rows, segment, lse_all, grad_heads):
    group_rows = queries.shape[0]
    block_rows = min(512, group_rows)
    scale = HEAD_DIM ** (-0.5)
    grad_keys = jnp.zeros(key_rows.shape, jnp.float32)
    grad_values = jnp.zeros(value_rows.shape, jnp.float32)
    query_blocks = []
    for begin_row in range(0, group_rows, block_rows):
        end_row = begin_row + block_rows
        scores, allowed = block_scores(queries, key_rows, segment, begin_row, end_row)
        probs_exact = jnp.where(allowed, jnp.exp(scores - lse_all[:, begin_row:end_row]), 0.0)
        grad_block = grad_heads[begin_row:end_row]
        grad_probs = jnp.einsum(
            "ihd,jhd->hij", grad_block, value_rows[:end_row], preferred_element_type=jnp.float32
        )
        delta = jnp.sum(probs_exact * grad_probs, axis=2, keepdims=True)
        grad_scores = (probs_exact * (grad_probs - delta)).astype(jnp.bfloat16)
        query_blocks.append(
            jnp.einsum(
                "hij,jhd->ihd", grad_scores, key_rows[:end_row], preferred_element_type=jnp.float32
            )
            * scale
        )
        grad_keys = grad_keys.at[:end_row].add(
            jnp.einsum(
                "hij,ihd->jhd",
                grad_scores,
                queries[begin_row:end_row],
                preferred_element_type=jnp.float32,
            )
            * scale
        )
        grad_values = grad_values.at[:end_row].add(
            jnp.einsum(
                "hij,ihd->jhd",
                probs_exact.astype(jnp.bfloat16),
                grad_block,
                preferred_element_type=jnp.float32,
            )
        )
    return (jnp.concatenate(query_blocks, axis=0), grad_keys, grad_values)


def gelu_tanh(values_in):
    return jax.nn.gelu(values_in, approximate=True)


def on_device(
    tokens,
    segment,
    ln_gain,
    ln_bias,
    w_qkv,
    b_qkv,
    w_out,
    b_out,
    w_up,
    b_up,
    w_down,
    b_down,
    cotangent,
):
    inputs = tokens.astype(jnp.float32)
    centered = inputs - jnp.mean(inputs, axis=1, keepdims=True)
    rstd_rows = lax.rsqrt(jnp.mean(centered * centered, axis=1, keepdims=True) + EPSILON)
    unit_rows = centered * rstd_rows
    gain_float = ln_gain.astype(jnp.float32)
    normed = (unit_rows * gain_float + ln_bias.astype(jnp.float32)).astype(jnp.bfloat16)
    gathered = lax.all_gather(normed, "tensor", axis=0, tiled=True)
    group_rows = gathered.shape[0]
    local_width = w_qkv.shape[2]
    local_heads = local_width // HEAD_DIM
    cosine_table, sine_table = rotary_tables(positions_of(segment))
    qkv_pre = jnp.einsum(
        "td,dcf->tcf", gathered, w_qkv, preferred_element_type=jnp.float32
    ) + b_qkv.astype(jnp.float32)
    shaped = qkv_pre.reshape(group_rows, 3, local_heads, HEAD_DIM)
    queries = rotate(shaped[:, 0], cosine_table, sine_table).astype(jnp.bfloat16)
    key_rows = rotate(shaped[:, 1], cosine_table, sine_table).astype(jnp.bfloat16)
    value_rows = shaped[:, 2].astype(jnp.bfloat16)
    up_pre = jnp.dot(gathered, w_up, preferred_element_type=jnp.float32) + b_up.astype(jnp.float32)
    activated = gelu_tanh(up_pre).astype(jnp.bfloat16)
    attended, lse_all = attend_forward(queries, key_rows, value_rows, segment)
    heads_out = attended.reshape(group_rows, local_width).astype(jnp.bfloat16)
    branches = lax.psum_scatter(
        jnp.dot(heads_out, w_out, preferred_element_type=jnp.float32)
        + jnp.dot(activated, w_down, preferred_element_type=jnp.float32),
        "tensor",
        scatter_dimension=0,
        tiled=True,
    )
    output = (inputs + branches + b_out.astype(jnp.float32) + b_down.astype(jnp.float32)).astype(
        jnp.bfloat16
    )
    grad_rows = lax.all_gather(cotangent, "tensor", axis=0, tiled=True)
    bias_total = jnp.sum(grad_rows, axis=0, dtype=jnp.float32)
    grad_w_out = jnp.einsum("tf,td->fd", heads_out, grad_rows, preferred_element_type=jnp.float32)
    grad_w_down = jnp.einsum("tf,td->fd", activated, grad_rows, preferred_element_type=jnp.float32)
    grad_heads = jnp.einsum(
        "td,fd->tf", grad_rows, w_out, preferred_element_type=jnp.float32
    ).astype(jnp.bfloat16)
    grad_act = jnp.einsum("td,fd->tf", grad_rows, w_down, preferred_element_type=jnp.float32)
    gelu_pullback = jax.vjp(gelu_tanh, up_pre)[1]
    grad_up = gelu_pullback(grad_act)[0].astype(jnp.bfloat16)
    grad_w_up = jnp.einsum("td,tf->df", gathered, grad_up, preferred_element_type=jnp.float32)
    grad_b_up = jnp.sum(grad_up, axis=0, dtype=jnp.float32)
    grad_queries, grad_keys, grad_values = attend_backward(
        queries,
        key_rows,
        value_rows,
        segment,
        lse_all,
        grad_heads.reshape(group_rows, local_heads, HEAD_DIM),
    )
    grad_qkv = (
        jnp.stack(
            [
                unrotate(grad_queries, cosine_table, sine_table),
                unrotate(grad_keys, cosine_table, sine_table),
                grad_values,
            ],
            axis=1,
        )
        .reshape(group_rows, 3, local_width)
        .astype(jnp.bfloat16)
    )
    grad_w_qkv = jnp.einsum("td,tcf->dcf", gathered, grad_qkv, preferred_element_type=jnp.float32)
    grad_b_qkv = jnp.sum(grad_qkv, axis=0, dtype=jnp.float32)
    grad_normed = lax.psum_scatter(
        jnp.einsum("tf,df->td", grad_up, w_up, preferred_element_type=jnp.float32)
        + jnp.einsum("tcf,dcf->td", grad_qkv, w_qkv, preferred_element_type=jnp.float32),
        "tensor",
        scatter_dimension=0,
        tiled=True,
    )
    scaled = grad_normed * gain_float
    mean_plain = jnp.mean(scaled, axis=1, keepdims=True)
    mean_unit = jnp.mean(scaled * unit_rows, axis=1, keepdims=True)
    input_grad = (
        cotangent.astype(jnp.float32) + rstd_rows * (scaled - mean_plain - unit_rows * mean_unit)
    ).astype(jnp.bfloat16)
    gain_part = jnp.sum(grad_normed * unit_rows, axis=0)
    shift_part = jnp.sum(grad_normed, axis=0)
    grad_ln_gain, grad_ln_bias = lax.psum((gain_part, shift_part), ("dp", "tensor"))
    bias_total, grad_b_up, grad_b_qkv = lax.psum((bias_total, grad_b_up, grad_b_qkv), "dp")
    grad_w_down, grad_w_out, grad_w_up, grad_w_qkv = from_pieces(
        sum_pieces(to_pieces(grad_w_down, grad_w_out, grad_w_up, grad_w_qkv))
    )
    return (
        output,
        input_grad,
        grad_ln_gain,
        grad_ln_bias,
        grad_w_qkv,
        grad_b_qkv,
        grad_w_out,
        bias_total,
        grad_w_up,
        grad_b_up,
        grad_w_down,
        bias_total,
    )


def solution(mesh):
    placed = (
        P(("dp", "tensor"), None),
        P("dp"),
        P(),
        P(),
        P(None, None, "tensor"),
        P(None, "tensor"),
        P("tensor", None),
        P(),
        P(None, "tensor"),
        P("tensor"),
        P("tensor", None),
        P(),
        P(("dp", "tensor"), None),
    )
    return jax.shard_map(
        on_device,
        mesh=mesh,
        in_specs=placed,
        out_specs=(
            P(("dp", "tensor"), None),
            P(("dp", "tensor"), None),
            P(),
            P(),
            P(None, None, "tensor"),
            P(None, "tensor"),
            P("tensor", None),
            P(),
            P(None, "tensor"),
            P("tensor"),
            P("tensor", None),
            P(),
        ),
        check_vma=False,
    )
```

```python
import jax
import jax.numpy as jnp
from jax import lax
from jax.experimental import pallas as pl
from jax.experimental.pallas import tpu as pltpu
from jax.sharding import PartitionSpec as P

HEAD_DIM = 64
ROT = 32
EPSILON = 1e-05
MESH = pl.DeviceIdType.MESH
BF = jnp.bfloat16
F32 = jnp.float32
NP = 24
VMEM_LIMIT = 64 << 20


def neighbours():
    dp = lax.axis_index("dp")
    tensor = lax.axis_index("tensor")
    y, zh, core = dp // 4, (dp // 2) % 2, dp % 2
    zl, x = tensor // 4, tensor % 4
    yl, yr, yo = (y + 3) % 4, (y + 1) % 4, (y + 2) % 4
    xl, xr, xo = (x + 3) % 4, (x + 1) % 4, (x + 2) % 4
    where = dict(y=y, core=core, zl=zl, x=x, yl=yl, yr=yr, yo=yo, xl=xl, xr=xr, xo=xo)
    where["dev_yl"] = (yl * 4 + zh * 2 + core, tensor)
    where["dev_yr"] = (yr * 4 + zh * 2 + core, tensor)
    where["dev_zh"] = (y * 4 + (1 - zh) * 2 + core, tensor)
    where["dev_core"] = (y * 4 + zh * 2 + 1 - core, tensor)
    where["dev_xl"] = (dp, zl * 4 + xl)
    where["dev_xr"] = (dp, zl * 4 + xr)
    where["dev_zl"] = (dp, (1 - zl) * 4 + x)
    return where


def greet(devices):
    barrier = pltpu.get_barrier_semaphore()
    for device in devices:
        pl.semaphore_signal(barrier, inc=1, device_id=device, device_id_type=MESH)
    pl.semaphore_wait(barrier, len(devices))


def rcopy(src, dst, send, recv, device):
    return pltpu.make_async_remote_copy(
        src_ref=src, dst_ref=dst, send_sem=send, recv_sem=recv, device_id=device, device_id_type=MESH
    )


def rows_at(index, size, count=None):
    return pl.ds(pl.multiple_of(index * size, size), size if count is None else count)


class GradSum:
    def scratch():
        return [
            pltpu.VMEM((2, 1024, 256), BF),
            pltpu.VMEM((4, 512, 256), BF),
            pltpu.VMEM((4, 512, 256), BF),
            pltpu.VMEM((4, 2, 64, 256), BF),
            pltpu.VMEM((4, 2, 128, 256), BF),
            pltpu.VMEM((4, 128, 256), BF),
            pltpu.VMEM((4, 128, 256), BF),
            pltpu.VMEM((4, 128, 256), BF),
            pltpu.SemaphoreType.DMA((11, 4)),
            pltpu.SemaphoreType.DMA((11, 4)),
            pltpu.SemaphoreType.DMA((4,)),
        ]

    def __init__(self, at, out, scratch):
        self.at, self.out = at, out
        (self.own, self.other, self.half, self.r1, self.r2, self.zs, self.zr, self.full,
         self.send, self.recv, self.local) = scratch

    def core_copy(self, p):
        s, at = p % 4, self.at
        return rcopy(self.own.at[p % 2, rows_at(1 - at["core"], 512)], self.other.at[s],
                     self.send.at[0, s], self.recv.at[0, s], at["dev_core"])

    def first_copies(self, p):
        s, at = p % 4, self.at
        top = self.half.at[s, rows_at(at["yo"], 128, 64)]
        low = self.half.at[s, pl.ds(pl.multiple_of(at["yo"] * 128 + 64, 64), 64)]
        return (rcopy(top, self.r1.at[s, 0], self.send.at[1, s], self.recv.at[1, s], at["dev_yr"]),
                rcopy(low, self.r1.at[s, 1], self.send.at[2, s], self.recv.at[2, s], at["dev_yl"]))

    def second_copies(self, p):
        s, at = p % 4, self.at
        return (rcopy(self.half.at[s, rows_at(at["yr"], 128)], self.r2.at[s, 0],
                      self.send.at[3, s], self.recv.at[3, s], at["dev_yr"]),
                rcopy(self.half.at[s, rows_at(at["yl"], 128)], self.r2.at[s, 1],
                      self.send.at[4, s], self.recv.at[4, s], at["dev_yl"]))

    def z_copy(self, p):
        s = p % 4
        return rcopy(self.zs.at[s], self.zr.at[s], self.send.at[5, s], self.recv.at[5, s],
                     self.at["dev_zh"])

    def back_first(self, p):
        s, at = p % 4, self.at
        mine = self.out.at[p, rows_at(at["core"] * 4 + at["y"], 128)]
        return (rcopy(self.full.at[s], mine, self.send.at[6, s], self.recv.at[6, s], at["dev_yr"]),
                rcopy(self.full.at[s], mine, self.send.at[7, s], self.recv.at[7, s], at["dev_yl"]),
                pltpu.make_async_copy(self.full.at[s], mine, self.local.at[s]))

    def back_second(self, p):
        s, at = p % 4, self.at
        top = self.out.at[p, rows_at(at["core"] * 4 + at["yl"], 128, 64)]
        low = self.out.at[p, pl.ds(pl.multiple_of((at["core"] * 4 + at["yr"]) * 128 + 64, 64), 64)]
        return (rcopy(top, top, self.send.at[9, s], self.recv.at[9, s], at["dev_yr"]),
                rcopy(low, low, self.send.at[10, s], self.recv.at[10, s], at["dev_yl"]))

    def back_core(self, p):
        s, at = p % 4, self.at
        mine = self.out.at[p, rows_at(at["core"], 512)]
        return rcopy(mine, mine, self.send.at[8, s], self.recv.at[8, s], at["dev_core"])

    def send_piece(self, p):
        self.core_copy(p).start()

    def add_core(self, p):
        s = p % 4
        self.core_copy(p).wait()

        @pl.loop(0, 4)
        def _(j):
            rows = rows_at(j, 128)
            mine = self.own[p % 2, pl.ds(pl.multiple_of(self.at["core"] * 512 + j * 128, 128), 128)]
            self.half[s, rows] = (mine.astype(F32) + self.other[s, rows].astype(F32)).astype(BF)

        for copy in self.first_copies(p):
            copy.start()

    def add_first(self, p):
        s, at = p % 4, self.at
        for copy in self.first_copies(p):
            copy.wait()
        top = rows_at(at["yr"], 128, 64)
        low = pl.ds(pl.multiple_of(at["yl"] * 128 + 64, 64), 64)
        self.half[s, top] = (self.half[s, top].astype(F32) + self.r1[s, 0].astype(F32)).astype(BF)
        self.half[s, low] = (self.half[s, low].astype(F32) + self.r1[s, 1].astype(F32)).astype(BF)
        for copy in self.second_copies(p):
            copy.start()

    def add_second(self, p):
        s = p % 4
        for copy in self.second_copies(p):
            copy.wait()
        mine = self.half[s, rows_at(self.at["y"], 128)].astype(F32)
        self.zs[s] = (mine + self.r2[s, 0].astype(F32) + self.r2[s, 1].astype(F32)).astype(BF)
        self.z_copy(p).start()

    def add_z(self, p):
        s = p % 4
        self.z_copy(p).wait()
        self.full[s] = (self.zs[s].astype(F32) + self.zr[s].astype(F32)).astype(BF)
        for copy in self.back_first(p):
            copy.start()

    def forward_y(self, p):
        for copy in self.back_first(p):
            copy.wait()
        for copy in self.back_second(p):
            copy.start()

    def forward_core(self, p):
        for copy in self.back_second(p):
            copy.wait()
        self.back_core(p).start()

    def finish(self, p):
        self.back_core(p).wait()

    def steps(self, t, begin=0):
        for lag, step in enumerate((self.add_core, self.add_first, self.add_second, self.add_z,
                                    self.forward_y, self.forward_core, self.finish), 1):
            p = t - lag
            pl.when((p >= 0) & (p < NP))(lambda step=step, p=p: step(p))


def dot(a, b):
    return lax.dot_general(a, b, (((1,), (0,)), ((), ())), preferred_element_type=F32)


def dot_nt(a, b):
    return lax.dot_general(a, b, (((1,), (1,)), ((), ())), preferred_element_type=F32)


def at_rows(index, size=256):
    return pl.ds(pl.multiple_of(index * size, size), size)


class Gather:
    def scratch():
        return [
            pltpu.VMEM((16, 128, 256), BF),
            pltpu.VMEM((8, 1024, 256), BF),
            pltpu.SemaphoreType.DMA((9, 4)),
            pltpu.SemaphoreType.DMA((9, 4)),
        ]

    def __init__(self, at, scratch):
        self.at = at
        self.own, self.all, self.send, self.recv = scratch

    def copy(self, kind, c, src, dst, device):
        s = c % 4
        return rcopy(src, dst, self.send.at[kind, s], self.recv.at[kind, s], device)

    def part(self, c, zl, x, begin=0, count=128):
        first = pl.multiple_of((zl * 4 + x) * 128 + begin, 64)
        return self.all.at[c % 8, pl.ds(first, count)]

    def first(self, c):
        at = self.at
        src, dst = self.own.at[c], self.part(c, at["zl"], at["x"])
        return [self.copy(0, c, src, dst, at["dev_xr"]), self.copy(1, c, src, dst, at["dev_xl"]),
                self.copy(2, c, src, dst, at["dev_zl"])]

    def second(self, c):
        at = self.at
        top = self.part(c, at["zl"], at["xl"], 0, 64)
        low = self.part(c, at["zl"], at["xr"], 64, 64)
        other = self.part(c, 1 - at["zl"], at["x"])
        return [self.copy(3, c, top, top, at["dev_xr"]), self.copy(4, c, low, low, at["dev_xl"]),
                self.copy(5, c, other, other, at["dev_xr"]), self.copy(6, c, other, other, at["dev_xl"])]

    def third(self, c):
        at = self.at
        top = self.part(c, 1 - at["zl"], at["xl"], 0, 64)
        low = self.part(c, 1 - at["zl"], at["xr"], 64, 64)
        return [self.copy(7, c, top, top, at["dev_xr"]), self.copy(8, c, low, low, at["dev_xl"])]

    def steps(self, t):
        @pl.when(t < 16)
        def _():
            for copy in self.first(t):
                copy.start()
            self.part(t, self.at["zl"], self.at["x"])[...] = self.own[t]

        @pl.when((t >= 1) & (t < 17))
        def _():
            for copy in self.first(t - 1):
                copy.wait()
            for copy in self.second(t - 1):
                copy.start()

        @pl.when((t >= 2) & (t < 18))
        def _():
            for copy in self.second(t - 2):
                copy.wait()
            for copy in self.third(t - 2):
                copy.start()

        @pl.when((t >= 3) & (t < 19))
        def _():
            for copy in self.third(t - 3):
                copy.wait()


class RowSum:
    def scratch():
        return [
            pltpu.VMEM((4, 2, 4, 128, 256), BF),
            pltpu.VMEM((4, 2, 2, 64, 256), BF),
            pltpu.VMEM((4, 2, 2, 128, 256), BF),
            pltpu.VMEM((4, 128, 256), BF),
            pltpu.VMEM((4, 128, 256), BF),
            pltpu.VMEM((4, 128, 256), F32),
            pltpu.SemaphoreType.DMA((5, 4)),
            pltpu.SemaphoreType.DMA((5, 4)),
        ]

    def __init__(self, at, scratch, result):
        self.at, self.result = at, result
        self.part, self.r1, self.r2, self.zs, self.zr, self.mine, self.send, self.recv = scratch

    def copy(self, kind, c, src, dst, device):
        s = c % 4
        return rcopy(src, dst, self.send.at[kind, s], self.recv.at[kind, s], device)

    def first(self, c):
        s, at = c % 4, self.at
        return [self.copy(0, c, self.part.at[s, :, at["xo"], pl.ds(0, 64)], self.r1.at[s, 0], at["dev_xr"]),
                self.copy(1, c, self.part.at[s, :, at["xo"], pl.ds(64, 64)], self.r1.at[s, 1], at["dev_xl"])]

    def second(self, c):
        s, at = c % 4, self.at
        return [self.copy(2, c, self.part.at[s, :, at["xr"]], self.r2.at[s, 0], at["dev_xr"]),
                self.copy(3, c, self.part.at[s, :, at["xl"]], self.r2.at[s, 1], at["dev_xl"])]

    def third(self, c):
        s = c % 4
        return [self.copy(4, c, self.zs.at[s], self.zr.at[s], self.at["dev_zl"])]

    def store(self, c, block, value):
        for k in range(2):
            r = block * 2 + k
            self.part[c % 4, r // 4, r % 4] = value[k * 128:(k + 1) * 128].astype(BF)

    def send_chunk(self, c):
        for copy in self.first(c):
            copy.start()

    def add_first(self, c):
        s, at = c % 4, self.at
        for copy in self.first(c):
            copy.wait()
        for z in range(2):
            top = self.part[s, z, at["xr"], 0:64].astype(F32) + self.r1[s, 0, z].astype(F32)
            self.part[s, z, at["xr"], 0:64] = top.astype(BF)
            low = self.part[s, z, at["xl"], 64:128].astype(F32) + self.r1[s, 1, z].astype(F32)
            self.part[s, z, at["xl"], 64:128] = low.astype(BF)
        for copy in self.second(c):
            copy.start()

    def add_second(self, c):
        s, at = c % 4, self.at
        for copy in self.second(c):
            copy.wait()

        def total(z):
            own = self.part[s, z, at["x"]].astype(F32)
            return own + self.r2[s, 0, z].astype(F32) + self.r2[s, 1, z].astype(F32)

        self.zs[s] = total(1 - at["zl"]).astype(BF)
        for copy in self.third(c):
            copy.start()
        self.mine[s] = total(at["zl"])

    def add_third(self, c):
        s = c % 4
        for copy in self.third(c):
            copy.wait()
        self.result(c, self.mine[s] + self.zr[s].astype(F32))

    def steps(self, t):
        for lag, step in enumerate((self.add_first, self.add_second, self.add_third), 1):
            c = t - lag
            pl.when((c >= 0) & (c < 8))(lambda step=step, c=c: step(c))
            pl.when((c >= 10) & (c < 18))(lambda step=step, c=c - 2: step(c))


class SmallSum:
    def scratch():
        return [
            pltpu.VMEM((8, 8, 1024), F32),
            pltpu.VMEM((4, 8, 1024), F32),
            pltpu.VMEM((4, 8, 1024), F32),
            pltpu.SemaphoreType.DMA((13,)),
            pltpu.SemaphoreType.DMA((13,)),
        ]

    def __init__(self, scratch):
        self.b1, self.b2, self.b3, self.send, self.recv = scratch
        dp, tensor = lax.axis_index("dp"), lax.axis_index("tensor")
        y, self.zh, core = dp // 4, (dp // 2) % 2, dp % 2
        self.zl, self.x = tensor // 4, tensor % 4
        self.i1 = y * 2 + core
        self.i2 = self.zh * 2 + self.zl
        self.d1, self.d2, self.d3 = [], [], []
        for k in range(1, 8):
            j = (self.i1 + k) % 8
            self.d1.append(((j // 2) * 4 + self.zh * 2 + j % 2, tensor))
        for k in range(1, 4):
            j = (self.i2 + k) % 4
            self.d2.append((y * 4 + (j // 2) * 2 + core, (j % 2) * 4 + self.x))
            self.d3.append((dp, self.zl * 4 + (self.x + k) % 4))

    def devices(self):
        return self.d1 + self.d2 + self.d3

    def copies(self, stage):
        buf, mine, devices, base = ((self.b1, self.i1, self.d1, 0), (self.b2, self.i2, self.d2, 7),
                                    (self.b3, self.x, self.d3, 10))[stage]
        return [rcopy(buf.at[mine], buf.at[mine], self.send.at[base + k], self.recv.at[base + k], device)
                for k, device in enumerate(devices)]

    def start(self, stage):
        for copy in self.copies(stage):
            copy.start()

    def wait(self, stage):
        for copy in self.copies(stage):
            copy.wait()

    def second(self):
        self.wait(0)
        total = self.b1[0]
        for k in range(1, 8):
            total = total + self.b1[k]
        self.b2[self.i2] = total
        self.start(1)

    def third(self):
        self.wait(1)
        wide = self.b2[0] + self.b2[1] + self.b2[2] + self.b2[3]
        narrow = self.b2[self.zl] + self.b2[2 + self.zl]
        row = lax.broadcasted_iota(jnp.int32, (8, 1024), 0)
        self.b3[self.x] = jnp.where(row < 6, wide, narrow)
        self.start(2)

    def result(self):
        self.wait(2)
        wide = self.b3[0] + self.b3[1] + self.b3[2] + self.b3[3]
        row = lax.broadcasted_iota(jnp.int32, (8, 1024), 0)
        return jnp.where(row < 6, wide, self.b3[self.x])


def gelu_parts(u):
    inner = 0.7978845608028654 * (u + 0.044715 * (u * u * u))
    return jnp.tanh(inner)


def swap_pairs(v):
    lane = lax.broadcasted_iota(jnp.int32, v.shape, 1)
    return jnp.where(lane % 32 < 16, pltpu.roll(v, 112, 1), pltpu.roll(v, 16, 1))


def turn(v, cosine, sine):
    return v * cosine + swap_pairs(v) * sine


HO = 12
RS = 20


def block_kernel(
    tokens, cotangent, seg_row, inverse, gain, shift, b_qkv, b_out, b_up, b_down,
    w_qkv_h, w_out_h, w_up_h, w_down_h,
    pieces, output, input_grad, sums,
    w_qkv, w_out, w_up, w_down, w_sem,
    normed_t, up, grad_act, qkv_f, rows, turned, act, act_t, heads, heads_t, outs_g, outs_gt, gqkv,
    cos_t, sin_t, seg_c, seg_r, lse, bias, p_f, dp_f, q_m, g_m, unit, rstd, grad_n,
    *scratch,
):
    at = neighbours()
    n1, n2, n3 = len(GradSum.scratch()), len(Gather.scratch()), len(RowSum.scratch())
    small = SmallSum(scratch[n1 + n2 + n3:])
    grads = GradSum(at, pieces, scratch[:n1])
    gather = Gather(at, scratch[n1:n1 + n2])

    def keep_rows(c, value):
        @pl.when(c < 8)
        def _():
            cols = at_rows(c)
            own = tokens[:, cols].astype(F32) + value
            own = own + b_out[0:1, cols].astype(F32) + b_down[0:1, cols].astype(F32)
            output[:, cols] = own.astype(BF)

        @pl.when(c >= 8)
        def _():
            grad_n[c - 8] = value

    row_sum = RowSum(at, scratch[n1 + n2:n1 + n2 + n3], keep_rows)
    do_acc = dp_f
    grad_up = act_t

    weights = [pltpu.make_async_copy(src, dst, w_sem.at[i]) for i, (src, dst) in enumerate(
        ((w_up_h, w_up), (w_qkv_h, w_qkv), (w_down_h, w_down), (w_out_h, w_out)))]
    for copy in weights:
        copy.start()

    barrier = pltpu.get_barrier_semaphore()
    greeted = small.devices()
    for device in greeted:
        pl.semaphore_signal(barrier, inc=1, device_id=device, device_id_type=MESH)

    x = tokens[...].astype(F32)
    centered = x - jnp.mean(x, axis=1, keepdims=True)
    scale = lax.rsqrt(jnp.mean(centered * centered, axis=1, keepdims=True) + EPSILON)
    rstd[...] = jnp.broadcast_to(scale, (128, 128))
    unit[...] = centered * scale
    for c in range(8):
        cols = slice(c * 256, c * 256 + 256)
        value = unit[:, cols] * gain[0:1, cols].astype(F32) + shift[0:1, cols].astype(F32)
        gather.own[c] = value.astype(BF)
        gather.own[8 + c] = cotangent[:, cols]

    pl.semaphore_wait(barrier, len(greeted))
    gather.steps(0)

    seg_f = seg_row[...].astype(F32)
    seg_r[...] = jnp.broadcast_to(seg_f, (8, 1024))
    seg_c[...] = jnp.broadcast_to(seg_f, (128, 1024)).T
    for ref in (q_m, g_m):
        ref[...] = jnp.zeros_like(ref)

    @pl.loop(0, 4)
    def _(b):
        r = at_rows(b)
        own_id = seg_c[r, 0:1]
        other = seg_r[0:1, :]
        i = lax.broadcasted_iota(jnp.int32, (256, 1024), 0) + b * 256
        j = lax.broadcasted_iota(jnp.int32, (256, 1024), 1)
        same = jnp.where((own_id == other) & (j < i), 1.0, 0.0)
        position = jnp.sum(same, axis=1, keepdims=True)
        angle = position * inverse[0:1, :]
        lane = lax.broadcasted_iota(jnp.int32, (256, 128), 1) % 64
        sine = jnp.sin(angle)
        cos_t[r, :] = jnp.where(lane < ROT, jnp.cos(angle), 1.0)
        sin_t[r, :] = jnp.where(lane < ROT // 2, -sine, jnp.where(lane < ROT, sine, 0.0))
        up[r, :] = jnp.broadcast_to(b_up[0:1, :].astype(F32), (256, 1024))
        for k in range(3):
            qkv_f[k, r, :] = jnp.broadcast_to(b_qkv[k:k + 1, :].astype(F32), (256, 256))

    @pl.loop(1, 11)
    def _(t):
        gather.steps(t)

        @pl.when(t == 3)
        def _():
            weights[0].wait()
            weights[1].wait()

        @pl.when(t >= 3)
        def _():
            c = t - 3

            @pl.loop(0, 4)
            def _(b):
                r = at_rows(b)
                a = gather.all[c % 8, r, :]
                for k in range(4):
                    cols = slice(k * 256, k * 256 + 256)
                    up[r, cols] += dot(a, w_up[at_rows(c), cols])
                for k in range(3):
                    qkv_f[k, r, :] += dot(a, w_qkv[k, at_rows(c), :])
                normed_t[at_rows(c), r] = a.T

    gather.steps(11)

    @pl.loop(0, 4)
    def _(b):
        r = at_rows(b)
        for k in range(4):
            cols = slice(k * 256, k * 256 + 256)
            u = up[r, cols]
            a = (u * (0.5 * (1.0 + gelu_parts(u)))).astype(BF)
            act[r, cols] = a
            act_t[cols, r] = a.T

    def make_rows(b):
        r = at_rows(b)
        for k in range(3):
            for half in range(2):
                cols = slice(half * 128, half * 128 + 128)
                v = qkv_f[k, r, cols]
                if k < 2:
                    v = turn(v, cos_t[r, :], sin_t[r, :])
                if k == 0:
                    v = v * HEAD_DIM ** -0.5
                v = v.astype(BF)
                rows[k, r, cols] = v
                turned[k, cols, r] = v.T

    def attend_bias(qb):
        cols = slice(qb * 256, qb * 256 + 256)
        for kb in range(qb + 1):
            r = slice(kb * 256, kb * 256 + 256)
            keep = seg_c[r, 0:1] == seg_r[0:1, cols]
            if kb == qb:
                i = lax.broadcasted_iota(jnp.int32, (256, 256), 0)
                j = lax.broadcasted_iota(jnp.int32, (256, 256), 1)
                keep = keep & (i <= j)
            bias[r, :] = jnp.where(keep, 0.0, -1e30)

    def head_rows(h):
        return pl.ds(pl.multiple_of(h * 64, 64), 64)

    def attend(qb):
        cols = slice(qb * 256, qb * 256 + 256)
        attend_bias(qb)

        @pl.loop(0, 4)
        def _(h):
            hr = head_rows(h)
            q_m[h, hr, :] = turned[0, hr, cols]
            most = jnp.full((1, 256), -jnp.inf, F32)
            for kb in range(qb + 1):
                r = slice(kb * 256, kb * 256 + 256)
                s = dot(rows[1, r, :], q_m[h]) + bias[r, :]
                p_f[r, :] = s
                most = jnp.maximum(most, jnp.max(s, axis=0, keepdims=True))
            total = jnp.zeros((1, 256), F32)
            for kb in range(qb + 1):
                r = slice(kb * 256, kb * 256 + 256)
                e = jnp.exp(p_f[r, :] - most)
                p_f[r, :] = e
                total = total + jnp.sum(e, axis=0, keepdims=True)
            share = 1.0 / total
            out = jnp.zeros((64, 256), F32)
            for kb in range(qb + 1):
                r = slice(kb * 256, kb * 256 + 256)
                p = (p_f[r, :] * share).astype(BF)
                out = out + dot(turned[2, hr, r], p)
            heads_t[hr, cols] = out.astype(BF)
            lse[pl.ds(h, 1), cols] = most + jnp.log(total)

    def attend_back(qb, first_head):
        cols = slice(qb * 256, qb * 256 + 256)
        if first_head == 0:
            attend_bias(qb)

        @pl.loop(first_head, first_head + 2)
        def _(h):
            hr = head_rows(h)
            q_m[h, hr, :] = turned[0, hr, cols]
            g_m[h, hr, :] = outs_gt[hr, cols]
            log_total = lse[pl.ds(h, 1), cols]
            delta = jnp.zeros((1, 256), F32)
            for kb in range(qb + 1):
                r = slice(kb * 256, kb * 256 + 256)
                p = jnp.exp(dot(rows[1, r, :], q_m[h]) + bias[r, :] - log_total)
                d = dot(rows[2, r, :], g_m[h])
                p_f[r, :] = p
                dp_f[r, :] = d
                delta = delta + jnp.sum(p * d, axis=0, keepdims=True)
            lane = lax.broadcasted_iota(jnp.int32, (256, 256), 1) // 64
            q_h = jnp.where(lane == h, rows[0, cols, :].astype(F32), 0.0).astype(BF)
            g_h = jnp.where(lane == h, outs_g[cols, :].astype(F32), 0.0).astype(BF)
            grad_q = jnp.zeros((64, 256), F32)
            for kb in range(qb + 1):
                r = slice(kb * 256, kb * 256 + 256)
                p = p_f[r, :]
                ds = (p * (dp_f[r, :] - delta)).astype(BF)
                qkv_f[1, r, :] += dot(ds, q_h)
                qkv_f[2, r, :] += dot(p.astype(BF), g_h)
                grad_q = grad_q + dot(turned[1, hr, r], ds)
            for half in range(2):
                qkv_f[0, pl.ds(pl.multiple_of(qb * 256 + h * 64, 64), 64),
                      half * 128:half * 128 + 128] = grad_q[:, half * 128:half * 128 + 128]

    @pl.loop(12, 20)
    def _(t):
        grads.steps(t - HO)
        gather.steps(t)
        c = t - 12

        @pl.when(t == 12)
        def _():
            weights[2].wait()
            weights[3].wait()

        @pl.loop(0, 4)
        def _(b):
            r = at_rows(b)
            grads.own[c % 2, r, :] = dot(act_t[r, :], gather.all[c % 8]).astype(BF)

        grads.send_piece(c)

        @pl.loop(0, 4)
        def _(b):
            r = at_rows(b)
            a = gather.all[c % 8, r, :]
            fresh = c == 0
            for k in range(4):
                cols = slice(k * 256, k * 256 + 256)
                grad_act[r, cols] = jnp.where(fresh, 0.0, grad_act[r, cols]) + dot_nt(a, w_down[cols, at_rows(c)])
            do_acc[r, :] = jnp.where(fresh, 0.0, do_acc[r, :]) + dot_nt(a, w_out[:, at_rows(c)])

        @pl.when(t < 16)
        def _():
            make_rows(t - 12)

        for qb in range(4):
            pl.when(t == 16 + qb)(lambda qb=qb: attend(qb))

    def branch_chunk(c):
        @pl.loop(0, 4)
        def _(b):
            r = at_rows(b)
            value = dot(act[r, :], w_down[:, at_rows(c)]) + dot(heads[r, :], w_out[:, at_rows(c)])
            row_sum.store(c, b, value)
        row_sum.send_chunk(c)

    def normed_chunk(c):
        @pl.loop(0, 4)
        def _(b):
            r = at_rows(b)
            d = at_rows(c)
            value = dot_nt(grad_up[r, :], w_up[d, :])
            for k in range(3):
                value = value + dot_nt(gqkv[k, r, :], w_qkv[k, d, :])
            row_sum.store(c + 8, b, value)
        row_sum.send_chunk(c + 8)

    @pl.loop(0, 4)
    def _(b):
        r = at_rows(b)
        heads[r, :] = heads_t[:, r].T
        g = do_acc[r, :].astype(BF)
        outs_g[r, :] = g
        outs_gt[:, r] = g.T

    @pl.loop(20, 22)
    def _(t):
        grads.steps(t - HO)
        row_sum.steps(t - RS)
        p = t - HO
        for j in range(4):
            r = slice(j * 256, j * 256 + 256)
            grads.own[p % 2, r, :] = dot(heads_t[...], gather.all[4 * (p - 8) + j]).astype(BF)
        grads.send_piece(p)
        branch_chunk(t - RS)

        @pl.loop(2 * (t - 20), 2 * (t - 20) + 2)
        def _(b):
            r = at_rows(b)
            for k in range(4):
                cols = slice(k * 256, k * 256 + 256)
                u = up[r, cols]
                th = gelu_parts(u)
                slope = 0.5 * (1.0 + th) + 0.5 * u * (1.0 - th * th) * (
                    0.7978845608028654 * (1.0 + 3 * 0.044715 * (u * u)))
                grad_up[r, cols] = (slope * grad_act[r, cols]).astype(BF)

        @pl.loop(0, 2)
        def _(half):
            for k in range(3):
                qkv_f[k, at_rows((t - 20) * 2 + half), :] = jnp.zeros((256, 256), F32)

    @pl.loop(22, 30)
    def _(t):
        grads.steps(t - HO)
        row_sum.steps(t - RS)
        p = t - HO
        q = p - 10

        @pl.loop(0, 4)
        def _(b):
            r = at_rows((q % 2) * 4 + b)
            grads.own[p % 2, at_rows(b), :] = dot(normed_t[r, :], grad_up[:, at_rows(q // 2)]).astype(BF)

        grads.send_piece(p)

        @pl.when(t < 28)
        def _():
            branch_chunk(t - RS)

        for qb in range(4):
            for half in range(2):
                pl.when(t == 22 + 2 * qb + half)(lambda qb=qb, half=half: attend_back(qb, 2 * half))

    mine = small.i1

    def column_sum(value):
        return jnp.sum(value.astype(F32), axis=0, keepdims=True)

    for b in range(4):
        r = slice(b * 256, b * 256 + 256)
        grad_q = qkv_f[0, r, :].T * HEAD_DIM ** -0.5
        for half in range(2):
            cols = slice(half * 128, half * 128 + 128)
            cosine, sine = cos_t[r, :], -sin_t[r, :]
            gqkv[0, r, cols] = turn(grad_q[:, cols], cosine, sine).astype(BF)
            gqkv[1, r, cols] = turn(qkv_f[1, r, cols], cosine, sine).astype(BF)
            gqkv[2, r, cols] = qkv_f[2, r, cols].astype(BF)

    @pl.loop(30, 36)
    def _(t):
        grads.steps(t - HO)
        row_sum.steps(t - RS)
        p = t - HO
        q = p - 18

        @pl.loop(0, 4)
        def _(b):
            r = at_rows((q % 2) * 4 + b)
            grads.own[p % 2, at_rows(b), :] = dot(normed_t[r, :], gqkv[q // 2]).astype(BF)

        grads.send_piece(p)
        normed_chunk(t - 30)

    @pl.loop(36, 41)
    def _(t):
        grads.steps(t - HO)
        row_sum.steps(t - RS)

        @pl.when(t < 38)
        def _():
            normed_chunk(t - 30)

    small.b1[mine] = jnp.zeros((8, 1024), F32)
    mean_plain = jnp.zeros((128, 1), F32)
    mean_unit = jnp.zeros((128, 1), F32)
    for c in range(8):
        cols = slice(c * 256, c * 256 + 256)
        row, lanes = c // 4, slice((c % 4) * 256, (c % 4) * 256 + 256)
        g = grad_n[c]
        n = unit[:, cols]
        scaled = g * gain[0:1, cols].astype(F32)
        mean_plain = mean_plain + jnp.sum(scaled, axis=1, keepdims=True)
        mean_unit = mean_unit + jnp.sum(scaled * n, axis=1, keepdims=True)
        small.b1[mine, row:row + 1, lanes] = column_sum(g * n)
        small.b1[mine, 2 + row:3 + row, lanes] = column_sum(g)
        small.b1[mine, 4 + row:5 + row, lanes] = column_sum(cotangent[:, cols])
    for k in range(4):
        cols = slice(k * 256, k * 256 + 256)
        small.b1[mine, 6:7, cols] = column_sum(grad_up[:, cols])
    for k in range(3):
        small.b1[mine, 7:8, k * 256:k * 256 + 256] = column_sum(gqkv[k])
    small.start(0)
    mean_plain = mean_plain / 2048.0
    mean_unit = mean_unit / 2048.0
    for c in range(8):
        cols = slice(c * 256, c * 256 + 256)
        scaled = grad_n[c] * gain[0:1, cols].astype(F32)
        inner = scaled - mean_plain - unit[:, cols] * mean_unit
        input_grad[:, cols] = (cotangent[:, cols].astype(F32) + rstd[:, 0:1] * inner).astype(BF)

    grads.steps(41 - HO)
    small.second()
    grads.steps(42 - HO)
    small.third()
    sums[...] = small.result()


def run_block(tokens, segment, ln_gain, ln_bias, w_qkv, b_qkv, w_out, b_out, w_up, b_up, w_down,
              b_down, cotangent):
    exponent = jnp.arange(ROT // 2, dtype=F32) * (2.0 / ROT)
    inverse = jnp.tile(jnp.power(10000.0, -exponent), 8).reshape(1, 128)
    vmem = pl.BlockSpec(memory_space=pltpu.VMEM)
    hbm = pl.BlockSpec(memory_space=pl.ANY)
    V = pltpu.VMEM
    scratch = [
        V((3, 2048, 256), BF), V((256, 2048), BF), V((2048, 1024), BF), V((1024, 2048), BF),
        pltpu.SemaphoreType.DMA((4,)),
        V((2048, 1024), BF),
        V((1024, 1024), F32), V((1024, 1024), F32),
        V((3, 1024, 256), F32),
        V((3, 1024, 256), BF), V((3, 256, 1024), BF),
        V((1024, 1024), BF), V((1024, 1024), BF),
        V((1024, 256), BF), V((256, 1024), BF),
        V((1024, 256), BF), V((256, 1024), BF),
        V((3, 1024, 256), BF),
        V((1024, 128), F32), V((1024, 128), F32),
        V((1024, 128), F32), V((8, 1024), F32),
        V((8, 1024), F32),
        V((1024, 256), F32), V((1024, 256), F32), V((1024, 256), F32),
        V((4, 256, 256), BF), V((4, 256, 256), BF),
        V((128, 2048), F32), V((128, 128), F32), V((8, 128, 256), F32),
    ] + GradSum.scratch() + Gather.scratch() + RowSum.scratch() + SmallSum.scratch()
    return pl.pallas_call(
        block_kernel,
        out_shape=(
            jax.ShapeDtypeStruct((NP, 1024, 256), BF),
            jax.ShapeDtypeStruct((128, 2048), BF),
            jax.ShapeDtypeStruct((128, 2048), BF),
            jax.ShapeDtypeStruct((8, 1024), F32),
        ),
        in_specs=[vmem] * 10 + [hbm] * 4,
        out_specs=(hbm, vmem, vmem, vmem),
        scratch_shapes=scratch,
        compiler_params=pltpu.CompilerParams(
            collective_id=0, has_side_effects=True, vmem_limit_bytes=VMEM_LIMIT),
        cost_estimate=pl.CostEstimate(flops=50 * 10**9, bytes_accessed=30 << 20, transcendentals=10**7),
    )(
        tokens, cotangent, segment.reshape(1, 1024), inverse, ln_gain.reshape(1, 2048),
        ln_bias.reshape(1, 2048), b_qkv, b_out.reshape(1, 2048), b_up.reshape(1, 1024),
        b_down.reshape(1, 2048), w_qkv.transpose(1, 0, 2), w_out, w_up, w_down,
    )


def widen_kernel(piece, down, out, up, qkv):
    i = pl.program_id(0)
    value = piece[0]

    @pl.when(i < 8)
    def _():
        down[...] = value.astype(F32)

    @pl.when((i >= 8) & (i < 10))
    def _():
        for j in range(4):
            out[:, j * 256:j * 256 + 256] = piece[0, j * 256:j * 256 + 256, :].astype(F32)

    @pl.when((i >= 10) & (i < 18))
    def _():
        up[...] = value.astype(F32)

    @pl.when(i >= 18)
    def _():
        qkv[0] = value.astype(F32)


def widen(pieces):
    down, out, up, qkv = pl.pallas_call(
        widen_kernel,
        grid=(NP,),
        out_shape=(
            jax.ShapeDtypeStruct((1024, 2048), F32),
            jax.ShapeDtypeStruct((256, 2048), F32),
            jax.ShapeDtypeStruct((2048, 1024), F32),
            jax.ShapeDtypeStruct((3, 2048, 256), F32),
        ),
        in_specs=[pl.BlockSpec((1, 1024, 256), lambda i: (i, 0, 0))],
        out_specs=(
            pl.BlockSpec((1024, 256), lambda i: (0, jnp.minimum(i, 7))),
            pl.BlockSpec((256, 1024), lambda i: (0, jnp.clip(i - 8, 0, 1))),
            pl.BlockSpec((1024, 256), lambda i: (jnp.clip(i - 10, 0, 7) % 2, jnp.clip(i - 10, 0, 7) // 2)),
            pl.BlockSpec((1, 1024, 256), lambda i: (jnp.clip(i - 18, 0, 5) // 2, jnp.clip(i - 18, 0, 5) % 2, 0)),
        ),
        compiler_params=pltpu.CompilerParams(vmem_limit_bytes=32 << 20),
    )(pieces)
    return down, out, up, qkv.transpose(1, 0, 2)


def on_device(*args):
    pieces, output, input_grad, sums = run_block(*args)
    grad_w_down, grad_w_out, grad_w_up, grad_w_qkv = widen(pieces)
    wide = sums[:6].reshape(3, 2048)
    bias_total = wide[2]
    return (
        output, input_grad, wide[0], wide[1], grad_w_qkv, sums[7, :768].reshape(3, 256), grad_w_out,
        bias_total, grad_w_up, sums[6], grad_w_down, bias_total,
    )


def solution(mesh):
    placed = (
        P(("dp", "tensor"), None),
        P("dp"),
        P(),
        P(),
        P(None, None, "tensor"),
        P(None, "tensor"),
        P("tensor", None),
        P(),
        P(None, "tensor"),
        P("tensor"),
        P("tensor", None),
        P(),
        P(("dp", "tensor"), None),
    )
    return jax.shard_map(
        on_device,
        mesh=mesh,
        in_specs=placed,
        out_specs=(
            P(("dp", "tensor"), None),
            P(("dp", "tensor"), None),
            P(),
            P(),
            P(None, None, "tensor"),
            P(None, "tensor"),
            P("tensor", None),
            P(),
            P(None, "tensor"),
            P("tensor"),
            P("tensor", None),
            P(),
        ),
        check_vma=False,
    )
```

```python
import jax
import jax.numpy as jnp
from jax import lax
from jax.experimental import pallas as pl
from jax.experimental.pallas import tpu as pltpu
from jax.sharding import PartitionSpec as P

HEAD_DIM = 64
ROT = 32
EPSILON = 1e-05
MESH = pl.DeviceIdType.MESH
BF = jnp.bfloat16
F32 = jnp.float32
NP = 24
VMEM_LIMIT = 64 << 20


def neighbours():
    dp = lax.axis_index("dp")
    tensor = lax.axis_index("tensor")
    y, zh, core = dp // 4, (dp // 2) % 2, dp % 2
    zl, x = tensor // 4, tensor % 4
    yl, yr, yo = (y + 3) % 4, (y + 1) % 4, (y + 2) % 4
    xl, xr, xo = (x + 3) % 4, (x + 1) % 4, (x + 2) % 4
    where = dict(y=y, core=core, zl=zl, x=x, yl=yl, yr=yr, yo=yo, xl=xl, xr=xr, xo=xo)
    where["dev_yl"] = (yl * 4 + zh * 2 + core, tensor)
    where["dev_yr"] = (yr * 4 + zh * 2 + core, tensor)
    where["dev_zh"] = (y * 4 + (1 - zh) * 2 + core, tensor)
    where["dev_core"] = (y * 4 + zh * 2 + 1 - core, tensor)
    where["dev_xl"] = (dp, zl * 4 + xl)
    where["dev_xr"] = (dp, zl * 4 + xr)
    where["dev_zl"] = (dp, (1 - zl) * 4 + x)
    return where


def greet(devices):
    barrier = pltpu.get_barrier_semaphore()
    for device in devices:
        pl.semaphore_signal(barrier, inc=1, device_id=device, device_id_type=MESH)
    pl.semaphore_wait(barrier, len(devices))


def rcopy(src, dst, send, recv, device):
    return pltpu.make_async_remote_copy(
        src_ref=src, dst_ref=dst, send_sem=send, recv_sem=recv, device_id=device, device_id_type=MESH
    )


def rows_at(index, size, count=None):
    return pl.ds(pl.multiple_of(index * size, size), size if count is None else count)


class GradSum:
    def scratch():
        return [
            pltpu.VMEM((2, 1024, 256), BF),
            pltpu.VMEM((2, 512, 256), BF),
            pltpu.VMEM((4, 512, 256), BF),
            pltpu.VMEM((4, 2, 64, 256), BF),
            pltpu.VMEM((4, 2, 128, 256), BF),
            pltpu.VMEM((4, 128, 256), BF),
            pltpu.VMEM((4, 128, 256), BF),
            pltpu.VMEM((4, 128, 256), BF),
            pltpu.SemaphoreType.DMA((11, 8)),
            pltpu.SemaphoreType.DMA((11, 8)),
            pltpu.SemaphoreType.DMA((8,)),
        ]

    def __init__(self, at, out, scratch):
        self.at, self.out = at, out
        (self.own, self.other, self.half, self.r1, self.r2, self.zs, self.zr, self.full,
         self.send, self.recv, self.local) = scratch

    def core_copy(self, p):
        s, at = p % 4, self.at
        return rcopy(self.own.at[p % 2, rows_at(1 - at["core"], 512)], self.other.at[p % 2],
                     self.send.at[0, p % 8], self.recv.at[0, p % 8], at["dev_core"])

    def first_copies(self, p):
        s, at = p % 4, self.at
        top = self.half.at[s, rows_at(at["yo"], 128, 64)]
        low = self.half.at[s, pl.ds(pl.multiple_of(at["yo"] * 128 + 64, 64), 64)]
        return (rcopy(top, self.r1.at[s, 0], self.send.at[1, p % 8], self.recv.at[1, p % 8], at["dev_yr"]),
                rcopy(low, self.r1.at[s, 1], self.send.at[2, p % 8], self.recv.at[2, p % 8], at["dev_yl"]))

    def second_copies(self, p):
        s, at = p % 4, self.at
        return (rcopy(self.half.at[s, rows_at(at["yr"], 128)], self.r2.at[s, 0],
                      self.send.at[3, p % 8], self.recv.at[3, p % 8], at["dev_yr"]),
                rcopy(self.half.at[s, rows_at(at["yl"], 128)], self.r2.at[s, 1],
                      self.send.at[4, p % 8], self.recv.at[4, p % 8], at["dev_yl"]))

    def z_copy(self, p):
        s = p % 4
        return rcopy(self.zs.at[s], self.zr.at[s], self.send.at[5, p % 8], self.recv.at[5, p % 8],
                     self.at["dev_zh"])

    def back_first(self, p):
        s, at = p % 4, self.at
        mine = self.out.at[p, rows_at(at["core"] * 4 + at["y"], 128)]
        return (rcopy(self.full.at[s], mine, self.send.at[6, p % 8], self.recv.at[6, p % 8], at["dev_yr"]),
                rcopy(self.full.at[s], mine, self.send.at[7, p % 8], self.recv.at[7, p % 8], at["dev_yl"]),
                pltpu.make_async_copy(self.full.at[s], mine, self.local.at[p % 8]))

    def back_second(self, p):
        s, at = p % 4, self.at
        top = self.out.at[p, rows_at(at["core"] * 4 + at["yl"], 128, 64)]
        low = self.out.at[p, pl.ds(pl.multiple_of((at["core"] * 4 + at["yr"]) * 128 + 64, 64), 64)]
        return (rcopy(top, top, self.send.at[9, p % 8], self.recv.at[9, p % 8], at["dev_yr"]),
                rcopy(low, low, self.send.at[10, p % 8], self.recv.at[10, p % 8], at["dev_yl"]))

    def back_core(self, p):
        s, at = p % 4, self.at
        mine = self.out.at[p, rows_at(at["core"], 512)]
        return rcopy(mine, mine, self.send.at[8, p % 8], self.recv.at[8, p % 8], at["dev_core"])

    def send_piece(self, p):
        self.core_copy(p).start()

    def add_core(self, p):
        s = p % 4
        self.core_copy(p).wait()

        @pl.loop(0, 4)
        def _(j):
            rows = rows_at(j, 128)
            mine = self.own[p % 2, pl.ds(pl.multiple_of(self.at["core"] * 512 + j * 128, 128), 128)]
            self.half[s, rows] = (mine.astype(F32) + self.other[p % 2, rows].astype(F32)).astype(BF)

        for copy in self.first_copies(p):
            copy.start()

    def add_first(self, p):
        s, at = p % 4, self.at
        for copy in self.first_copies(p):
            copy.wait()
        top = rows_at(at["yr"], 128, 64)
        low = pl.ds(pl.multiple_of(at["yl"] * 128 + 64, 64), 64)
        self.half[s, top] = (self.half[s, top].astype(F32) + self.r1[s, 0].astype(F32)).astype(BF)
        self.half[s, low] = (self.half[s, low].astype(F32) + self.r1[s, 1].astype(F32)).astype(BF)
        for copy in self.second_copies(p):
            copy.start()

    def add_second(self, p):
        s = p % 4
        for copy in self.second_copies(p):
            copy.wait()
        mine = self.half[s, rows_at(self.at["y"], 128)].astype(F32)
        self.zs[s] = (mine + self.r2[s, 0].astype(F32) + self.r2[s, 1].astype(F32)).astype(BF)
        self.z_copy(p).start()

    def add_z(self, p):
        s = p % 4
        self.z_copy(p).wait()
        self.full[s] = (self.zs[s].astype(F32) + self.zr[s].astype(F32)).astype(BF)
        for copy in self.back_first(p):
            copy.start()

    def forward_y(self, p):
        for copy in self.back_first(p):
            copy.wait()
        for copy in self.back_second(p):
            copy.start()

    def forward_core(self, p):
        for copy in self.back_second(p):
            copy.wait()
        self.back_core(p).start()

    def finish(self, p):
        self.back_core(p).wait()

    def steps(self, t):
        for lag, step in ((1, self.add_core), (2, self.add_first), (3, self.add_second), (4, self.add_z),
                          (6, self.forward_y), (8, self.forward_core), (9, self.finish)):
            p = t - lag
            pl.when((p >= 0) & (p < NP))(lambda step=step, p=p: step(p))


def dot(a, b):
    return lax.dot_general(a, b, (((1,), (0,)), ((), ())), preferred_element_type=F32)


def dot_nt(a, b):
    return lax.dot_general(a, b, (((1,), (1,)), ((), ())), preferred_element_type=F32)


def at_rows(index, size=256):
    return pl.ds(pl.multiple_of(index * size, size), size)


class Gather:
    AHEAD = 2

    def scratch():
        return [
            pltpu.VMEM((16, 128, 256), BF),
            pltpu.VMEM((8, 1024, 256), BF),
            pltpu.SemaphoreType.DMA((9, 8)),
            pltpu.SemaphoreType.DMA((9, 8)),
        ]

    def __init__(self, at, scratch):
        self.at = at
        self.own, self.all, self.send, self.recv = scratch

    def copy(self, kind, c, src, dst, device):
        s = c % 8
        return rcopy(src, dst, self.send.at[kind, s], self.recv.at[kind, s], self.at[device])

    def part(self, c, zl, x, begin=0, count=128):
        first = pl.multiple_of((zl * 4 + x) * 128 + begin, 64)
        return self.all.at[c % 8, pl.ds(first, count)]

    def same(self, kind, c, block, device):
        return self.copy(kind, c, block, block, device)

    def first(self, c, wide):
        at = self.at
        src, dst = self.own.at[c], self.part(c, at["zl"], at["x"])
        copies = [self.copy(0, c, src, dst, "dev_xr"), self.copy(1, c, src, dst, "dev_xl")]
        return copies if wide else copies + [self.copy(2, c, src, dst, "dev_zl")]

    def ring(self, c):
        at = self.at
        return [self.same(3, c, self.part(c, at["zl"], at["xl"], 0, 64), "dev_xr"),
                self.same(4, c, self.part(c, at["zl"], at["xr"], 64, 64), "dev_xl")]

    def second(self, c, wide):
        at = self.at
        if wide:
            return [self.copy(5, c, self.own.at[c], self.part(c, at["zl"], at["x"]), "dev_zl"),
                    self.same(6, c, self.part(c, at["zl"], at["xl"]), "dev_zl"),
                    self.same(7, c, self.part(c, at["zl"], at["xr"]), "dev_zl")]
        other = self.part(c, 1 - at["zl"], at["x"])
        return [self.same(5, c, other, "dev_xr"), self.same(6, c, other, "dev_xl")]

    def third(self, c, wide):
        at = self.at
        if wide:
            return [self.same(8, c, self.part(c, at["zl"], at["xo"]), "dev_zl")]
        return [self.same(7, c, self.part(c, 1 - at["zl"], at["xl"], 0, 64), "dev_xr"),
                self.same(8, c, self.part(c, 1 - at["zl"], at["xr"], 64, 64), "dev_xl")]

    def begin(self, c):
        def start(wide):
            for copy in self.first(c, wide):
                copy.start()

        self.either(c, start)
        self.part(c, self.at["zl"], self.at["x"])[...] = self.own[c]

    def either(self, c, step):
        wide = (c % 2 == 1) & (c < WIDE)
        pl.when((c >= 0) & (c < 16) & wide)(lambda: step(True))
        pl.when((c >= 0) & (c < 16) & jnp.logical_not(wide))(lambda: step(False))

    def steps(self, c):
        def second(wide):
            for copy in self.first(c, wide):
                copy.wait()
            for copy in self.ring(c) + self.second(c, wide):
                copy.start()

        def third(wide):
            for copy in self.ring(c - 1) if wide else self.ring(c - 1) + self.second(c - 1, wide):
                copy.wait()
            for copy in self.third(c - 1, wide):
                copy.start()

        def last(wide):
            for copy in self.second(c - 2, wide) + self.third(c - 2, wide) if wide else self.third(c - 2, wide):
                copy.wait()

        self.either(c, second)
        pl.when(c + self.AHEAD < 16)(lambda: self.begin(c + self.AHEAD))
        self.either(c - 1, third)
        self.either(c - 2, last)


class RowSum:
    def scratch():
        return [
            pltpu.VMEM((4, 2, 4, 128, 256), BF),
            pltpu.VMEM((8, 2, 2, 64, 256), BF),
            pltpu.VMEM((4, 2, 2, 128, 256), BF),
            pltpu.VMEM((4, 128, 256), BF),
            pltpu.VMEM((4, 128, 256), BF),
            pltpu.VMEM((4, 128, 256), F32),
            pltpu.SemaphoreType.DMA((5, 8)),
            pltpu.SemaphoreType.DMA((5, 8)),
        ]

    def __init__(self, at, scratch, result):
        self.at, self.result = at, result
        self.part, self.r1, self.r2, self.zs, self.zr, self.mine, self.send, self.recv = scratch

    def copy(self, kind, c, src, dst, device):
        s = c % 8
        return rcopy(src, dst, self.send.at[kind, s], self.recv.at[kind, s], device)

    def first(self, c):
        s, at = c % 4, self.at
        return [self.copy(0, c, self.part.at[s, :, at["xo"], pl.ds(0, 64)], self.r1.at[c % 8, 0], at["dev_xr"]),
                self.copy(1, c, self.part.at[s, :, at["xo"], pl.ds(64, 64)], self.r1.at[c % 8, 1], at["dev_xl"])]

    def second(self, c):
        s, at = c % 4, self.at
        return [self.copy(2, c, self.part.at[s, :, at["xr"]], self.r2.at[s, 0], at["dev_xr"]),
                self.copy(3, c, self.part.at[s, :, at["xl"]], self.r2.at[s, 1], at["dev_xl"])]

    def third(self, c):
        s = c % 4
        return [self.copy(4, c, self.zs.at[s], self.zr.at[s], self.at["dev_zl"])]

    def store(self, c, value):
        for k in range(8):
            self.part[c % 4, k // 4, k % 4] = value[k * 128:(k + 1) * 128].astype(BF)

    def send_chunk(self, c):
        for copy in self.first(c):
            copy.start()

    def add_first(self, c):
        s, at = c % 4, self.at
        for copy in self.first(c):
            copy.wait()
        for z in range(2):
            top = self.part[s, z, at["xr"], 0:64].astype(F32) + self.r1[c % 8, 0, z].astype(F32)
            self.part[s, z, at["xr"], 0:64] = top.astype(BF)
            low = self.part[s, z, at["xl"], 64:128].astype(F32) + self.r1[c % 8, 1, z].astype(F32)
            self.part[s, z, at["xl"], 64:128] = low.astype(BF)
        for copy in self.second(c):
            copy.start()

    def add_second(self, c):
        s, at = c % 4, self.at
        for copy in self.second(c):
            copy.wait()

        def total(z):
            own = self.part[s, z, at["x"]].astype(F32)
            return own + self.r2[s, 0, z].astype(F32) + self.r2[s, 1, z].astype(F32)

        self.zs[s] = total(1 - at["zl"]).astype(BF)
        for copy in self.third(c):
            copy.start()
        self.mine[s] = total(at["zl"])

    def add_third(self, c):
        s = c % 4
        for copy in self.third(c):
            copy.wait()
        self.result(c, self.mine[s] + self.zr[s].astype(F32))

    def steps(self, t):
        for lag, step in ((2, self.add_first), (3, self.add_second), (4, self.add_third)):
            c = t - lag
            pl.when((c >= 0) & (c < 8))(lambda step=step, c=c: step(c))
            pl.when((c >= 10) & (c < 18))(lambda step=step, c=c - 2: step(c))


class SmallSum:
    def scratch():
        return [
            pltpu.VMEM((8, 8, 1024), F32),
            pltpu.VMEM((4, 8, 1024), F32),
            pltpu.VMEM((4, 8, 1024), F32),
            pltpu.SemaphoreType.DMA((13,)),
            pltpu.SemaphoreType.DMA((13,)),
        ]

    def __init__(self, scratch):
        self.b1, self.b2, self.b3, self.send, self.recv = scratch
        dp, tensor = lax.axis_index("dp"), lax.axis_index("tensor")
        y, self.zh, core = dp // 4, (dp // 2) % 2, dp % 2
        self.zl, self.x = tensor // 4, tensor % 4
        self.i1 = y * 2 + core
        self.i2 = self.zh * 2 + self.zl
        self.d1, self.d2, self.d3 = [], [], []
        for k in range(1, 8):
            j = (self.i1 + k) % 8
            self.d1.append(((j // 2) * 4 + self.zh * 2 + j % 2, tensor))
        for k in range(1, 4):
            j = (self.i2 + k) % 4
            self.d2.append((y * 4 + (j // 2) * 2 + core, (j % 2) * 4 + self.x))
            self.d3.append((dp, self.zl * 4 + (self.x + k) % 4))

    def devices(self):
        return self.d1 + self.d2 + self.d3

    def copies(self, stage):
        buf, mine, devices, base = ((self.b1, self.i1, self.d1, 0), (self.b2, self.i2, self.d2, 7),
                                    (self.b3, self.x, self.d3, 10))[stage]
        return [rcopy(buf.at[mine], buf.at[mine], self.send.at[base + k], self.recv.at[base + k], device)
                for k, device in enumerate(devices)]

    def start(self, stage):
        for copy in self.copies(stage):
            copy.start()

    def wait(self, stage):
        for copy in self.copies(stage):
            copy.wait()

    def second(self):
        self.wait(0)
        total = self.b1[0]
        for k in range(1, 8):
            total = total + self.b1[k]
        self.b2[self.i2] = total
        self.start(1)

    def third(self):
        self.wait(1)
        wide = self.b2[0] + self.b2[1] + self.b2[2] + self.b2[3]
        narrow = self.b2[self.zl] + self.b2[2 + self.zl]
        row = lax.broadcasted_iota(jnp.int32, (8, 1024), 0)
        self.b3[self.x] = jnp.where(row < 6, wide, narrow)
        self.start(2)

    def result(self):
        self.wait(2)
        wide = self.b3[0] + self.b3[1] + self.b3[2] + self.b3[3]
        row = lax.broadcasted_iota(jnp.int32, (8, 1024), 0)
        return jnp.where(row < 6, wide, self.b3[self.x])


def gelu_parts(u):
    inner = 0.7978845608028654 * (u + 0.044715 * (u * u * u))
    return jnp.tanh(inner)


def swap_pairs(v):
    lane = lax.broadcasted_iota(jnp.int32, v.shape, 1)
    return jnp.where(lane % 32 < 16, pltpu.roll(v, 112, 1), pltpu.roll(v, 16, 1))


def turn(v, cosine, sine):
    return v * cosine + swap_pairs(v) * sine


WIDE = 14
RS = 8
FEAT, MID = 1792, 1280


def block_kernel(
    tokens, cotangent, seg_row, gain_h, shift_h, b_qkv, b_out_h, b_up_h, b_down_h,
    w_qkv_h, w_out_h, w_up_h, w_down_h,
    pieces, output, input_grad, sums,
    w_in, w_mid, w_sem,
    gain, shift, b_sum,
    normed_t, pre, grad_mid, rows, turned, mid, heads_t, outs_g, outs_gt, grad_feat,
    cos_t, sin_t, seg_c, seg_r, lse, bias, p_f, q_m, g_m, ds_b, mean_row, rstd,
    *scratch,
):
    at = neighbours()
    grad_n = p_f
    dp_f = grad_mid.at[:, pl.ds(0, 256)]
    act_t = grad_feat
    n1, n2, n3 = len(GradSum.scratch()), len(Gather.scratch()), len(RowSum.scratch())
    small = SmallSum(scratch[n1 + n2 + n3:])
    grads = GradSum(at, pieces, scratch[:n1])
    gather = Gather(at, scratch[n1:n1 + n2])

    def keep_rows(c, value):
        @pl.when(c < 8)
        def _():
            cols = at_rows(c)
            own = tokens[:, cols].astype(F32) + value + b_sum[0:1, cols]
            output[:, cols] = own.astype(BF)

        @pl.when(c >= 8)
        def _():
            grad_n[at_rows(c - 8, 128), :] = value

    row_sum = RowSum(at, scratch[n1 + n2:n1 + n2 + n3], keep_rows)

    moves = [(w_up_h, w_in.at[:, pl.ds(0, 1024)])]
    moves += [(w_qkv_h.at[k], w_in.at[:, pl.ds(1024 + 256 * k, 256)]) for k in range(3)]
    moves += [(w_down_h, w_mid.at[pl.ds(0, 1024)]), (w_out_h, w_mid.at[pl.ds(1024, 256)])]
    weights = [pltpu.make_async_copy(src, dst, w_sem.at[i]) for i, (src, dst) in enumerate(moves)]

    barrier = pltpu.get_barrier_semaphore()
    greeted = small.devices()
    for device in greeted:
        pl.semaphore_signal(barrier, inc=1, device_id=device, device_id_type=MESH)
    for copy in weights:
        copy.start()

    gain[...] = gain_h[...].astype(F32)
    shift[...] = shift_h[...].astype(F32)
    b_sum[...] = b_out_h[...].astype(F32) + b_down_h[...].astype(F32)
    x = tokens[...].astype(F32)
    mean = jnp.mean(x, axis=1, keepdims=True)
    centered = x - mean
    scale = lax.rsqrt(jnp.mean(centered * centered, axis=1, keepdims=True) + EPSILON)
    rstd[...] = jnp.broadcast_to(scale, (128, 128))
    mean_row[...] = jnp.broadcast_to(mean, (128, 128))

    def unit(cols):
        return (tokens[:, cols].astype(F32) - mean_row[:, 0:1]) * rstd[:, 0:1]

    for c in range(8):
        cols = slice(c * 256, c * 256 + 256)
        gather.own[c] = (unit(cols) * gain[0:1, cols] + shift[0:1, cols]).astype(BF)
        gather.own[8 + c] = cotangent[:, cols]

    pl.semaphore_wait(barrier, len(greeted))
    for c in range(Gather.AHEAD):
        gather.begin(c)

    seg_f = seg_row[...].astype(F32)
    seg_r[...] = jnp.broadcast_to(seg_f, (8, 1024))
    seg_c[...] = jnp.broadcast_to(seg_f, (128, 1024)).T
    @pl.loop(0, 4)
    def _(b):
        r = at_rows(b)
        i = lax.broadcasted_iota(jnp.int32, (256, 1024), 0) + b * 256
        j = lax.broadcasted_iota(jnp.int32, (256, 1024), 1)
        same = jnp.where((seg_c[r, 0:1] == seg_r[0:1, :]) & (j < i), 1.0, 0.0)
        position = jnp.sum(same, axis=1, keepdims=True)
        lane = lax.broadcasted_iota(jnp.int32, (256, 128), 1) % 64
        power = jnp.exp((lane % 16).astype(F32) * (-2.0 / ROT * 9.210340371976184))
        angle = position * power
        sine = jnp.sin(angle)
        cos_t[r, :] = jnp.where(lane < ROT, jnp.cos(angle), 1.0)
        sin_t[r, :] = jnp.where(lane < ROT // 2, -sine, jnp.where(lane < ROT, sine, 0.0))
        pre[r, 0:1024] = jnp.broadcast_to(b_up_h[...].astype(F32), (256, 1024))
        for k in range(3):
            cols = slice(1024 + k * 256, 1280 + k * 256)
            pre[r, cols] = jnp.broadcast_to(b_qkv[k:k + 1, :].astype(F32), (256, 256))

    @pl.loop(0, 10)
    def _(i):
        gather.steps(i)

        @pl.when(i == 2)
        def _():
            for copy in weights[:4]:
                copy.wait()

        @pl.when(i >= 2)
        def _():
            c = i - 2

            @pl.loop(0, 2)
            def _(b):
                r = at_rows(b, 512)
                a = gather.all[c % 8, r, :]
                pre[r, :] += dot(a, w_in[at_rows(c), :])
            normed_t[at_rows(c), :] = gather.all[c % 8].T

    @pl.loop(0, 4)
    def _(b):
        r = at_rows(b)
        for k in range(4):
            cols = slice(k * 256, k * 256 + 256)
            u = pre[r, cols]
            a = (u * (0.5 * (1.0 + gelu_parts(u)))).astype(BF)
            mid[r, cols] = a
            act_t[cols, r] = a.T

    for copy in weights[4:]:
        copy.wait()
    gather.steps(10)

    def make_rows(b):
        r = at_rows(b)
        for k in range(3):
            for half in range(2):
                v = pre[r, 1024 + k * 256 + half * 128:1152 + k * 256 + half * 128]
                if k < 2:
                    v = turn(v, cos_t[r, :], sin_t[r, :])
                if k == 0:
                    v = v * HEAD_DIM ** -0.5
                v = v.astype(BF)
                cols = slice(half * 128, half * 128 + 128)
                rows[k, r, cols] = v
                turned[k, cols, r] = v.T

    def attend_bias(qb):
        cols = slice(qb * 256, qb * 256 + 256)
        for kb in range(qb + 1):
            r = slice(kb * 256, kb * 256 + 256)
            keep = seg_c[r, 0:1] == seg_r[0:1, cols]
            if kb == qb:
                i = lax.broadcasted_iota(jnp.int32, (256, 256), 0)
                j = lax.broadcasted_iota(jnp.int32, (256, 256), 1)
                keep = keep & (i <= j)
            bias[r, :] = jnp.where(keep, 0.0, -1e30).astype(BF)

    def one_head(ref, source, h, cols):
        ref[...] = jnp.zeros_like(ref)
        ref[head_rows(h), :] = source[head_rows(h), cols]

    def head_rows(h):
        return pl.ds(pl.multiple_of(h * 64, 64), 64)

    def attend(qb):
        cols = slice(qb * 256, qb * 256 + 256)
        n = (qb + 1) * 256
        attend_bias(qb)

        @pl.loop(0, 4)
        def _(h):
            hr = head_rows(h)
            one_head(q_m, turned.at[0], h, cols)
            s = dot(rows[1, 0:n, :], q_m[...]) + bias[0:n, :].astype(F32)
            p_f[0:n, :] = s
            most = jnp.max(s, axis=0, keepdims=True)
            e = jnp.exp(p_f[0:n, :] - most)
            p_f[0:n, :] = e
            total = jnp.sum(e, axis=0, keepdims=True)
            ds_b[0:n, :] = (p_f[0:n, :] * (1.0 / total)).astype(BF)
            heads_t[hr, cols] = dot(
                turned[2, hr, 0:n], ds_b[0:n, :]).astype(BF)
            lse[pl.ds(h, 1), cols] = most + jnp.log(total)

    def attend_back(qb, first_head):
        cols = slice(qb * 256, qb * 256 + 256)
        n = (qb + 1) * 256
        if first_head == 0:
            attend_bias(qb)

        @pl.loop(first_head, first_head + 2)
        def _(h):
            hr = head_rows(h)
            one_head(q_m, turned.at[0], h, cols)
            one_head(g_m, outs_gt, h, cols)
            p = jnp.exp(dot(rows[1, 0:n, :], q_m[...]) + bias[0:n, :].astype(F32) - lse[pl.ds(h, 1), cols])
            p_f[0:n, :] = p
            d = dot(rows[2, 0:n, :], g_m[...])
            dp_f[0:n, :] = d
            delta = jnp.sum(p_f[0:n, :] * d, axis=0, keepdims=True)
            lane = lax.broadcasted_iota(jnp.int32, (256, 256), 1) // 64
            q_h = jnp.where(lane == h, rows[0, cols, :].astype(F32), 0.0).astype(BF)
            g_h = jnp.where(lane == h, outs_g[cols, :].astype(F32), 0.0).astype(BF)
            pre[0:n, 1536:1792] += dot(p_f[0:n, :].astype(BF), g_h)
            ds_b[0:n, :] = (p_f[0:n, :] * (dp_f[0:n, :] - delta)).astype(BF)
            pre[0:n, 1280:1536] += dot(ds_b[0:n, :], q_h)
            pre[pl.ds(pl.multiple_of(qb * 256 + h * 64, 64), 64), 1024:1280] = dot(
                turned[1, hr, 0:n], ds_b[0:n, :])

    @pl.loop(0, 8)
    def _(t):
        grads.steps(t)
        chunk = gather.all[t]
        grads.own[t % 2] = dot(act_t[:, 0:1024], chunk).astype(BF)
        grads.send_piece(t)
        gather.steps(11 + t)

        @pl.when(t == 0)
        def _():
            grad_mid[...] = jnp.zeros_like(grad_mid)

        @pl.loop(0, 2)
        def _(b):
            r = at_rows(b, 512)
            grad_mid[r, :] += dot_nt(gather.all[t, r, :], w_mid[:, at_rows(t)])

        pl.when(t < 4)(lambda: make_rows(t))
        for qb in range(4):
            pl.when(t == 4 + qb)(lambda qb=qb: attend(qb))

    def branch_chunk(c):
        row_sum.store(c, dot(mid[...], w_mid[:, at_rows(c)]))
        row_sum.send_chunk(c)

    def normed_chunk(c):
        row_sum.store(c + 8, dot_nt(grad_feat[...], w_in[at_rows(c), :]))
        row_sum.send_chunk(c + 8)

    @pl.loop(0, 4)
    def _(b):
        r = at_rows(b)
        mid[r, 1024:1280] = heads_t[:, r].T
        g = grad_mid[r, 1024:1280].astype(BF)
        outs_g[r, :] = g
        outs_gt[:, r] = g.T

    @pl.loop(8, 10)
    def _(t):
        grads.steps(t)
        row_sum.steps(t - RS)
        for j in range(4):
            r = slice(j * 256, j * 256 + 256)
            grads.own[t % 2, r, :] = dot(heads_t[...], gather.all[4 * (t - 8) + j]).astype(BF)
        grads.send_piece(t)
        branch_chunk(t - RS)

        @pl.loop(2 * (t - 8), 2 * (t - 8) + 2)
        def _(b):
            r = at_rows(b)
            for k in range(4):
                cols = slice(k * 256, k * 256 + 256)
                u = pre[r, cols]
                th = gelu_parts(u)
                slope = 0.5 * (1.0 + th) + 0.5 * u * (1.0 - th * th) * (
                    0.7978845608028654 * (1.0 + 3 * 0.044715 * (u * u)))
                grad_feat[r, cols] = (slope * grad_mid[r, cols]).astype(BF)
            pre[r, 1024:1792] = jnp.zeros((256, 768), F32)

    def feature_piece(t):
        q = t - 10
        grads.own[t % 2] = dot(
            normed_t[at_rows(q % 2, 1024), :], grad_feat[:, at_rows(q // 2)]).astype(BF)
        grads.send_piece(t)

    @pl.loop(10, 18)
    def _(t):
        grads.steps(t)
        row_sum.steps(t - RS)
        feature_piece(t)
        pl.when(t < RS + 8)(lambda: branch_chunk(t - RS))
        for qb in range(4):
            for half in range(2):
                pl.when(t == 10 + 2 * qb + half)(lambda qb=qb, half=half: attend_back(qb, 2 * half))

    for b in range(4):
        r = slice(b * 256, b * 256 + 256)
        grad_q = pre[r, 1024:1280].T * HEAD_DIM ** -0.5
        for half in range(2):
            a = half * 128
            cosine, sine = cos_t[r, :], -sin_t[r, :]
            grad_feat[r, 1024 + a:1152 + a] = turn(grad_q[:, a:a + 128], cosine, sine).astype(BF)
            grad_feat[r, 1280 + a:1408 + a] = turn(pre[r, 1280 + a:1408 + a], cosine, sine).astype(BF)
        grad_feat[r, 1536:1792] = pre[r, 1536:1792].astype(BF)

    @pl.loop(18, 24)
    def _(t):
        grads.steps(t)
        row_sum.steps(t - RS)
        feature_piece(t)
        normed_chunk(t - 18)

    @pl.loop(24, 30)
    def _(t):
        grads.steps(t)
        row_sum.steps(t - RS)
        pl.when(t < 26)(lambda: normed_chunk(t - 18))

    def column_sum(value):
        return jnp.sum(value.astype(F32), axis=0, keepdims=True)

    mine = small.i1
    small.b1[mine] = jnp.zeros((8, 1024), F32)
    mean_plain = jnp.zeros((128, 1), F32)
    mean_unit = jnp.zeros((128, 1), F32)
    for c in range(8):
        cols = slice(c * 256, c * 256 + 256)
        row, lanes = c // 4, slice((c % 4) * 256, (c % 4) * 256 + 256)
        g = grad_n[c * 128:c * 128 + 128, :]
        n = unit(cols)
        scaled = g * gain[0:1, cols]
        mean_plain = mean_plain + jnp.sum(scaled, axis=1, keepdims=True)
        mean_unit = mean_unit + jnp.sum(scaled * n, axis=1, keepdims=True)
        small.b1[mine, row:row + 1, lanes] = column_sum(g * n)
        small.b1[mine, 2 + row:3 + row, lanes] = column_sum(g)
        small.b1[mine, 4 + row:5 + row, lanes] = column_sum(cotangent[:, cols])
    for k in range(7):
        row, lanes = 6 + k // 4, slice((k % 4) * 256, (k % 4) * 256 + 256)
        small.b1[mine, row:row + 1, lanes] = column_sum(grad_feat[:, k * 256:k * 256 + 256])
    small.start(0)
    grads.steps(30)
    mean_plain = mean_plain / 2048.0
    mean_unit = mean_unit / 2048.0
    for c in range(8):
        cols = slice(c * 256, c * 256 + 256)
        inner = grad_n[c * 128:c * 128 + 128, :] * gain[0:1, cols] - mean_plain - unit(cols) * mean_unit
        input_grad[:, cols] = (cotangent[:, cols].astype(F32) + rstd[:, 0:1] * inner).astype(BF)

    small.second()
    grads.steps(31)
    small.third()
    grads.steps(32)
    sums[...] = small.result()


def run_block(tokens, segment, ln_gain, ln_bias, w_qkv, b_qkv, w_out, b_out, w_up, b_up, w_down,
              b_down, cotangent):
    vmem = pl.BlockSpec(memory_space=pltpu.VMEM)
    hbm = pl.BlockSpec(memory_space=pl.ANY)
    V = pltpu.VMEM
    scratch = [
        V((2048, FEAT), BF), V((MID, 2048), BF), pltpu.SemaphoreType.DMA((6,)),
        V((1, 2048), F32), V((1, 2048), F32), V((1, 2048), F32),
        V((2048, 1024), BF),
        V((1024, FEAT), F32), V((1024, MID), F32),
        V((3, 1024, 256), BF), V((3, 256, 1024), BF),
        V((1024, MID), BF), V((256, 1024), BF),
        V((1024, 256), BF), V((256, 1024), BF),
        V((1024, FEAT), BF),
        V((1024, 128), F32), V((1024, 128), F32),
        V((1024, 128), F32), V((8, 1024), F32),
        V((8, 1024), F32),
        V((1024, 256), BF), V((1024, 256), F32),
        V((256, 256), BF), V((256, 256), BF), V((1024, 256), BF),
        V((128, 128), F32), V((128, 128), F32),
    ] + GradSum.scratch() + Gather.scratch() + RowSum.scratch() + SmallSum.scratch()
    return pl.pallas_call(
        block_kernel,
        out_shape=(
            jax.ShapeDtypeStruct((NP, 1024, 256), BF),
            jax.ShapeDtypeStruct((128, 2048), BF),
            jax.ShapeDtypeStruct((128, 2048), BF),
            jax.ShapeDtypeStruct((8, 1024), F32),
        ),
        in_specs=[vmem] * 9 + [hbm] * 4,
        out_specs=(hbm, vmem, vmem, vmem),
        scratch_shapes=scratch,
        compiler_params=pltpu.CompilerParams(
            collective_id=0, has_side_effects=True, vmem_limit_bytes=VMEM_LIMIT),
        cost_estimate=pl.CostEstimate(flops=50 * 10**9, bytes_accessed=30 << 20, transcendentals=10**7),
    )(
        tokens, cotangent, segment.reshape(1, 1024), ln_gain.reshape(1, 2048),
        ln_bias.reshape(1, 2048), b_qkv, b_out.reshape(1, 2048), b_up.reshape(1, 1024),
        b_down.reshape(1, 2048), w_qkv.transpose(1, 0, 2), w_out, w_up, w_down,
    )


def widen_kernel(piece, down, out, up, qkv):
    i = pl.program_id(0)
    value = piece[0]

    @pl.when(i < 8)
    def _():
        down[...] = value.astype(F32)

    @pl.when((i >= 8) & (i < 10))
    def _():
        for j in range(4):
            out[:, j * 256:j * 256 + 256] = piece[0, j * 256:j * 256 + 256, :].astype(F32)

    @pl.when((i >= 10) & (i < 18))
    def _():
        up[...] = value.astype(F32)

    @pl.when(i >= 18)
    def _():
        qkv[0] = value.astype(F32)


def widen(pieces):
    down, out, up, qkv = pl.pallas_call(
        widen_kernel,
        grid=(NP,),
        out_shape=(
            jax.ShapeDtypeStruct((1024, 2048), F32),
            jax.ShapeDtypeStruct((256, 2048), F32),
            jax.ShapeDtypeStruct((2048, 1024), F32),
            jax.ShapeDtypeStruct((3, 2048, 256), F32),
        ),
        in_specs=[pl.BlockSpec((1, 1024, 256), lambda i: (i, 0, 0))],
        out_specs=(
            pl.BlockSpec((1024, 256), lambda i: (0, jnp.minimum(i, 7))),
            pl.BlockSpec((256, 1024), lambda i: (0, jnp.clip(i - 8, 0, 1))),
            pl.BlockSpec((1024, 256), lambda i: (jnp.clip(i - 10, 0, 7) % 2, jnp.clip(i - 10, 0, 7) // 2)),
            pl.BlockSpec((1, 1024, 256), lambda i: (jnp.clip(i - 18, 0, 5) // 2, jnp.clip(i - 18, 0, 5) % 2, 0)),
        ),
        compiler_params=pltpu.CompilerParams(vmem_limit_bytes=VMEM_LIMIT),
    )(pieces)
    return down, out, up, qkv.transpose(1, 0, 2)


def on_device(*args):
    pieces, output, input_grad, sums = run_block(*args)
    grad_w_down, grad_w_out, grad_w_up, grad_w_qkv = widen(pieces)
    wide = sums[:6].reshape(3, 2048)
    bias_total = wide[2]
    return (
        output, input_grad, wide[0], wide[1], grad_w_qkv, sums[7, :768].reshape(3, 256), grad_w_out,
        bias_total, grad_w_up, sums[6], grad_w_down, bias_total,
    )


def solution(mesh):
    placed = (
        P(("dp", "tensor"), None),
        P("dp"),
        P(),
        P(),
        P(None, None, "tensor"),
        P(None, "tensor"),
        P("tensor", None),
        P(),
        P(None, "tensor"),
        P("tensor"),
        P("tensor", None),
        P(),
        P(("dp", "tensor"), None),
    )
    return jax.shard_map(
        on_device,
        mesh=mesh,
        in_specs=placed,
        out_specs=(
            P(("dp", "tensor"), None),
            P(("dp", "tensor"), None),
            P(),
            P(),
            P(None, None, "tensor"),
            P(None, "tensor"),
            P("tensor", None),
            P(),
            P(None, "tensor"),
            P("tensor"),
            P("tensor", None),
            P(),
        ),
        check_vma=False,
    )
```

```python
import jax
import jax.numpy as jnp
from jax import lax
from jax.experimental import pallas as pl
from jax.experimental.pallas import tpu as pltpu
from jax.sharding import PartitionSpec as P

HEAD_DIM = 64
ROT = 32
EPSILON = 1e-05
MESH = pl.DeviceIdType.MESH
BF = jnp.bfloat16
F32 = jnp.float32
NP = 24
VMEM_LIMIT = 64 << 20


def neighbours():
    dp = lax.axis_index("dp")
    tensor = lax.axis_index("tensor")
    y, zh, core = dp // 4, (dp // 2) % 2, dp % 2
    zl, x = tensor // 4, tensor % 4
    yl, yr, yo = (y + 3) % 4, (y + 1) % 4, (y + 2) % 4
    xl, xr, xo = (x + 3) % 4, (x + 1) % 4, (x + 2) % 4
    where = dict(y=y, core=core, zl=zl, x=x, yl=yl, yr=yr, yo=yo, xl=xl, xr=xr, xo=xo)
    where["dev_yl"] = (yl * 4 + zh * 2 + core, tensor)
    where["dev_yr"] = (yr * 4 + zh * 2 + core, tensor)
    where["dev_zh"] = (y * 4 + (1 - zh) * 2 + core, tensor)
    where["dev_core"] = (y * 4 + zh * 2 + 1 - core, tensor)
    where["dev_xl"] = (dp, zl * 4 + xl)
    where["dev_xr"] = (dp, zl * 4 + xr)
    where["dev_zl"] = (dp, (1 - zl) * 4 + x)
    return where


def greet(devices):
    barrier = pltpu.get_barrier_semaphore()
    for device in devices:
        pl.semaphore_signal(barrier, inc=1, device_id=device, device_id_type=MESH)
    pl.semaphore_wait(barrier, len(devices))


def rcopy(src, dst, send, recv, device):
    return pltpu.make_async_remote_copy(
        src_ref=src, dst_ref=dst, send_sem=send, recv_sem=recv, device_id=device, device_id_type=MESH
    )


def rows_at(index, size, count=None):
    return pl.ds(pl.multiple_of(index * size, size), size if count is None else count)


class GradSum:
    def scratch():
        return [
            pltpu.VMEM((2, 1024, 256), BF),
            pltpu.VMEM((2, 512, 256), BF),
            pltpu.VMEM((4, 512, 256), BF),
            pltpu.VMEM((4, 2, 64, 256), BF),
            pltpu.VMEM((4, 2, 128, 256), BF),
            pltpu.VMEM((4, 128, 256), BF),
            pltpu.VMEM((4, 128, 256), BF),
            pltpu.VMEM((4, 128, 256), BF),
            pltpu.SemaphoreType.DMA((11, 8)),
            pltpu.SemaphoreType.DMA((11, 8)),
            pltpu.SemaphoreType.DMA((8,)),
        ]

    def __init__(self, at, out, scratch):
        self.at, self.out = at, out
        (self.own, self.other, self.half, self.r1, self.r2, self.zs, self.zr, self.full,
         self.send, self.recv, self.local) = scratch

    def place(self, p):
        return jnp.where(p < 8, p + 8, jnp.where(p < 10, p - 2, jnp.where(p < 18, p + 6, p - 18)))

    def core_copy(self, p):
        s, at = p % 4, self.at
        return rcopy(self.own.at[p % 2, rows_at(1 - at["core"], 512)], self.other.at[p % 2],
                     self.send.at[0, p % 8], self.recv.at[0, p % 8], at["dev_core"])

    def first_copies(self, p):
        s, at = p % 4, self.at
        top = self.half.at[s, rows_at(at["yo"], 128, 64)]
        low = self.half.at[s, pl.ds(pl.multiple_of(at["yo"] * 128 + 64, 64), 64)]
        return (rcopy(top, self.r1.at[s, 0], self.send.at[1, p % 8], self.recv.at[1, p % 8], at["dev_yr"]),
                rcopy(low, self.r1.at[s, 1], self.send.at[2, p % 8], self.recv.at[2, p % 8], at["dev_yl"]))

    def second_copies(self, p):
        s, at = p % 4, self.at
        return (rcopy(self.half.at[s, rows_at(at["yr"], 128)], self.r2.at[s, 0],
                      self.send.at[3, p % 8], self.recv.at[3, p % 8], at["dev_yr"]),
                rcopy(self.half.at[s, rows_at(at["yl"], 128)], self.r2.at[s, 1],
                      self.send.at[4, p % 8], self.recv.at[4, p % 8], at["dev_yl"]))

    def z_copy(self, p):
        s = p % 4
        return rcopy(self.zs.at[s], self.zr.at[s], self.send.at[5, p % 8], self.recv.at[5, p % 8],
                     self.at["dev_zh"])

    def back_first(self, p):
        s, at = p % 4, self.at
        mine = self.out.at[self.place(p), rows_at(at["core"] * 4 + at["y"], 128)]
        return (rcopy(self.full.at[s], mine, self.send.at[6, p % 8], self.recv.at[6, p % 8], at["dev_yr"]),
                rcopy(self.full.at[s], mine, self.send.at[7, p % 8], self.recv.at[7, p % 8], at["dev_yl"]),
                pltpu.make_async_copy(self.full.at[s], mine, self.local.at[p % 8]))

    def back_second(self, p):
        s, at = p % 4, self.at
        top = self.out.at[self.place(p), rows_at(at["core"] * 4 + at["yl"], 128, 64)]
        low = self.out.at[self.place(p), pl.ds(pl.multiple_of((at["core"] * 4 + at["yr"]) * 128 + 64, 64), 64)]
        return (rcopy(top, top, self.send.at[9, p % 8], self.recv.at[9, p % 8], at["dev_yr"]),
                rcopy(low, low, self.send.at[10, p % 8], self.recv.at[10, p % 8], at["dev_yl"]))

    def back_core(self, p):
        s, at = p % 4, self.at
        mine = self.out.at[self.place(p), rows_at(at["core"], 512)]
        return rcopy(mine, mine, self.send.at[8, p % 8], self.recv.at[8, p % 8], at["dev_core"])

    def send_piece(self, p):
        self.core_copy(p).start()

    def add_core(self, p):
        s = p % 4
        self.core_copy(p).wait()

        @pl.loop(0, 4)
        def _(j):
            rows = rows_at(j, 128)
            mine = self.own[p % 2, pl.ds(pl.multiple_of(self.at["core"] * 512 + j * 128, 128), 128)]
            self.half[s, rows] = (mine.astype(F32) + self.other[p % 2, rows].astype(F32)).astype(BF)

        for copy in self.first_copies(p):
            copy.start()

    def add_first(self, p):
        s, at = p % 4, self.at
        for copy in self.first_copies(p):
            copy.wait()
        top = rows_at(at["yr"], 128, 64)
        low = pl.ds(pl.multiple_of(at["yl"] * 128 + 64, 64), 64)
        self.half[s, top] = (self.half[s, top].astype(F32) + self.r1[s, 0].astype(F32)).astype(BF)
        self.half[s, low] = (self.half[s, low].astype(F32) + self.r1[s, 1].astype(F32)).astype(BF)
        for copy in self.second_copies(p):
            copy.start()

    def add_second(self, p):
        s = p % 4
        for copy in self.second_copies(p):
            copy.wait()
        mine = self.half[s, rows_at(self.at["y"], 128)].astype(F32)
        self.zs[s] = (mine + self.r2[s, 0].astype(F32) + self.r2[s, 1].astype(F32)).astype(BF)
        self.z_copy(p).start()

    def add_z(self, p):
        s = p % 4
        self.z_copy(p).wait()
        self.full[s] = (self.zs[s].astype(F32) + self.zr[s].astype(F32)).astype(BF)
        for copy in self.back_first(p):
            copy.start()

    def forward_y(self, p):
        for copy in self.back_first(p):
            copy.wait()
        for copy in self.back_second(p):
            copy.start()

    def forward_core(self, p):
        for copy in self.back_second(p):
            copy.wait()
        self.back_core(p).start()

    def finish(self, p):
        self.back_core(p).wait()

    def steps(self, t):
        for lag, step in ((1, self.add_core), (2, self.add_first), (3, self.add_second), (4, self.add_z),
                          (6, self.forward_y), (8, self.forward_core), (9, self.finish)):
            p = t - lag
            pl.when((p >= 0) & (p < NP))(lambda step=step, p=p: step(p))


def dot(a, b):
    return lax.dot_general(a, b, (((1,), (0,)), ((), ())), preferred_element_type=F32)


def dot_nt(a, b):
    return lax.dot_general(a, b, (((1,), (1,)), ((), ())), preferred_element_type=F32)


def at_rows(index, size=256):
    return pl.ds(pl.multiple_of(index * size, size), size)


class Gather:
    AHEAD = 2

    def scratch():
        return [
            pltpu.VMEM((16, 128, 256), BF),
            pltpu.VMEM((8, 1024, 256), BF),
            pltpu.SemaphoreType.DMA((9, 8)),
            pltpu.SemaphoreType.DMA((9, 8)),
        ]

    def __init__(self, at, scratch):
        self.at = at
        self.own, self.all, self.send, self.recv = scratch

    def copy(self, kind, c, src, dst, device):
        s = c % 8
        return rcopy(src, dst, self.send.at[kind, s], self.recv.at[kind, s], self.at[device])

    def part(self, c, zl, x, begin=0, count=128):
        first = pl.multiple_of((zl * 4 + x) * 128 + begin, 64)
        return self.all.at[c % 8, pl.ds(first, count)]

    def same(self, kind, c, block, device):
        return self.copy(kind, c, block, block, device)

    def first(self, c, wide):
        at = self.at
        src, dst = self.own.at[c], self.part(c, at["zl"], at["x"])
        copies = [self.copy(0, c, src, dst, "dev_xr"), self.copy(1, c, src, dst, "dev_xl")]
        return copies if wide else copies + [self.copy(2, c, src, dst, "dev_zl")]

    def ring(self, c):
        at = self.at
        return [self.same(3, c, self.part(c, at["zl"], at["xl"], 0, 64), "dev_xr"),
                self.same(4, c, self.part(c, at["zl"], at["xr"], 64, 64), "dev_xl")]

    def second(self, c, wide):
        at = self.at
        if wide:
            return [self.copy(5, c, self.own.at[c], self.part(c, at["zl"], at["x"]), "dev_zl"),
                    self.same(6, c, self.part(c, at["zl"], at["xl"]), "dev_zl"),
                    self.same(7, c, self.part(c, at["zl"], at["xr"]), "dev_zl")]
        other = self.part(c, 1 - at["zl"], at["x"])
        return [self.same(5, c, other, "dev_xr"), self.same(6, c, other, "dev_xl")]

    def third(self, c, wide):
        at = self.at
        if wide:
            return [self.same(8, c, self.part(c, at["zl"], at["xo"]), "dev_zl")]
        return [self.same(7, c, self.part(c, 1 - at["zl"], at["xl"], 0, 64), "dev_xr"),
                self.same(8, c, self.part(c, 1 - at["zl"], at["xr"], 64, 64), "dev_xl")]

    def begin(self, c):
        def start(wide):
            for copy in self.first(c, wide):
                copy.start()

        self.either(c, start)
        self.part(c, self.at["zl"], self.at["x"])[...] = self.own[c]

    def either(self, c, step):
        wide = (c % 2 == 1) & (c < WIDE)
        pl.when((c >= 0) & (c < 16) & wide)(lambda: step(True))
        pl.when((c >= 0) & (c < 16) & jnp.logical_not(wide))(lambda: step(False))

    def steps(self, c):
        def second(wide):
            for copy in self.first(c, wide):
                copy.wait()
            for copy in self.ring(c) + self.second(c, wide):
                copy.start()

        def third(wide):
            for copy in self.ring(c - 1) if wide else self.ring(c - 1) + self.second(c - 1, wide):
                copy.wait()
            for copy in self.third(c - 1, wide):
                copy.start()

        def last(wide):
            for copy in self.second(c - 2, wide) + self.third(c - 2, wide) if wide else self.third(c - 2, wide):
                copy.wait()

        self.either(c, second)
        pl.when(c + self.AHEAD < 16)(lambda: self.begin(c + self.AHEAD))
        self.either(c - 1, third)
        self.either(c - 2, last)


class RowSum:
    def scratch():
        return [
            pltpu.VMEM((4, 2, 4, 128, 256), BF),
            pltpu.VMEM((8, 2, 2, 64, 256), BF),
            pltpu.VMEM((4, 2, 2, 128, 256), BF),
            pltpu.VMEM((4, 128, 256), BF),
            pltpu.VMEM((4, 128, 256), BF),
            pltpu.VMEM((4, 128, 256), F32),
            pltpu.SemaphoreType.DMA((5, 8)),
            pltpu.SemaphoreType.DMA((5, 8)),
        ]

    def __init__(self, at, scratch, result):
        self.at, self.result = at, result
        self.part, self.r1, self.r2, self.zs, self.zr, self.mine, self.send, self.recv = scratch

    def copy(self, kind, c, src, dst, device):
        s = c % 8
        return rcopy(src, dst, self.send.at[kind, s], self.recv.at[kind, s], device)

    def first(self, c):
        s, at = c % 4, self.at
        return [self.copy(0, c, self.part.at[s, :, at["xo"], pl.ds(0, 64)], self.r1.at[c % 8, 0], at["dev_xr"]),
                self.copy(1, c, self.part.at[s, :, at["xo"], pl.ds(64, 64)], self.r1.at[c % 8, 1], at["dev_xl"])]

    def second(self, c):
        s, at = c % 4, self.at
        return [self.copy(2, c, self.part.at[s, :, at["xr"]], self.r2.at[s, 0], at["dev_xr"]),
                self.copy(3, c, self.part.at[s, :, at["xl"]], self.r2.at[s, 1], at["dev_xl"])]

    def third(self, c):
        s = c % 4
        return [self.copy(4, c, self.zs.at[s], self.zr.at[s], self.at["dev_zl"])]

    def store(self, c, value):
        for k in range(8):
            self.part[c % 4, k // 4, k % 4] = value[k * 128:(k + 1) * 128].astype(BF)

    def send_chunk(self, c):
        for copy in self.first(c):
            copy.start()

    def add_first(self, c):
        s, at = c % 4, self.at
        for copy in self.first(c):
            copy.wait()
        for z in range(2):
            top = self.part[s, z, at["xr"], 0:64].astype(F32) + self.r1[c % 8, 0, z].astype(F32)
            self.part[s, z, at["xr"], 0:64] = top.astype(BF)
            low = self.part[s, z, at["xl"], 64:128].astype(F32) + self.r1[c % 8, 1, z].astype(F32)
            self.part[s, z, at["xl"], 64:128] = low.astype(BF)
        for copy in self.second(c):
            copy.start()

    def add_second(self, c):
        s, at = c % 4, self.at
        for copy in self.second(c):
            copy.wait()

        def total(z):
            own = self.part[s, z, at["x"]].astype(F32)
            return own + self.r2[s, 0, z].astype(F32) + self.r2[s, 1, z].astype(F32)

        self.zs[s] = total(1 - at["zl"]).astype(BF)
        for copy in self.third(c):
            copy.start()
        self.mine[s] = total(at["zl"])

    def add_third(self, c):
        s = c % 4
        for copy in self.third(c):
            copy.wait()
        self.result(c, self.mine[s] + self.zr[s].astype(F32))

    def steps(self, t):
        for lag, step in ((2, self.add_first), (3, self.add_second), (4, self.add_third)):
            c = t - lag
            pl.when((c >= 0) & (c < 16))(lambda step=step, c=c: step(c))


class SmallSum:
    def scratch():
        return [
            pltpu.VMEM((8, 8, 1024), F32),
            pltpu.VMEM((4, 8, 1024), F32),
            pltpu.VMEM((4, 8, 1024), F32),
            pltpu.SemaphoreType.DMA((13,)),
            pltpu.SemaphoreType.DMA((13,)),
        ]

    def __init__(self, scratch):
        self.b1, self.b2, self.b3, self.send, self.recv = scratch
        dp, tensor = lax.axis_index("dp"), lax.axis_index("tensor")
        y, self.zh, core = dp // 4, (dp // 2) % 2, dp % 2
        self.zl, self.x = tensor // 4, tensor % 4
        self.i1 = y * 2 + core
        self.i2 = self.zh * 2 + self.zl
        self.d1, self.d2, self.d3 = [], [], []
        for k in range(1, 8):
            j = (self.i1 + k) % 8
            self.d1.append(((j // 2) * 4 + self.zh * 2 + j % 2, tensor))
        for k in range(1, 4):
            j = (self.i2 + k) % 4
            self.d2.append((y * 4 + (j // 2) * 2 + core, (j % 2) * 4 + self.x))
            self.d3.append((dp, self.zl * 4 + (self.x + k) % 4))

    def devices(self):
        return self.d1 + self.d2 + self.d3

    def copies(self, stage):
        buf, mine, devices, base = ((self.b1, self.i1, self.d1, 0), (self.b2, self.i2, self.d2, 7),
                                    (self.b3, self.x, self.d3, 10))[stage]
        return [rcopy(buf.at[mine], buf.at[mine], self.send.at[base + k], self.recv.at[base + k], device)
                for k, device in enumerate(devices)]

    def start(self, stage):
        for copy in self.copies(stage):
            copy.start()

    def wait(self, stage):
        for copy in self.copies(stage):
            copy.wait()

    def second(self):
        self.wait(0)
        total = self.b1[0]
        for k in range(1, 8):
            total = total + self.b1[k]
        self.b2[self.i2] = total
        self.start(1)

    def third(self):
        self.wait(1)
        wide = self.b2[0] + self.b2[1] + self.b2[2] + self.b2[3]
        narrow = self.b2[self.zl] + self.b2[2 + self.zl]
        row = lax.broadcasted_iota(jnp.int32, (8, 1024), 0)
        self.b3[self.x] = jnp.where(row < 6, wide, narrow)
        self.start(2)

    def result(self):
        self.wait(2)
        wide = self.b3[0] + self.b3[1] + self.b3[2] + self.b3[3]
        row = lax.broadcasted_iota(jnp.int32, (8, 1024), 0)
        return jnp.where(row < 6, wide, self.b3[self.x])


def gelu_parts(u):
    inner = 0.7978845608028654 * (u + 0.044715 * (u * u * u))
    return jnp.tanh(inner)


def swap_pairs(v):
    lane = lax.broadcasted_iota(jnp.int32, v.shape, 1)
    return jnp.where(lane % 32 < 16, pltpu.roll(v, 112, 1), pltpu.roll(v, 16, 1))


def turn(v, cosine, sine):
    return v * cosine + swap_pairs(v) * sine


WIDE = 14
UNITS = ((3, (0, 2)), (3, (2, 4)), (2, (0, 2)), (2, (2, 4)), (1, (0, 4)), (0, (0, 4)))
RS = 8
FEAT, MID = 1792, 1280


def block_kernel(
    tokens, cotangent, seg_row, gain_h, shift_h, b_qkv, b_out_h, b_up_h, b_down_h,
    w_qkv_h, w_out_h, w_up_h, w_down_h,
    pieces, output, input_grad, sums,
    w_in, w_mid, w_sem,
    gain, shift, b_sum,
    normed_t, pre, grad_mid, rows, turned, mid, heads_t, outs_g, outs_gt, grad_feat,
    cos_t, sin_t, seg_c, seg_r, lse, bias, p_f, q_m, g_m, ds_b, mean_row, rstd,
    *scratch,
):
    at = neighbours()
    grad_n = p_f
    dp_f = grad_mid.at[:, pl.ds(1024, 256)]
    act_t = grad_feat
    n1, n2, n3 = len(GradSum.scratch()), len(Gather.scratch()), len(RowSum.scratch())
    small = SmallSum(scratch[n1 + n2 + n3:])
    grads = GradSum(at, pieces, scratch[:n1])
    gather = Gather(at, scratch[n1:n1 + n2])

    def keep_rows(c, value):
        branch = (c < 6) | (c >= 14)

        @pl.when(branch)
        def _():
            cols = at_rows(jnp.where(c < 6, c, c - 8))
            own = tokens[:, cols].astype(F32) + value + b_sum[0:1, cols]
            output[:, cols] = own.astype(BF)

        @pl.when(jnp.logical_not(branch))
        def _():
            grad_n[at_rows(c - 6, 128), :] = value

    row_sum = RowSum(at, scratch[n1 + n2:n1 + n2 + n3], keep_rows)

    moves = [(w_up_h, w_in.at[:, pl.ds(0, 1024)])]
    moves += [(w_qkv_h.at[k], w_in.at[:, pl.ds(1024 + 256 * k, 256)]) for k in range(3)]
    moves += [(w_down_h, w_mid.at[pl.ds(0, 1024)]), (w_out_h, w_mid.at[pl.ds(1024, 256)])]
    weights = [pltpu.make_async_copy(src, dst, w_sem.at[i]) for i, (src, dst) in enumerate(moves)]

    barrier = pltpu.get_barrier_semaphore()
    greeted = small.devices()
    for device in greeted:
        pl.semaphore_signal(barrier, inc=1, device_id=device, device_id_type=MESH)
    for copy in weights:
        copy.start()

    gain[...] = gain_h[...].astype(F32).reshape(1, 2048)
    shift[...] = shift_h[...].astype(F32).reshape(1, 2048)
    b_sum[...] = (b_out_h[...].astype(F32) + b_down_h[...].astype(F32)).reshape(1, 2048)
    x = tokens[...].astype(F32)
    mean = jnp.mean(x, axis=1, keepdims=True)
    centered = x - mean
    scale = lax.rsqrt(jnp.mean(centered * centered, axis=1, keepdims=True) + EPSILON)
    rstd[...] = jnp.broadcast_to(scale, (128, 128))
    mean_row[...] = jnp.broadcast_to(mean, (128, 128))

    def unit(cols):
        return (tokens[:, cols].astype(F32) - mean_row[:, 0:1]) * rstd[:, 0:1]

    for c in range(8):
        cols = slice(c * 256, c * 256 + 256)
        gather.own[c] = (unit(cols) * gain[0:1, cols] + shift[0:1, cols]).astype(BF)
        gather.own[8 + c] = cotangent[:, cols]

    pl.semaphore_wait(barrier, len(greeted))
    for c in range(Gather.AHEAD):
        gather.begin(c)

    seg_f = seg_row[...].astype(F32)
    seg_r[...] = jnp.broadcast_to(seg_f, (8, 1024))
    seg_c[...] = jnp.broadcast_to(seg_f, (128, 1024)).T
    @pl.loop(0, 4)
    def _(b):
        r = at_rows(b)
        i = lax.broadcasted_iota(jnp.int32, (256, 1024), 0) + b * 256
        j = lax.broadcasted_iota(jnp.int32, (256, 1024), 1)
        same = jnp.where((seg_c[r, 0:1] == seg_r[0:1, :]) & (j < i), 1.0, 0.0)
        position = jnp.sum(same, axis=1, keepdims=True)
        lane = lax.broadcasted_iota(jnp.int32, (256, 128), 1) % 64
        power = jnp.exp((lane % 16).astype(F32) * (-2.0 / ROT * 9.210340371976184))
        angle = position * power
        sine = jnp.sin(angle)
        cos_t[r, :] = jnp.where(lane < ROT, jnp.cos(angle), 1.0)
        sin_t[r, :] = jnp.where(lane < ROT // 2, -sine, jnp.where(lane < ROT, sine, 0.0))
        pre[r, 0:1024] = jnp.broadcast_to(b_up_h[...].astype(F32).reshape(1, 1024), (256, 1024))
        for k in range(3):
            cols = slice(1024 + k * 256, 1280 + k * 256)
            pre[r, cols] = jnp.broadcast_to(b_qkv[k:k + 1, :].astype(F32), (256, 256))

    @pl.loop(0, 10)
    def _(i):
        gather.steps(i)

        @pl.when(i == 2)
        def _():
            for copy in weights[:4]:
                copy.wait()

        @pl.when(i >= 2)
        def _():
            c = i - 2

            @pl.loop(0, 2)
            def _(b):
                r = at_rows(b, 512)
                a = gather.all[c % 8, r, :]
                pre[r, :] += dot(a, w_in[at_rows(c), :])
            normed_t[at_rows(c), :] = gather.all[c % 8].T

    @pl.loop(0, 4)
    def _(b):
        r = at_rows(b)
        for k in range(4):
            cols = slice(k * 256, k * 256 + 256)
            u = pre[r, cols]
            a = (u * (0.5 * (1.0 + gelu_parts(u)))).astype(BF)
            mid[r, cols] = a
            act_t[cols, r] = a.T

    for copy in weights[4:]:
        copy.wait()
    gather.steps(10)

    def make_rows(b):
        r = at_rows(b)
        for k in range(3):
            for half in range(2):
                v = pre[r, 1024 + k * 256 + half * 128:1152 + k * 256 + half * 128]
                if k < 2:
                    v = turn(v, cos_t[r, :], sin_t[r, :])
                if k == 0:
                    v = v * HEAD_DIM ** -0.5
                v = v.astype(BF)
                cols = slice(half * 128, half * 128 + 128)
                rows[k, r, cols] = v
                turned[k, cols, r] = v.T

    def attend_bias(qb):
        cols = slice(qb * 256, qb * 256 + 256)
        for kb in range(qb + 1):
            r = slice(kb * 256, kb * 256 + 256)
            keep = seg_c[r, 0:1] == seg_r[0:1, cols]
            if kb == qb:
                i = lax.broadcasted_iota(jnp.int32, (256, 256), 0)
                j = lax.broadcasted_iota(jnp.int32, (256, 256), 1)
                keep = keep & (i <= j)
            bias[r, :] = jnp.where(keep, 0.0, -1e30).astype(BF)

    def one_head(ref, source, h, cols):
        ref[...] = jnp.zeros_like(ref)
        ref[head_rows(h), :] = source[head_rows(h), cols]

    def head_rows(h):
        return pl.ds(pl.multiple_of(h * 64, 64), 64)

    def attend(qb, heads):
        cols = slice(qb * 256, qb * 256 + 256)
        n = (qb + 1) * 256
        if heads[0] == 0:
            attend_bias(qb)

        @pl.loop(*heads)
        def _(h):
            hr = head_rows(h)
            one_head(q_m, turned.at[0], h, cols)
            s = dot(rows[1, 0:n, :], q_m[...]) + bias[0:n, :].astype(F32)
            p_f[0:n, :] = s
            most = jnp.max(s, axis=0, keepdims=True)
            e = jnp.exp(p_f[0:n, :] - most)
            p_f[0:n, :] = e
            total = jnp.sum(e, axis=0, keepdims=True)
            ds_b[0:n, :] = (p_f[0:n, :] * (1.0 / total)).astype(BF)
            heads_t[hr, cols] = dot(
                turned[2, hr, 0:n], ds_b[0:n, :]).astype(BF)
            lse[pl.ds(h, 1), cols] = most + jnp.log(total)

    def attend_back(qb, heads):
        cols = slice(qb * 256, qb * 256 + 256)
        n = (qb + 1) * 256
        if heads[0] == 0:
            attend_bias(qb)

        @pl.loop(*heads)
        def _(h):
            hr = head_rows(h)
            one_head(q_m, turned.at[0], h, cols)
            one_head(g_m, outs_gt, h, cols)
            p = jnp.exp(dot(rows[1, 0:n, :], q_m[...]) + bias[0:n, :].astype(F32) - lse[pl.ds(h, 1), cols])
            p_f[0:n, :] = p
            d = dot(rows[2, 0:n, :], g_m[...])
            dp_f[0:n, :] = d
            delta = jnp.sum(p_f[0:n, :] * d, axis=0, keepdims=True)
            lane = lax.broadcasted_iota(jnp.int32, (256, 256), 1) // 64
            q_h = jnp.where(lane == h, rows[0, cols, :].astype(F32), 0.0).astype(BF)
            g_h = jnp.where(lane == h, outs_g[cols, :].astype(F32), 0.0).astype(BF)
            pre[0:n, 1536:1792] += dot(p_f[0:n, :].astype(BF), g_h)
            ds_b[0:n, :] = (p_f[0:n, :] * (dp_f[0:n, :] - delta)).astype(BF)
            pre[0:n, 1280:1536] += dot(ds_b[0:n, :], q_h)
            pre[pl.ds(pl.multiple_of(qb * 256 + h * 64, 64), 64), 1024:1280] = dot(
                turned[1, hr, 0:n], ds_b[0:n, :])

    @pl.loop(0, 8)
    def _(t):
        grads.steps(t)
        chunk = gather.all[t]
        grads.own[t % 2] = dot(act_t[:, 0:1024], chunk).astype(BF)
        grads.send_piece(t)
        gather.steps(11 + t)

        @pl.when(t == 0)
        def _():
            grad_mid[...] = jnp.zeros_like(grad_mid)

        @pl.loop(0, 2)
        def _(b):
            r = at_rows(b, 512)
            grad_mid[r, :] += dot_nt(gather.all[t, r, :], w_mid[:, at_rows(t)])

        @pl.when(t < 2)
        def _():
            make_rows(2 * t)
            make_rows(2 * t + 1)

        for i, (qb, heads) in enumerate(UNITS):
            pl.when(t == 2 + i)(lambda qb=qb, heads=heads: attend(qb, heads))

    def branch_chunk(t, c):
        row_sum.store(t - RS, dot(mid[...], w_mid[:, at_rows(c)]))
        row_sum.send_chunk(t - RS)

    def normed_chunk(t, c):
        row_sum.store(t - RS, dot_nt(grad_feat[...], w_in[at_rows(c), :]))
        row_sum.send_chunk(t - RS)

    def gelu_back(k):
        @pl.loop(0, 4)
        def _(b):
            r, cols = at_rows(b), at_rows(k)
            u = pre[r, cols]
            th = gelu_parts(u)
            slope = 0.5 * (1.0 + th) + 0.5 * u * (1.0 - th * th) * (
                0.7978845608028654 * (1.0 + 3 * 0.044715 * (u * u)))
            grad_feat[r, cols] = (slope * grad_mid[r, cols]).astype(BF)

    def feature_piece(t):
        q = t - 10
        grads.own[t % 2] = dot(
            normed_t[at_rows(q % 2, 1024), :], grad_feat[:, at_rows(q // 2)]).astype(BF)
        grads.send_piece(t)

    @pl.loop(0, 4)
    def _(b):
        r = at_rows(b)
        mid[r, 1024:1280] = heads_t[:, r].T
        g = grad_mid[r, 1024:1280].astype(BF)
        outs_g[r, :] = g
        outs_gt[:, r] = g.T
        pre[r, 1024:1792] = jnp.zeros((256, 768), F32)

    @pl.loop(8, 10)
    def _(t):
        grads.steps(t)
        row_sum.steps(t - RS)
        for j in range(4):
            r = slice(j * 256, j * 256 + 256)
            grads.own[t % 2, r, :] = dot(heads_t[...], gather.all[4 * (t - 8) + j]).astype(BF)
        grads.send_piece(t)
        branch_chunk(t, t - RS)
        pl.when(t == 9)(lambda: gelu_back(0))
        for i, (qb, heads) in enumerate(UNITS[:2]):
            pl.when(t == 8 + i)(lambda qb=qb, heads=heads: attend_back(qb, heads))

    @pl.loop(10, 14)
    def _(t):
        grads.steps(t)
        row_sum.steps(t - RS)
        feature_piece(t)
        branch_chunk(t, t - RS)
        pl.when(t >= 11)(lambda: gelu_back(t - 10))
        for i, (qb, heads) in enumerate(UNITS[2:]):
            pl.when(t == 10 + i)(lambda qb=qb, heads=heads: attend_back(qb, heads))

    for b in range(4):
        r = slice(b * 256, b * 256 + 256)
        grad_q = pre[r, 1024:1280].T * HEAD_DIM ** -0.5
        for half in range(2):
            a = half * 128
            cosine, sine = cos_t[r, :], -sin_t[r, :]
            grad_feat[r, 1024 + a:1152 + a] = turn(grad_q[:, a:a + 128], cosine, sine).astype(BF)
            grad_feat[r, 1280 + a:1408 + a] = turn(pre[r, 1280 + a:1408 + a], cosine, sine).astype(BF)
        grad_feat[r, 1536:1792] = pre[r, 1536:1792].astype(BF)

    @pl.loop(14, 24)
    def _(t):
        grads.steps(t)
        row_sum.steps(t - RS)
        feature_piece(t)
        pl.when(t < 22)(lambda: normed_chunk(t, t - 14))
        pl.when(t >= 22)(lambda: branch_chunk(t, t - 16))

    def late_steps(t):
        grads.steps(t)
        row_sum.steps(t - RS)

    late_steps(24)
    late_steps(25)

    def column_sum(value):
        return jnp.sum(value.astype(F32), axis=0, keepdims=True)

    mine = small.i1
    small.b1[mine] = jnp.zeros((8, 1024), F32)
    mean_plain = jnp.zeros((128, 1), F32)
    mean_unit = jnp.zeros((128, 1), F32)
    for c in range(8):
        cols = slice(c * 256, c * 256 + 256)
        row, lanes = c // 4, slice((c % 4) * 256, (c % 4) * 256 + 256)
        g = grad_n[c * 128:c * 128 + 128, :]
        n = unit(cols)
        scaled = g * gain[0:1, cols]
        mean_plain = mean_plain + jnp.sum(scaled, axis=1, keepdims=True)
        mean_unit = mean_unit + jnp.sum(scaled * n, axis=1, keepdims=True)
        small.b1[mine, row:row + 1, lanes] = column_sum(g * n)
        small.b1[mine, 2 + row:3 + row, lanes] = column_sum(g)
        small.b1[mine, 4 + row:5 + row, lanes] = column_sum(cotangent[:, cols])
    for k in range(7):
        row, lanes = 6 + k // 4, slice((k % 4) * 256, (k % 4) * 256 + 256)
        small.b1[mine, row:row + 1, lanes] = column_sum(grad_feat[:, k * 256:k * 256 + 256])
    small.start(0)
    late_steps(26)
    mean_plain = mean_plain / 2048.0
    mean_unit = mean_unit / 2048.0
    for c in range(8):
        cols = slice(c * 256, c * 256 + 256)
        inner = grad_n[c * 128:c * 128 + 128, :] * gain[0:1, cols] - mean_plain - unit(cols) * mean_unit
        input_grad[:, cols] = (cotangent[:, cols].astype(F32) + rstd[:, 0:1] * inner).astype(BF)

    late_steps(27)
    small.second()
    late_steps(28)
    late_steps(29)
    small.third()
    late_steps(30)
    late_steps(31)
    sums[...] = small.result()
    late_steps(32)


def run_block(tokens, segment, ln_gain, ln_bias, w_qkv, b_qkv, w_out, b_out, w_up, b_up, w_down,
              b_down, cotangent):
    vmem = pl.BlockSpec(memory_space=pltpu.VMEM)
    hbm = pl.BlockSpec(memory_space=pl.ANY)
    V = pltpu.VMEM
    scratch = [
        V((2048, FEAT), BF), V((MID, 2048), BF), pltpu.SemaphoreType.DMA((6,)),
        V((1, 2048), F32), V((1, 2048), F32), V((1, 2048), F32),
        V((2048, 1024), BF),
        V((1024, FEAT), F32), V((1024, MID), F32),
        V((3, 1024, 256), BF), V((3, 256, 1024), BF),
        V((1024, MID), BF), V((256, 1024), BF),
        V((1024, 256), BF), V((256, 1024), BF),
        V((1024, FEAT), BF),
        V((1024, 128), F32), V((1024, 128), F32),
        V((1024, 128), F32), V((8, 1024), F32),
        V((8, 1024), F32),
        V((1024, 256), BF), V((1024, 256), F32),
        V((256, 256), BF), V((256, 256), BF), V((1024, 256), BF),
        V((128, 128), F32), V((128, 128), F32),
    ] + GradSum.scratch() + Gather.scratch() + RowSum.scratch() + SmallSum.scratch()
    return pl.pallas_call(
        block_kernel,
        out_shape=(
            jax.ShapeDtypeStruct((NP, 1024, 256), BF),
            jax.ShapeDtypeStruct((128, 2048), BF),
            jax.ShapeDtypeStruct((128, 2048), BF),
            jax.ShapeDtypeStruct((8, 1024), F32),
        ),
        in_specs=[vmem] * 9 + [hbm] * 4,
        out_specs=(hbm, vmem, vmem, vmem),
        scratch_shapes=scratch,
        compiler_params=pltpu.CompilerParams(
            collective_id=0, has_side_effects=True, vmem_limit_bytes=VMEM_LIMIT),
        cost_estimate=pl.CostEstimate(flops=50 * 10**9, bytes_accessed=30 << 20, transcendentals=10**7),
    )(
        tokens, cotangent, segment.reshape(1, 1024), ln_gain, ln_bias, b_qkv, b_out, b_up, b_down,
        w_qkv.transpose(1, 0, 2), w_out, w_up, w_down,
    )


def widen_kernel(qkv_p, out_p, down_p, up_p, output, input_grad, sums,
                 down, out, up, qkv, output_o, input_grad_o, gain_o, shift_o, b_out_o, b_down_o, b_up_o, b_qkv_o):
    for c in range(8):
        cols = slice(c * 256, c * 256 + 256)
        down[:, cols] = down_p[c].astype(F32)
        out[:, cols] = out_p[c].astype(F32)
    for c in range(4):
        up[:, c * 256:c * 256 + 256] = up_p[c, 0].astype(F32)
    qkv[...] = qkv_p[...].astype(F32)
    output_o[...] = output[...]
    input_grad_o[...] = input_grad[...]

    @pl.when(pl.program_id(0) == 0)
    def _():
        gain_o[...] = sums[0:2, :].reshape(2048)
        shift_o[...] = sums[2:4, :].reshape(2048)
        b_out_o[...] = sums[4:6, :].reshape(2048)
        b_down_o[...] = sums[4:6, :].reshape(2048)
        b_up_o[...] = sums[6:7, :].reshape(1024)
        for c in range(3):
            b_qkv_o[c:c + 1, :] = sums[7:8, c * 256:c * 256 + 256]


def widen(pieces, output, input_grad, sums):
    def rows(count, width):
        return pl.BlockSpec((count, width), lambda i: (i, 0))

    def whole(*shape):
        return pl.BlockSpec(shape, lambda i: (0,) * len(shape))

    def shape(*dims, kind=F32):
        return jax.ShapeDtypeStruct(dims, kind)

    down, out, up, qkv, *rest = pl.pallas_call(
        widen_kernel,
        grid=(8,),
        out_shape=(
            shape(1024, 2048), shape(256, 2048), shape(2048, 1024), shape(6144, 256),
            shape(128, 2048, kind=BF), shape(128, 2048, kind=BF),
            shape(2048), shape(2048), shape(2048), shape(2048), shape(1024), shape(3, 256),
        ),
        in_specs=[
            rows(768, 256),
            pl.BlockSpec((8, 32, 256), lambda i: (3, i, 0)),
            pl.BlockSpec((8, 128, 256), lambda i: (1, i, 0)),
            pl.BlockSpec((4, 1, 256, 256), lambda i: (2, i // 4, i % 4, 0)),
            rows(16, 2048), rows(16, 2048), whole(8, 1024),
        ],
        out_specs=(
            rows(128, 2048), rows(32, 2048), rows(256, 1024), rows(768, 256),
            rows(16, 2048), rows(16, 2048),
            whole(2048), whole(2048), whole(2048), whole(2048), whole(1024), whole(3, 256),
        ),
        compiler_params=pltpu.CompilerParams(vmem_limit_bytes=VMEM_LIMIT),
    )(
        pieces.reshape(NP * 1024, 256), pieces.reshape(NP * 4, 256, 256), pieces,
        pieces.reshape(NP // 2, 2, 1024, 256), output, input_grad, sums,
    )
    return down, out, up, qkv.reshape(3, 2048, 256).transpose(1, 0, 2), rest


def on_device(*args):
    pieces, output, input_grad, sums = run_block(*args)
    down, out, up, qkv, rest = widen(pieces, output, input_grad, sums)
    output, input_grad, gain, shift, b_out, b_down, b_up, b_qkv = rest
    return output, input_grad, gain, shift, qkv, b_qkv, out, b_out, up, b_up, down, b_down


def solution(mesh):
    placed = (
        P(("dp", "tensor"), None),
        P("dp"),
        P(),
        P(),
        P(None, None, "tensor"),
        P(None, "tensor"),
        P("tensor", None),
        P(),
        P(None, "tensor"),
        P("tensor"),
        P("tensor", None),
        P(),
        P(("dp", "tensor"), None),
    )
    return jax.shard_map(
        on_device,
        mesh=mesh,
        in_specs=placed,
        out_specs=(
            P(("dp", "tensor"), None),
            P(("dp", "tensor"), None),
            P(),
            P(),
            P(None, None, "tensor"),
            P(None, "tensor"),
            P("tensor", None),
            P(),
            P(None, "tensor"),
            P("tensor"),
            P("tensor", None),
            P(),
        ),
        check_vma=False,
    )
```

```python
import jax
import jax.numpy as jnp
from jax import lax
from jax.experimental import pallas as pl
from jax.experimental.pallas import tpu as pltpu
from jax.sharding import PartitionSpec as P

HEAD_DIM = 64
ROT = 32
EPSILON = 1e-05
MESH = pl.DeviceIdType.MESH
BF = jnp.bfloat16
F32 = jnp.float32
NP = 24
VMEM_LIMIT = 64 << 20


def neighbours():
    dp = lax.axis_index("dp")
    tensor = lax.axis_index("tensor")
    y, zh, core = dp // 4, (dp // 2) % 2, dp % 2
    zl, x = tensor // 4, tensor % 4
    yl, yr, yo = (y + 3) % 4, (y + 1) % 4, (y + 2) % 4
    xl, xr, xo = (x + 3) % 4, (x + 1) % 4, (x + 2) % 4
    where = dict(y=y, core=core, zl=zl, x=x, yl=yl, yr=yr, yo=yo, xl=xl, xr=xr, xo=xo)
    where["dev_yl"] = (yl * 4 + zh * 2 + core, tensor)
    where["dev_yr"] = (yr * 4 + zh * 2 + core, tensor)
    where["dev_zh"] = (y * 4 + (1 - zh) * 2 + core, tensor)
    where["dev_core"] = (y * 4 + zh * 2 + 1 - core, tensor)
    where["dev_xl"] = (dp, zl * 4 + xl)
    where["dev_xr"] = (dp, zl * 4 + xr)
    where["dev_zl"] = (dp, (1 - zl) * 4 + x)
    return where


def greet(devices):
    barrier = pltpu.get_barrier_semaphore()
    for device in devices:
        pl.semaphore_signal(barrier, inc=1, device_id=device, device_id_type=MESH)
    pl.semaphore_wait(barrier, len(devices))


def rcopy(src, dst, send, recv, device):
    return pltpu.make_async_remote_copy(
        src_ref=src, dst_ref=dst, send_sem=send, recv_sem=recv, device_id=device, device_id_type=MESH
    )


def rows_at(index, size, count=None):
    return pl.ds(pl.multiple_of(index * size, size), size if count is None else count)


class GradSum:
    def scratch():
        return [
            pltpu.VMEM((2, 1024, 256), BF),
            pltpu.VMEM((2, 512, 256), BF),
            pltpu.VMEM((4, 512, 256), BF),
            pltpu.VMEM((4, 2, 64, 256), BF),
            pltpu.VMEM((6, 2, 128, 256), BF),
            pltpu.VMEM((2, 128, 256), BF),
            pltpu.VMEM((4, 128, 256), BF),
            pltpu.VMEM((3, 128, 256), BF),
            pltpu.SemaphoreType.DMA((11, 8)),
            pltpu.SemaphoreType.DMA((11, 8)),
            pltpu.SemaphoreType.DMA((8,)),
        ]

    def __init__(self, at, out, scratch):
        self.at, self.out = at, out
        (self.own, self.other, self.half, self.r1, self.r2, self.zs, self.zr, self.full,
         self.send, self.recv, self.local) = scratch

    def place(self, p):
        return jnp.where(p < 8, p + 8, jnp.where(p < 10, p - 2, jnp.where(p < 18, p + 6, p - 18)))

    def core_copy(self, p):
        s, at = p % 4, self.at
        return rcopy(self.own.at[p % 2, rows_at(1 - at["core"], 512)], self.other.at[p % 2],
                     self.send.at[0, p % 8], self.recv.at[0, p % 8], at["dev_core"])

    def first_copies(self, p):
        s, at = p % 4, self.at
        top = self.half.at[s, rows_at(at["yo"], 128, 64)]
        low = self.half.at[s, pl.ds(pl.multiple_of(at["yo"] * 128 + 64, 64), 64)]
        return (rcopy(top, self.r1.at[s, 0], self.send.at[1, p % 8], self.recv.at[1, p % 8], at["dev_yr"]),
                rcopy(low, self.r1.at[s, 1], self.send.at[2, p % 8], self.recv.at[2, p % 8], at["dev_yl"]))

    def second_copies(self, p):
        s, at = p % 4, self.at
        return (rcopy(self.half.at[s, rows_at(at["yr"], 128)], self.r2.at[p % 6, 0],
                      self.send.at[3, p % 8], self.recv.at[3, p % 8], at["dev_yr"]),
                rcopy(self.half.at[s, rows_at(at["yl"], 128)], self.r2.at[p % 6, 1],
                      self.send.at[4, p % 8], self.recv.at[4, p % 8], at["dev_yl"]))

    def z_copy(self, p):
        s = p % 4
        return rcopy(self.zs.at[p % 2], self.zr.at[s], self.send.at[5, p % 8], self.recv.at[5, p % 8],
                     self.at["dev_zh"])

    def back_first(self, p):
        s, at = p % 4, self.at
        mine = self.out.at[self.place(p), rows_at(at["core"] * 4 + at["y"], 128)]
        return (rcopy(self.full.at[p % 3], mine, self.send.at[6, p % 8], self.recv.at[6, p % 8], at["dev_yr"]),
                rcopy(self.full.at[p % 3], mine, self.send.at[7, p % 8], self.recv.at[7, p % 8], at["dev_yl"]),
                pltpu.make_async_copy(self.full.at[p % 3], mine, self.local.at[p % 8]))

    def back_second(self, p):
        s, at = p % 4, self.at
        top = self.out.at[self.place(p), rows_at(at["core"] * 4 + at["yl"], 128, 64)]
        low = self.out.at[self.place(p), pl.ds(pl.multiple_of((at["core"] * 4 + at["yr"]) * 128 + 64, 64), 64)]
        return (rcopy(top, top, self.send.at[9, p % 8], self.recv.at[9, p % 8], at["dev_yr"]),
                rcopy(low, low, self.send.at[10, p % 8], self.recv.at[10, p % 8], at["dev_yl"]))

    def back_core(self, p):
        s, at = p % 4, self.at
        mine = self.out.at[self.place(p), rows_at(at["core"], 512)]
        return rcopy(mine, mine, self.send.at[8, p % 8], self.recv.at[8, p % 8], at["dev_core"])

    def send_piece(self, p):
        self.core_copy(p).start()

    def add_core(self, p):
        s = p % 4
        self.core_copy(p).wait()

        @pl.loop(0, 4)
        def _(j):
            rows = rows_at(j, 128)
            mine = self.own[p % 2, pl.ds(pl.multiple_of(self.at["core"] * 512 + j * 128, 128), 128)]
            self.half[s, rows] = (mine.astype(F32) + self.other[p % 2, rows].astype(F32)).astype(BF)

        for copy in self.first_copies(p):
            copy.start()

    def add_first(self, p):
        s, at = p % 4, self.at
        for copy in self.first_copies(p):
            copy.wait()
        top = rows_at(at["yr"], 128, 64)
        low = pl.ds(pl.multiple_of(at["yl"] * 128 + 64, 64), 64)
        self.half[s, top] = (self.half[s, top].astype(F32) + self.r1[s, 0].astype(F32)).astype(BF)
        self.half[s, low] = (self.half[s, low].astype(F32) + self.r1[s, 1].astype(F32)).astype(BF)
        for copy in self.second_copies(p):
            copy.start()

    def add_second(self, p):
        s = p % 4
        for copy in self.second_copies(p):
            copy.wait()
        mine = self.half[s, rows_at(self.at["y"], 128)].astype(F32)
        self.zs[p % 2] = (mine + self.r2[p % 6, 0].astype(F32) + self.r2[p % 6, 1].astype(F32)).astype(BF)
        self.z_copy(p).start()

    def add_z(self, p):
        s = p % 4
        self.z_copy(p).wait()
        self.full[p % 3] = (self.zs[p % 2].astype(F32) + self.zr[s].astype(F32)).astype(BF)
        for copy in self.back_first(p):
            copy.start()

    def forward_y(self, p):
        for copy in self.back_first(p):
            copy.wait()
        for copy in self.back_second(p):
            copy.start()

    def forward_core(self, p):
        for copy in self.back_second(p):
            copy.wait()
        self.back_core(p).start()

    def finish(self, p):
        self.back_core(p).wait()

    def steps(self, t):
        for lag, step in ((1, self.add_core), (2, self.add_first), (4, self.add_second), (5, self.add_z),
                          (7, self.forward_y), (9, self.forward_core), (10, self.finish)):
            p = t - lag
            pl.when((p >= 0) & (p < NP))(lambda step=step, p=p: step(p))


def dot(a, b):
    return lax.dot_general(a, b, (((1,), (0,)), ((), ())), preferred_element_type=F32)


def dot_nt(a, b):
    return lax.dot_general(a, b, (((1,), (1,)), ((), ())), preferred_element_type=F32)


def at_rows(index, size=256):
    return pl.ds(pl.multiple_of(index * size, size), size)


class Gather:
    AHEAD = 2

    def scratch():
        return [
            pltpu.VMEM((8, 1024, 256), BF),
            pltpu.SemaphoreType.DMA((9, 8)),
            pltpu.SemaphoreType.DMA((9, 8)),
        ]

    def __init__(self, at, own, scratch):
        self.at, self.own = at, own
        self.all, self.send, self.recv = scratch

    def copy(self, kind, c, src, dst, device):
        s = c % 8
        return rcopy(src, dst, self.send.at[kind, s], self.recv.at[kind, s], self.at[device])

    def part(self, c, zl, x, begin=0, count=128):
        first = pl.multiple_of((zl * 4 + x) * 128 + begin, 64)
        return self.all.at[c % 8, pl.ds(first, count)]

    def same(self, kind, c, block, device):
        return self.copy(kind, c, block, block, device)

    def first(self, c, wide):
        at = self.at
        mine = self.part(c, at["zl"], at["x"])
        copies = [self.same(0, c, mine, "dev_xr"), self.same(1, c, mine, "dev_xl")]
        return copies if wide else copies + [self.same(2, c, mine, "dev_zl")]

    def ring(self, c):
        at = self.at
        return [self.same(3, c, self.part(c, at["zl"], at["xl"], 0, 64), "dev_xr"),
                self.same(4, c, self.part(c, at["zl"], at["xr"], 64, 64), "dev_xl")]

    def second(self, c, wide):
        at = self.at
        if wide:
            return [self.same(5, c, self.part(c, at["zl"], at["x"]), "dev_zl"),
                    self.same(6, c, self.part(c, at["zl"], at["xl"]), "dev_zl"),
                    self.same(7, c, self.part(c, at["zl"], at["xr"]), "dev_zl")]
        other = self.part(c, 1 - at["zl"], at["x"])
        return [self.same(5, c, other, "dev_xr"), self.same(6, c, other, "dev_xl")]

    def third(self, c, wide):
        at = self.at
        if wide:
            return [self.same(8, c, self.part(c, at["zl"], at["xo"]), "dev_zl")]
        return [self.same(7, c, self.part(c, 1 - at["zl"], at["xl"], 0, 64), "dev_xr"),
                self.same(8, c, self.part(c, 1 - at["zl"], at["xr"], 64, 64), "dev_xl")]

    def begin(self, c):
        def start(wide):
            for copy in self.first(c, wide):
                copy.start()

        self.part(c, self.at["zl"], self.at["x"])[...] = self.own(c)
        self.either(c, start)

    def either(self, c, step):
        wide = (c % 2 == 1) & (c < WIDE)
        pl.when((c >= 0) & (c < 16) & wide)(lambda: step(True))
        pl.when((c >= 0) & (c < 16) & jnp.logical_not(wide))(lambda: step(False))

    def steps(self, c):
        def second(wide):
            for copy in self.first(c, wide):
                copy.wait()
            for copy in self.ring(c) + self.second(c, wide):
                copy.start()

        def third(wide):
            for copy in self.ring(c - 1) if wide else self.ring(c - 1) + self.second(c - 1, wide):
                copy.wait()
            for copy in self.third(c - 1, wide):
                copy.start()

        def last(wide):
            for copy in self.second(c - 2, wide) + self.third(c - 2, wide) if wide else self.third(c - 2, wide):
                copy.wait()

        self.either(c, second)
        pl.when(c + self.AHEAD < 16)(lambda: self.begin(c + self.AHEAD))
        self.either(c - 1, third)
        self.either(c - 2, last)


class RowSum:
    def scratch():
        return [
            pltpu.VMEM((4, 2, 4, 128, 256), BF),
            pltpu.VMEM((6, 2, 2, 64, 256), BF),
            pltpu.VMEM((6, 2, 2, 128, 256), BF),
            pltpu.VMEM((2, 128, 256), BF),
            pltpu.VMEM((4, 128, 256), BF),
            pltpu.VMEM((2, 128, 256), F32),
            pltpu.SemaphoreType.DMA((5, 8)),
            pltpu.SemaphoreType.DMA((5, 8)),
        ]

    def __init__(self, at, scratch, result):
        self.at, self.result = at, result
        self.part, self.r1, self.r2, self.zs, self.zr, self.mine, self.send, self.recv = scratch

    def copy(self, kind, c, src, dst, device):
        s = c % 8
        return rcopy(src, dst, self.send.at[kind, s], self.recv.at[kind, s], device)

    def first(self, c):
        s, at = c % 4, self.at
        return [self.copy(0, c, self.part.at[s, :, at["xo"], pl.ds(0, 64)], self.r1.at[c % 6, 0], at["dev_xr"]),
                self.copy(1, c, self.part.at[s, :, at["xo"], pl.ds(64, 64)], self.r1.at[c % 6, 1], at["dev_xl"])]

    def second(self, c):
        s, at = c % 4, self.at
        return [self.copy(2, c, self.part.at[s, :, at["xr"]], self.r2.at[c % 6, 0], at["dev_xr"]),
                self.copy(3, c, self.part.at[s, :, at["xl"]], self.r2.at[c % 6, 1], at["dev_xl"])]

    def third(self, c):
        s = c % 4
        return [self.copy(4, c, self.zs.at[c % 2], self.zr.at[s], self.at["dev_zl"])]

    def store(self, c, value):
        for k in range(8):
            self.part[c % 4, k // 4, k % 4] = value[k * 128:(k + 1) * 128].astype(BF)

    def send_chunk(self, c):
        for copy in self.first(c):
            copy.start()

    def add_first(self, c):
        s, at = c % 4, self.at
        for copy in self.first(c):
            copy.wait()
        for z in range(2):
            top = self.part[s, z, at["xr"], 0:64].astype(F32) + self.r1[c % 6, 0, z].astype(F32)
            self.part[s, z, at["xr"], 0:64] = top.astype(BF)
            low = self.part[s, z, at["xl"], 64:128].astype(F32) + self.r1[c % 6, 1, z].astype(F32)
            self.part[s, z, at["xl"], 64:128] = low.astype(BF)
        for copy in self.second(c):
            copy.start()

    def add_second(self, c):
        s, at = c % 4, self.at
        for copy in self.second(c):
            copy.wait()

        def total(z):
            own = self.part[s, z, at["x"]].astype(F32)
            return own + self.r2[c % 6, 0, z].astype(F32) + self.r2[c % 6, 1, z].astype(F32)

        self.zs[c % 2] = total(1 - at["zl"]).astype(BF)
        for copy in self.third(c):
            copy.start()
        self.mine[c % 2] = total(at["zl"])

    def add_third(self, c):
        s = c % 4
        for copy in self.third(c):
            copy.wait()
        self.result(c, self.mine[c % 2] + self.zr[s].astype(F32))

    def steps(self, t):
        for lag, step in ((2, self.add_first), (4, self.add_second), (5, self.add_third)):
            c = t - lag
            pl.when((c >= 0) & (c < 14))(lambda step=step, c=c: step(c))
            pl.when((c >= 16) & (c < 18))(lambda step=step, c=c - 2: step(c))


class SmallSum:
    def scratch():
        return [
            pltpu.VMEM((8, 8, 1024), F32),
            pltpu.VMEM((4, 8, 1024), F32),
            pltpu.VMEM((4, 8, 1024), F32),
            pltpu.SemaphoreType.DMA((13,)),
            pltpu.SemaphoreType.DMA((13,)),
        ]

    def __init__(self, scratch):
        self.b1, self.b2, self.b3, self.send, self.recv = scratch
        dp, tensor = lax.axis_index("dp"), lax.axis_index("tensor")
        y, self.zh, core = dp // 4, (dp // 2) % 2, dp % 2
        self.zl, self.x = tensor // 4, tensor % 4
        self.i1 = y * 2 + core
        self.i2 = self.zh * 2 + self.zl
        self.d1, self.d2, self.d3 = [], [], []
        for k in range(1, 8):
            j = (self.i1 + k) % 8
            self.d1.append(((j // 2) * 4 + self.zh * 2 + j % 2, tensor))
        for k in range(1, 4):
            j = (self.i2 + k) % 4
            self.d2.append((y * 4 + (j // 2) * 2 + core, (j % 2) * 4 + self.x))
            self.d3.append((dp, self.zl * 4 + (self.x + k) % 4))

    def devices(self):
        return self.d1 + self.d2 + self.d3

    def copies(self, stage):
        buf, mine, devices, base = ((self.b1, self.i1, self.d1, 0), (self.b2, self.i2, self.d2, 7),
                                    (self.b3, self.x, self.d3, 10))[stage]
        return [rcopy(buf.at[mine], buf.at[mine], self.send.at[base + k], self.recv.at[base + k], device)
                for k, device in enumerate(devices)]

    def start(self, stage):
        for copy in self.copies(stage):
            copy.start()

    def wait(self, stage):
        for copy in self.copies(stage):
            copy.wait()

    def second(self):
        self.wait(0)
        total = self.b1[0]
        for k in range(1, 8):
            total = total + self.b1[k]
        self.b2[self.i2] = total
        self.start(1)

    def third(self):
        self.wait(1)
        wide = self.b2[0] + self.b2[1] + self.b2[2] + self.b2[3]
        narrow = self.b2[self.zl] + self.b2[2 + self.zl]
        row = lax.broadcasted_iota(jnp.int32, (8, 1024), 0)
        self.b3[self.x] = jnp.where(row < 6, wide, narrow)
        self.start(2)

    def result(self):
        self.wait(2)
        wide = self.b3[0] + self.b3[1] + self.b3[2] + self.b3[3]
        row = lax.broadcasted_iota(jnp.int32, (8, 1024), 0)
        return jnp.where(row < 6, wide, self.b3[self.x])


def gelu_parts(u):
    inner = 0.7978845608028654 * (u + 0.044715 * (u * u * u))
    return jnp.tanh(inner)


def swap_pairs(v):
    lane = lax.broadcasted_iota(jnp.int32, v.shape, 1)
    return jnp.where(lane % 32 < 16, pltpu.roll(v, 112, 1), pltpu.roll(v, 16, 1))


def turn(v, cosine, sine):
    return v * cosine + swap_pairs(v) * sine


WIDE = 14
UNITS = ((3, (0, 2)), (3, (2, 4)), (2, (0, 2)), (2, (2, 4)), (1, (0, 4)), (0, (0, 4)))
RS = 8
FEAT, MID = 1792, 1280


def block_kernel(
    tokens, cotangent, seg_row, gain_h, shift_h, b_qkv, b_out_h, b_up_h, b_down_h,
    w_qkv_h, w_out_h, w_up_h, w_down_h,
    pieces, output, input_grad, sums,
    w_in, w_mid, w_sem,
    gain, shift, b_sum,
    normed_t, pre, grad_mid, rows, turned, mid, heads_t, outs_gt, grad_feat,
    cos_t, sin_t, seg_c, seg_r, lse, out_f, q_m, g_m, ds_b, q_2, g_2, mean_row, rstd,
    *scratch,
):
    at = neighbours()
    bias, p_b = grad_feat.at[:, pl.ds(1024, 256)], grad_feat.at[:, pl.ds(1280, 512)]
    s_f, d_f, grad_n = (grad_mid.at[:, pl.ds(a, n)] for a, n in ((0, 512), (512, 512), (1024, 256)))
    act_t = grad_feat
    n1, n2, n3 = len(GradSum.scratch()), len(Gather.scratch()), len(RowSum.scratch())
    small = SmallSum(scratch[n1 + n2 + n3:])

    def unit(cols):
        return (tokens[:, cols].astype(F32) - mean_row[:, 0:1]) * rstd[:, 0:1]

    def own_chunk(c):
        cols = at_rows(c % 8)
        normed = (unit(cols) * gain[0:1, cols] + shift[0:1, cols]).astype(BF)
        return jnp.where(c < 8, normed, cotangent[:, cols])

    grads = GradSum(at, pieces, scratch[:n1])
    gather = Gather(at, own_chunk, scratch[n1:n1 + n2])

    def keep_rows(c, value):
        branch = (c < 6) | (c >= 14)

        @pl.when(branch)
        def _():
            cols = at_rows(jnp.where(c < 6, c, c - 8))
            own = tokens[:, cols].astype(F32) + value + b_sum[0:1, cols]
            output[:, cols] = own.astype(BF)

        @pl.when(jnp.logical_not(branch))
        def _():
            grad_n[at_rows(c - 6, 128), :] = value

    row_sum = RowSum(at, scratch[n1 + n2:n1 + n2 + n3], keep_rows)

    moves = [(w_up_h, w_in.at[:, pl.ds(0, 1024)])]
    moves += [(w_qkv_h.at[k], w_in.at[:, pl.ds(1024 + 256 * k, 256)]) for k in range(3)]
    moves += [(w_down_h, w_mid.at[pl.ds(0, 1024)]), (w_out_h, w_mid.at[pl.ds(1024, 256)])]
    weights = [pltpu.make_async_copy(src, dst, w_sem.at[i]) for i, (src, dst) in enumerate(moves)]

    barrier = pltpu.get_barrier_semaphore()
    greeted = small.devices()
    for device in greeted:
        pl.semaphore_signal(barrier, inc=1, device_id=device, device_id_type=MESH)
    for copy in weights:
        copy.start()

    gain[...] = gain_h[...].astype(F32).reshape(1, 2048)
    shift[...] = shift_h[...].astype(F32).reshape(1, 2048)
    b_sum[...] = (b_out_h[...].astype(F32) + b_down_h[...].astype(F32)).reshape(1, 2048)
    x = tokens[...].astype(F32)
    mean = jnp.mean(x, axis=1, keepdims=True)
    centered = x - mean
    scale = lax.rsqrt(jnp.mean(centered * centered, axis=1, keepdims=True) + EPSILON)
    rstd[...] = jnp.broadcast_to(scale, (128, 128))
    mean_row[...] = jnp.broadcast_to(mean, (128, 128))

    pl.semaphore_wait(barrier, len(greeted))
    for c in range(Gather.AHEAD):
        gather.begin(c)

    seg_f = seg_row[...].astype(F32)
    seg_r[...] = jnp.broadcast_to(seg_f, (8, 1024))
    seg_c[...] = jnp.broadcast_to(seg_f, (128, 1024)).T
    @pl.loop(0, 4)
    def _(b):
        r = at_rows(b)
        i = lax.broadcasted_iota(jnp.int32, (256, 1024), 0) + b * 256
        j = lax.broadcasted_iota(jnp.int32, (256, 1024), 1)
        same = jnp.where((seg_c[r, 0:1] == seg_r[0:1, :]) & (j < i), 1.0, 0.0)
        position = jnp.sum(same, axis=1, keepdims=True)
        lane = lax.broadcasted_iota(jnp.int32, (256, 128), 1) % 64
        power = jnp.exp((lane % 16).astype(F32) * (-2.0 / ROT * 9.210340371976184))
        angle = position * power
        sine = jnp.sin(angle)
        cos_t[r, :] = jnp.where(lane < ROT, jnp.cos(angle), 1.0)
        sin_t[r, :] = jnp.where(lane < ROT // 2, -sine, jnp.where(lane < ROT, sine, 0.0))
        pre[r, 0:1024] = jnp.broadcast_to(b_up_h[...].astype(F32).reshape(1, 1024), (256, 1024))
        for k in range(3):
            cols = slice(1024 + k * 256, 1280 + k * 256)
            pre[r, cols] = jnp.broadcast_to(b_qkv[k:k + 1, :].astype(F32), (256, 256))

    @pl.loop(0, 10)
    def _(i):
        gather.steps(i)

        @pl.when(i == 2)
        def _():
            for copy in weights[:4]:
                copy.wait()

        @pl.when(i >= 2)
        def _():
            c = i - 2

            @pl.loop(0, 2)
            def _(b):
                r = at_rows(b, 512)
                a = gather.all[c % 8, r, :]
                pre[r, :] += dot(a, w_in[at_rows(c), :])
            normed_t[at_rows(c), :] = gather.all[c % 8].T

    def gelu(b):
        r = at_rows(b)
        for k in range(4):
            cols = slice(k * 256, k * 256 + 256)
            u = pre[r, cols]
            a = (u * (0.5 * (1.0 + gelu_parts(u)))).astype(BF)
            mid[r, cols] = a
            act_t[cols, r] = a.T

    pl.loop(0, 2)(gelu)
    gather.steps(10)
    pl.loop(2, 4)(gelu)
    for copy in weights[4:]:
        copy.wait()

    def make_rows(b):
        r = at_rows(b)
        for k in range(3):
            for half in range(2):
                v = pre[r, 1024 + k * 256 + half * 128:1152 + k * 256 + half * 128]
                if k < 2:
                    v = turn(v, cos_t[r, :], sin_t[r, :])
                if k == 0:
                    v = v * HEAD_DIM ** -0.5
                v = v.astype(BF)
                cols = slice(half * 128, half * 128 + 128)
                if k > 0:
                    rows[k - 1, r, cols] = v
                turned[k, cols, r] = v.T

    def attend_bias(qb):
        cols = slice(qb * 256, qb * 256 + 256)
        for kb in range(qb + 1):
            r = slice(kb * 256, kb * 256 + 256)
            keep = seg_c[r, 0:1] == seg_r[0:1, cols]
            if kb == qb:
                i = lax.broadcasted_iota(jnp.int32, (256, 256), 0)
                j = lax.broadcasted_iota(jnp.int32, (256, 256), 1)
                keep = keep & (i <= j)
            bias[r, :] = jnp.where(keep, 0.0, -1e30).astype(BF)

    def head_rows(h, count=64):
        return pl.ds(pl.multiple_of(h * 64, 64), count)

    def two_heads(ref, source, pair, cols):
        ref[...] = jnp.zeros_like(ref)
        for k in range(2):
            hr = head_rows(pair * 2 + k)
            ref[hr, k * 256:k * 256 + 256] = source[hr, cols]

    def both(value):
        return jnp.concatenate([value, value], axis=1)

    def blocks(n):
        return [slice(b, b + 64) for b in range(0, n, 64)]

    def over_rows(op, value):
        return op(value.reshape(8, 8, 512), axis=0)

    def attend(qb, heads):
        cols = slice(qb * 256, qb * 256 + 256)
        n = (qb + 1) * 256
        if heads[0] == 0:
            attend_bias(qb)
        s_f = pre.at[:, pl.ds(1024, 512)]

        @pl.loop(heads[0] // 2, heads[1] // 2)
        def _(pair):
            two_heads(q_m, turned.at[0], pair, cols)
            s_f[0:n, :] = dot(rows[0, 0:n, :], q_m[...])
            most = jnp.full((8, 512), -jnp.inf, F32)
            for r in blocks(n):
                s = s_f[r, :] + both(bias[r, :].astype(F32))
                s_f[r, :] = s
                most = jnp.maximum(most, over_rows(jnp.max, s))
            most = jnp.max(most, axis=0, keepdims=True)
            total = jnp.zeros((8, 512), F32)
            for r in blocks(n):
                e = jnp.exp(s_f[r, :] - most)
                total = total + over_rows(jnp.sum, e)
                ds_b[r, :] = e.astype(BF)
            total = jnp.sum(total, axis=0, keepdims=True)
            share, log_total = 1.0 / total, most + jnp.log(total)
            out = dot(turned[2, head_rows(pair * 2, 128), 0:n], ds_b[0:n, :])
            for k in range(2):
                h, side = pair * 2 + k, slice(k * 256, k * 256 + 256)
                value = out[k * 64:k * 64 + 64, side] * share[:, side]
                out_f[head_rows(h), cols] = value
                heads_t[head_rows(h), cols] = value.astype(BF)
                lse[pl.ds(h, 1), cols] = log_total[:, side]

    def attend_back(qb, heads):
        cols = slice(qb * 256, qb * 256 + 256)
        n = (qb + 1) * 256
        if heads[0] == 0:
            attend_bias(qb)

        @pl.loop(heads[0] // 2, heads[1] // 2)
        def _(pair):
            pair_rows = head_rows(pair * 2, 128)
            two_heads(q_m, turned.at[0], pair, cols)
            two_heads(g_m, outs_gt, pair, cols)
            s_f[0:n, :] = dot(rows[0, 0:n, :], q_m[...])
            d_f[0:n, :] = dot(rows[1, 0:n, :], g_m[...])
            log_total = jnp.concatenate([lse[pl.ds(pair * 2 + k, 1), cols] for k in range(2)], axis=1)
            product = outs_gt[pair_rows, cols].astype(F32) * out_f[pair_rows, cols]
            delta = jnp.concatenate([jnp.sum(product[k * 64:k * 64 + 64], axis=0, keepdims=True)
                                     for k in range(2)], axis=1)
            for r in blocks(n):
                p = jnp.exp(s_f[r, :] + both(bias[r, :].astype(F32)) - log_total)
                p_b[r, :] = p.astype(BF)
                ds_b[r, :] = (p * (d_f[r, :] - delta)).astype(BF)
            q_2[...] = q_m[...].T
            g_2[...] = g_m[...].T
            grad_q = dot(turned[1, pair_rows, 0:n], ds_b[0:n, :])
            for k in range(2):
                pre[pl.ds(pl.multiple_of(qb * 256 + pair * 128 + k * 64, 64), 64), 1024:1280] = grad_q[
                    k * 64:k * 64 + 64, k * 256:k * 256 + 256]
            pre[0:n, 1536:1792] += dot(p_b[0:n, :], g_2[...])
            pre[0:n, 1280:1536] += dot(ds_b[0:n, :], q_2[...])

    @pl.loop(0, 8)
    def _(t):
        grads.steps(t)
        chunk = gather.all[t]
        grads.own[t % 2] = dot(act_t[:, 0:1024], chunk).astype(BF)
        grads.send_piece(t)
        gather.steps(11 + t)

        @pl.when(t == 0)
        def _():
            grad_mid[...] = jnp.zeros_like(grad_mid)

        @pl.loop(0, 2)
        def _(b):
            r = at_rows(b, 512)
            grad_mid[r, :] += dot_nt(gather.all[t, r, :], w_mid[:, at_rows(t)])

        @pl.when(t < 2)
        def _():
            make_rows(2 * t)
            make_rows(2 * t + 1)

        for i, (qb, heads) in enumerate(UNITS):
            pl.when(t == 2 + i)(lambda qb=qb, heads=heads: attend(qb, heads))

    def branch_chunk(t, c):
        row_sum.store(t - RS, dot(mid[...], w_mid[:, at_rows(c)]))
        row_sum.send_chunk(t - RS)

    def normed_chunk(t, c):
        row_sum.store(t - RS, dot_nt(grad_feat[...], w_in[at_rows(c), :]))
        row_sum.send_chunk(t - RS)

    def gelu_back(k):
        @pl.loop(0, 4)
        def _(b):
            r, cols = at_rows(b), at_rows(k)
            u = pre[r, cols]
            th = gelu_parts(u)
            slope = 0.5 * (1.0 + th) + 0.5 * u * (1.0 - th * th) * (
                0.7978845608028654 * (1.0 + 3 * 0.044715 * (u * u)))
            grad_feat[r, cols] = (slope * grad_mid[r, cols]).astype(BF)

    def feature_piece(t):
        @pl.when(t % 2 == 0)
        def _():
            value = dot(normed_t[...], grad_feat[:, at_rows((t - 10) // 2)])
            for k in range(2):
                grads.own[k] = value[k * 1024:k * 1024 + 1024].astype(BF)

        grads.send_piece(t)

    @pl.loop(0, 4)
    def _(b):
        r = at_rows(b)
        mid[r, 1024:1280] = heads_t[:, r].T
        outs_gt[:, r] = grad_mid[r, 1024:1280].astype(BF).T
        pre[r, 1024:1792] = jnp.zeros((256, 768), F32)

    @pl.loop(8, 10)
    def _(t):
        grads.steps(t)
        row_sum.steps(t - RS)
        for j in range(4):
            r = slice(j * 256, j * 256 + 256)
            grads.own[t % 2, r, :] = dot(heads_t[...], gather.all[4 * (t - 8) + j]).astype(BF)
        grads.send_piece(t)
        branch_chunk(t, t - RS)

        @pl.when(t == 8)
        def _():
            for k in range(4):
                gelu_back(k)

        pl.when(t == 9)(lambda: attend_back(*UNITS[0]))

    @pl.loop(10, 14)
    def _(t):
        grads.steps(t)
        row_sum.steps(t - RS)
        feature_piece(t)
        branch_chunk(t, t - RS)
        for i, (qb, heads) in enumerate((UNITS[1], (2, (0, 4)), *UNITS[4:])):
            pl.when(t == 10 + i)(lambda qb=qb, heads=heads: attend_back(qb, heads))

    for b in range(4):
        r = slice(b * 256, b * 256 + 256)
        grad_q = pre[r, 1024:1280].T * HEAD_DIM ** -0.5
        for half in range(2):
            a = half * 128
            cosine, sine = cos_t[r, :], -sin_t[r, :]
            grad_feat[r, 1024 + a:1152 + a] = turn(grad_q[:, a:a + 128], cosine, sine).astype(BF)
            grad_feat[r, 1280 + a:1408 + a] = turn(pre[r, 1280 + a:1408 + a], cosine, sine).astype(BF)
        grad_feat[r, 1536:1792] = pre[r, 1536:1792].astype(BF)

    @pl.loop(14, 24)
    def _(t):
        grads.steps(t)
        row_sum.steps(t - RS)
        feature_piece(t)
        pl.when(t < 22)(lambda: normed_chunk(t, t - 14))

    def late_steps(t):
        grads.steps(t)
        row_sum.steps(t - RS)

    @pl.loop(24, 27)
    def _(t):
        late_steps(t)
        pl.when(t < 26)(lambda: branch_chunk(t - 2, t - 18))

    def column_sum(value):
        return jnp.sum(value.astype(F32), axis=0, keepdims=True)

    mine = small.i1
    small.b1[mine] = jnp.zeros((8, 1024), F32)
    mean_plain = jnp.zeros((128, 1), F32)
    mean_unit = jnp.zeros((128, 1), F32)
    for c in range(8):
        cols = slice(c * 256, c * 256 + 256)
        row, lanes = c // 4, slice((c % 4) * 256, (c % 4) * 256 + 256)
        g = grad_n[c * 128:c * 128 + 128, :]
        n = unit(cols)
        scaled = g * gain[0:1, cols]
        mean_plain = mean_plain + jnp.sum(scaled, axis=1, keepdims=True)
        mean_unit = mean_unit + jnp.sum(scaled * n, axis=1, keepdims=True)
        small.b1[mine, row:row + 1, lanes] = column_sum(g * n)
        small.b1[mine, 2 + row:3 + row, lanes] = column_sum(g)
        small.b1[mine, 4 + row:5 + row, lanes] = column_sum(cotangent[:, cols])
    for k in range(7):
        row, lanes = 6 + k // 4, slice((k % 4) * 256, (k % 4) * 256 + 256)
        small.b1[mine, row:row + 1, lanes] = column_sum(grad_feat[:, k * 256:k * 256 + 256])
    small.start(0)
    late_steps(27)
    mean_plain = mean_plain / 2048.0
    mean_unit = mean_unit / 2048.0
    for c in range(8):
        cols = slice(c * 256, c * 256 + 256)
        inner = grad_n[c * 128:c * 128 + 128, :] * gain[0:1, cols] - mean_plain - unit(cols) * mean_unit
        input_grad[:, cols] = (cotangent[:, cols].astype(F32) + rstd[:, 0:1] * inner).astype(BF)

    late_steps(28)
    small.second()
    late_steps(29)
    late_steps(30)
    small.third()
    late_steps(31)
    late_steps(32)
    sums[...] = small.result()
    late_steps(33)


def run_block(tokens, segment, ln_gain, ln_bias, w_qkv, b_qkv, w_out, b_out, w_up, b_up, w_down,
              b_down, cotangent):
    vmem = pl.BlockSpec(memory_space=pltpu.VMEM)
    hbm = pl.BlockSpec(memory_space=pl.ANY)
    V = pltpu.VMEM
    scratch = [
        V((2048, FEAT), BF), V((MID, 2048), BF), pltpu.SemaphoreType.DMA((6,)),
        V((1, 2048), F32), V((1, 2048), F32), V((1, 2048), F32),
        V((2048, 1024), BF),
        V((1024, FEAT), F32), V((1024, MID), F32),
        V((2, 1024, 256), BF), V((3, 256, 1024), BF),
        V((1024, MID), BF), V((256, 1024), BF),
        V((256, 1024), BF),
        V((1024, FEAT), BF),
        V((1024, 128), F32), V((1024, 128), F32),
        V((1024, 128), F32), V((8, 1024), F32),
        V((8, 1024), F32),
        V((256, 1024), F32),
        V((256, 512), BF), V((256, 512), BF), V((1024, 512), BF),
        V((512, 256), BF), V((512, 256), BF),
        V((128, 128), F32), V((128, 128), F32),
    ] + GradSum.scratch() + Gather.scratch() + RowSum.scratch() + SmallSum.scratch()
    return pl.pallas_call(
        block_kernel,
        out_shape=(
            jax.ShapeDtypeStruct((NP, 1024, 256), BF),
            jax.ShapeDtypeStruct((128, 2048), BF),
            jax.ShapeDtypeStruct((128, 2048), BF),
            jax.ShapeDtypeStruct((8, 1024), F32),
        ),
        in_specs=[vmem] * 9 + [hbm] * 4,
        out_specs=(hbm, vmem, vmem, vmem),
        scratch_shapes=scratch,
        compiler_params=pltpu.CompilerParams(
            collective_id=0, has_side_effects=True, vmem_limit_bytes=VMEM_LIMIT),
        cost_estimate=pl.CostEstimate(flops=50 * 10**9, bytes_accessed=30 << 20, transcendentals=10**7),
    )(
        tokens, cotangent, segment.reshape(1, 1024), ln_gain, ln_bias, b_qkv, b_out, b_up, b_down,
        w_qkv.transpose(1, 0, 2), w_out, w_up, w_down,
    )


def widen_kernel(qkv_p, out_p, down_p, up_p, output, input_grad, sums,
                 down, out, up, qkv, output_o, input_grad_o, gain_o, shift_o, b_out_o, b_down_o, b_up_o, b_qkv_o):
    for c in range(8):
        cols = slice(c * 256, c * 256 + 256)
        down[:, cols] = down_p[c].astype(F32)
        out[:, cols] = out_p[c].astype(F32)
    for c in range(4):
        up[:, c * 256:c * 256 + 256] = up_p[c, 0].astype(F32)
    qkv[...] = qkv_p[...].astype(F32)
    output_o[...] = output[...]
    input_grad_o[...] = input_grad[...]

    @pl.when(pl.program_id(0) == 0)
    def _():
        gain_o[...] = sums[0:2, :].reshape(2048)
        shift_o[...] = sums[2:4, :].reshape(2048)
        b_out_o[...] = sums[4:6, :].reshape(2048)
        b_down_o[...] = sums[4:6, :].reshape(2048)
        b_up_o[...] = sums[6:7, :].reshape(1024)
        for c in range(3):
            b_qkv_o[c:c + 1, :] = sums[7:8, c * 256:c * 256 + 256]


def widen(pieces, output, input_grad, sums):
    def rows(count, width):
        return pl.BlockSpec((count, width), lambda i: (i, 0))

    def whole(*shape):
        return pl.BlockSpec(shape, lambda i: (0,) * len(shape))

    def shape(*dims, kind=F32):
        return jax.ShapeDtypeStruct(dims, kind)

    down, out, up, qkv, *rest = pl.pallas_call(
        widen_kernel,
        grid=(8,),
        out_shape=(
            shape(1024, 2048), shape(256, 2048), shape(2048, 1024), shape(6144, 256),
            shape(128, 2048, kind=BF), shape(128, 2048, kind=BF),
            shape(2048), shape(2048), shape(2048), shape(2048), shape(1024), shape(3, 256),
        ),
        in_specs=[
            rows(768, 256),
            pl.BlockSpec((8, 32, 256), lambda i: (3, i, 0)),
            pl.BlockSpec((8, 128, 256), lambda i: (1, i, 0)),
            pl.BlockSpec((4, 1, 256, 256), lambda i: (2, i // 4, i % 4, 0)),
            rows(16, 2048), rows(16, 2048), whole(8, 1024),
        ],
        out_specs=(
            rows(128, 2048), rows(32, 2048), rows(256, 1024), rows(768, 256),
            rows(16, 2048), rows(16, 2048),
            whole(2048), whole(2048), whole(2048), whole(2048), whole(1024), whole(3, 256),
        ),
        compiler_params=pltpu.CompilerParams(vmem_limit_bytes=VMEM_LIMIT),
    )(
        pieces.reshape(NP * 1024, 256), pieces.reshape(NP * 4, 256, 256), pieces,
        pieces.reshape(NP // 2, 2, 1024, 256), output, input_grad, sums,
    )
    return down, out, up, qkv.reshape(3, 2048, 256).transpose(1, 0, 2), rest


def on_device(*args):
    pieces, output, input_grad, sums = run_block(*args)
    down, out, up, qkv, rest = widen(pieces, output, input_grad, sums)
    output, input_grad, gain, shift, b_out, b_down, b_up, b_qkv = rest
    return output, input_grad, gain, shift, qkv, b_qkv, out, b_out, up, b_up, down, b_down


def solution(mesh):
    placed = (
        P(("dp", "tensor"), None),
        P("dp"),
        P(),
        P(),
        P(None, None, "tensor"),
        P(None, "tensor"),
        P("tensor", None),
        P(),
        P(None, "tensor"),
        P("tensor"),
        P("tensor", None),
        P(),
        P(("dp", "tensor"), None),
    )
    return jax.shard_map(
        on_device,
        mesh=mesh,
        in_specs=placed,
        out_specs=(
            P(("dp", "tensor"), None),
            P(("dp", "tensor"), None),
            P(),
            P(),
            P(None, None, "tensor"),
            P(None, "tensor"),
            P("tensor", None),
            P(),
            P(None, "tensor"),
            P("tensor"),
            P("tensor", None),
            P(),
        ),
        check_vma=False,
    )
```

```python
import jax
import jax.numpy as jnp
from jax import lax
from jax.experimental import pallas as pl
from jax.experimental.pallas import tpu as pltpu
from jax.sharding import PartitionSpec as P

HEAD_DIM = 64
ROT = 32
EPSILON = 1e-05
MESH = pl.DeviceIdType.MESH
BF = jnp.bfloat16
F32 = jnp.float32
NP = 24
VMEM_LIMIT = 64 << 20


def neighbours():
    dp = lax.axis_index("dp")
    tensor = lax.axis_index("tensor")
    y, zh, core = dp // 4, (dp // 2) % 2, dp % 2
    zl, x = tensor // 4, tensor % 4
    yl, yr, yo = (y + 3) % 4, (y + 1) % 4, (y + 2) % 4
    xl, xr, xo = (x + 3) % 4, (x + 1) % 4, (x + 2) % 4
    where = dict(y=y, core=core, zl=zl, x=x, yl=yl, yr=yr, yo=yo, xl=xl, xr=xr, xo=xo)
    where["dev_yl"] = (yl * 4 + zh * 2 + core, tensor)
    where["dev_yr"] = (yr * 4 + zh * 2 + core, tensor)
    where["dev_zh"] = (y * 4 + (1 - zh) * 2 + core, tensor)
    where["dev_core"] = (y * 4 + zh * 2 + 1 - core, tensor)
    where["dev_xl"] = (dp, zl * 4 + xl)
    where["dev_xr"] = (dp, zl * 4 + xr)
    where["dev_zl"] = (dp, (1 - zl) * 4 + x)
    return where


def greet(devices):
    barrier = pltpu.get_barrier_semaphore()
    for device in devices:
        pl.semaphore_signal(barrier, inc=1, device_id=device, device_id_type=MESH)
    pl.semaphore_wait(barrier, len(devices))


def rcopy(src, dst, send, recv, device):
    return pltpu.make_async_remote_copy(
        src_ref=src, dst_ref=dst, send_sem=send, recv_sem=recv, device_id=device, device_id_type=MESH
    )


def rows_at(index, size, count=None):
    return pl.ds(pl.multiple_of(index * size, size), size if count is None else count)


class GradSum:
    def scratch():
        return [
            pltpu.VMEM((2, 1024, 256), BF),
            pltpu.VMEM((2, 512, 256), BF),
            pltpu.VMEM((4, 512, 256), BF),
            pltpu.VMEM((4, 2, 64, 256), BF),
            pltpu.VMEM((6, 2, 128, 256), BF),
            pltpu.VMEM((2, 128, 256), BF),
            pltpu.VMEM((4, 128, 256), BF),
            pltpu.VMEM((3, 128, 256), BF),
            pltpu.SemaphoreType.DMA((11, 8)),
            pltpu.SemaphoreType.DMA((11, 8)),
            pltpu.SemaphoreType.DMA((8,)),
        ]

    def __init__(self, at, out, scratch):
        self.at, self.out = at, out
        (self.own, self.other, self.half, self.r1, self.r2, self.zs, self.zr, self.full,
         self.send, self.recv, self.local) = scratch

    def place(self, p):
        return jnp.where(p < 8, p + 8, jnp.where(p < 10, p - 2, jnp.where(p < 18, p + 6, p - 18)))

    def core_copy(self, p):
        s, at = p % 4, self.at
        return rcopy(self.own.at[p % 2, rows_at(1 - at["core"], 512)], self.other.at[p % 2],
                     self.send.at[0, p % 8], self.recv.at[0, p % 8], at["dev_core"])

    def first_copies(self, p):
        s, at = p % 4, self.at
        top = self.half.at[s, rows_at(at["yo"], 128, 64)]
        low = self.half.at[s, pl.ds(pl.multiple_of(at["yo"] * 128 + 64, 64), 64)]
        return (rcopy(top, self.r1.at[s, 0], self.send.at[1, p % 8], self.recv.at[1, p % 8], at["dev_yr"]),
                rcopy(low, self.r1.at[s, 1], self.send.at[2, p % 8], self.recv.at[2, p % 8], at["dev_yl"]))

    def second_copies(self, p):
        s, at = p % 4, self.at
        return (rcopy(self.half.at[s, rows_at(at["yr"], 128)], self.r2.at[p % 6, 0],
                      self.send.at[3, p % 8], self.recv.at[3, p % 8], at["dev_yr"]),
                rcopy(self.half.at[s, rows_at(at["yl"], 128)], self.r2.at[p % 6, 1],
                      self.send.at[4, p % 8], self.recv.at[4, p % 8], at["dev_yl"]))

    def z_copy(self, p):
        s = p % 4
        return rcopy(self.zs.at[p % 2], self.zr.at[s], self.send.at[5, p % 8], self.recv.at[5, p % 8],
                     self.at["dev_zh"])

    def back_first(self, p):
        s, at = p % 4, self.at
        mine = self.out.at[self.place(p), rows_at(at["core"] * 4 + at["y"], 128)]
        return (rcopy(self.full.at[p % 3], mine, self.send.at[6, p % 8], self.recv.at[6, p % 8], at["dev_yr"]),
                rcopy(self.full.at[p % 3], mine, self.send.at[7, p % 8], self.recv.at[7, p % 8], at["dev_yl"]),
                pltpu.make_async_copy(self.full.at[p % 3], mine, self.local.at[p % 8]))

    def back_second(self, p):
        s, at = p % 4, self.at
        top = self.out.at[self.place(p), rows_at(at["core"] * 4 + at["yl"], 128, 64)]
        low = self.out.at[self.place(p), pl.ds(pl.multiple_of((at["core"] * 4 + at["yr"]) * 128 + 64, 64), 64)]
        return (rcopy(top, top, self.send.at[9, p % 8], self.recv.at[9, p % 8], at["dev_yr"]),
                rcopy(low, low, self.send.at[10, p % 8], self.recv.at[10, p % 8], at["dev_yl"]))

    def back_core(self, p):
        s, at = p % 4, self.at
        mine = self.out.at[self.place(p), rows_at(at["core"], 512)]
        return rcopy(mine, mine, self.send.at[8, p % 8], self.recv.at[8, p % 8], at["dev_core"])

    def send_piece(self, p):
        self.core_copy(p).start()

    def add_core(self, p):
        s = p % 4
        self.core_copy(p).wait()

        @pl.loop(0, 4)
        def _(j):
            rows = rows_at(j, 128)
            mine = self.own[p % 2, pl.ds(pl.multiple_of(self.at["core"] * 512 + j * 128, 128), 128)]
            self.half[s, rows] = (mine.astype(F32) + self.other[p % 2, rows].astype(F32)).astype(BF)

        for copy in self.first_copies(p):
            copy.start()

    def add_first(self, p):
        s, at = p % 4, self.at
        for copy in self.first_copies(p):
            copy.wait()
        top = rows_at(at["yr"], 128, 64)
        low = pl.ds(pl.multiple_of(at["yl"] * 128 + 64, 64), 64)
        self.half[s, top] = (self.half[s, top].astype(F32) + self.r1[s, 0].astype(F32)).astype(BF)
        self.half[s, low] = (self.half[s, low].astype(F32) + self.r1[s, 1].astype(F32)).astype(BF)
        for copy in self.second_copies(p):
            copy.start()

    def add_second(self, p):
        s = p % 4
        for copy in self.second_copies(p):
            copy.wait()
        mine = self.half[s, rows_at(self.at["y"], 128)].astype(F32)
        self.zs[p % 2] = (mine + self.r2[p % 6, 0].astype(F32) + self.r2[p % 6, 1].astype(F32)).astype(BF)
        self.z_copy(p).start()

    def add_z(self, p):
        s = p % 4
        self.z_copy(p).wait()
        self.full[p % 3] = (self.zs[p % 2].astype(F32) + self.zr[s].astype(F32)).astype(BF)
        for copy in self.back_first(p):
            copy.start()

    def forward_y(self, p):
        for copy in self.back_first(p):
            copy.wait()
        for copy in self.back_second(p):
            copy.start()

    def forward_core(self, p):
        for copy in self.back_second(p):
            copy.wait()
        self.back_core(p).start()

    def finish(self, p):
        self.back_core(p).wait()

    def steps(self, t):
        for lag, step in ((1, self.add_core), (2, self.add_first), (4, self.add_second), (5, self.add_z),
                          (7, self.forward_y), (9, self.forward_core), (10, self.finish)):
            p = t - lag
            pl.when((p >= 0) & (p < NP))(lambda step=step, p=p: step(p))


def dot(a, b):
    return lax.dot_general(a, b, (((1,), (0,)), ((), ())), preferred_element_type=F32)


def dot_nt(a, b):
    return lax.dot_general(a, b, (((1,), (1,)), ((), ())), preferred_element_type=F32)


def at_rows(index, size=256):
    return pl.ds(pl.multiple_of(index * size, size), size)


class Gather:
    AHEAD = 2

    def scratch():
        return [
            pltpu.VMEM((8, 1024, 256), BF),
            pltpu.SemaphoreType.DMA((9, 8)),
            pltpu.SemaphoreType.DMA((9, 8)),
        ]

    def __init__(self, at, own, scratch):
        self.at, self.own = at, own
        self.all, self.send, self.recv = scratch

    def copy(self, kind, c, src, dst, device):
        s = c % 8
        return rcopy(src, dst, self.send.at[kind, s], self.recv.at[kind, s], self.at[device])

    def part(self, c, zl, x, begin=0, count=128):
        first = pl.multiple_of((zl * 4 + x) * 128 + begin, 64)
        return self.all.at[c % 8, pl.ds(first, count)]

    def same(self, kind, c, block, device):
        return self.copy(kind, c, block, block, device)

    def first(self, c, wide):
        at = self.at
        mine = self.part(c, at["zl"], at["x"])
        copies = [self.same(0, c, mine, "dev_xr"), self.same(1, c, mine, "dev_xl")]
        return copies if wide else copies + [self.same(2, c, mine, "dev_zl")]

    def ring(self, c):
        at = self.at
        return [self.same(3, c, self.part(c, at["zl"], at["xl"], 0, 64), "dev_xr"),
                self.same(4, c, self.part(c, at["zl"], at["xr"], 64, 64), "dev_xl")]

    def second(self, c, wide):
        at = self.at
        if wide:
            return [self.same(5, c, self.part(c, at["zl"], at["x"]), "dev_zl"),
                    self.same(6, c, self.part(c, at["zl"], at["xl"]), "dev_zl"),
                    self.same(7, c, self.part(c, at["zl"], at["xr"]), "dev_zl")]
        other = self.part(c, 1 - at["zl"], at["x"])
        return [self.same(5, c, other, "dev_xr"), self.same(6, c, other, "dev_xl")]

    def third(self, c, wide):
        at = self.at
        if wide:
            return [self.same(8, c, self.part(c, at["zl"], at["xo"]), "dev_zl")]
        return [self.same(7, c, self.part(c, 1 - at["zl"], at["xl"], 0, 64), "dev_xr"),
                self.same(8, c, self.part(c, 1 - at["zl"], at["xr"], 64, 64), "dev_xl")]

    def begin(self, c):
        def start(wide):
            for copy in self.first(c, wide):
                copy.start()

        self.part(c, self.at["zl"], self.at["x"])[...] = self.own(c)
        self.either(c, start)

    def either(self, c, step):
        wide = (c % 2 == 1) & (c < WIDE)
        pl.when((c >= 0) & (c < 16) & wide)(lambda: step(True))
        pl.when((c >= 0) & (c < 16) & jnp.logical_not(wide))(lambda: step(False))

    def steps(self, c):
        def second(wide):
            for copy in self.first(c, wide):
                copy.wait()
            for copy in self.ring(c) + self.second(c, wide):
                copy.start()

        def third(wide):
            for copy in self.ring(c - 1) if wide else self.ring(c - 1) + self.second(c - 1, wide):
                copy.wait()
            for copy in self.third(c - 1, wide):
                copy.start()

        def last(wide):
            for copy in self.second(c - 2, wide) + self.third(c - 2, wide) if wide else self.third(c - 2, wide):
                copy.wait()

        self.either(c, second)
        pl.when(c + self.AHEAD < 16)(lambda: self.begin(c + self.AHEAD))
        self.either(c - 1, third)
        self.either(c - 2, last)


class RowSum:
    def scratch():
        return [
            pltpu.VMEM((4, 2, 4, 128, 256), BF),
            pltpu.VMEM((6, 2, 2, 64, 256), BF),
            pltpu.VMEM((6, 2, 2, 128, 256), BF),
            pltpu.VMEM((2, 128, 256), BF),
            pltpu.VMEM((4, 128, 256), BF),
            pltpu.VMEM((2, 128, 256), F32),
            pltpu.SemaphoreType.DMA((5, 8)),
            pltpu.SemaphoreType.DMA((5, 8)),
        ]

    def __init__(self, at, scratch, result):
        self.at, self.result = at, result
        self.part, self.r1, self.r2, self.zs, self.zr, self.mine, self.send, self.recv = scratch

    def copy(self, kind, c, src, dst, device):
        s = c % 8
        return rcopy(src, dst, self.send.at[kind, s], self.recv.at[kind, s], device)

    def first(self, c):
        s, at = c % 4, self.at
        return [self.copy(0, c, self.part.at[s, :, at["xo"], pl.ds(0, 64)], self.r1.at[c % 6, 0], at["dev_xr"]),
                self.copy(1, c, self.part.at[s, :, at["xo"], pl.ds(64, 64)], self.r1.at[c % 6, 1], at["dev_xl"])]

    def second(self, c):
        s, at = c % 4, self.at
        return [self.copy(2, c, self.part.at[s, :, at["xr"]], self.r2.at[c % 6, 0], at["dev_xr"]),
                self.copy(3, c, self.part.at[s, :, at["xl"]], self.r2.at[c % 6, 1], at["dev_xl"])]

    def third(self, c):
        s = c % 4
        return [self.copy(4, c, self.zs.at[c % 2], self.zr.at[s], self.at["dev_zl"])]

    def store(self, c, value):
        for k in range(8):
            self.part[c % 4, k // 4, k % 4] = value[k * 128:(k + 1) * 128].astype(BF)

    def send_chunk(self, c):
        for copy in self.first(c):
            copy.start()

    def add_first(self, c):
        s, at = c % 4, self.at
        for copy in self.first(c):
            copy.wait()
        for z in range(2):
            top = self.part[s, z, at["xr"], 0:64].astype(F32) + self.r1[c % 6, 0, z].astype(F32)
            self.part[s, z, at["xr"], 0:64] = top.astype(BF)
            low = self.part[s, z, at["xl"], 64:128].astype(F32) + self.r1[c % 6, 1, z].astype(F32)
            self.part[s, z, at["xl"], 64:128] = low.astype(BF)
        for copy in self.second(c):
            copy.start()

    def add_second(self, c):
        s, at = c % 4, self.at
        for copy in self.second(c):
            copy.wait()

        def total(z):
            own = self.part[s, z, at["x"]].astype(F32)
            return own + self.r2[c % 6, 0, z].astype(F32) + self.r2[c % 6, 1, z].astype(F32)

        self.zs[c % 2] = total(1 - at["zl"]).astype(BF)
        for copy in self.third(c):
            copy.start()
        self.mine[c % 2] = total(at["zl"])

    def add_third(self, c):
        s = c % 4
        for copy in self.third(c):
            copy.wait()
        self.result(c, self.mine[c % 2] + self.zr[s].astype(F32))

    def steps(self, t):
        for lag, step in ((2, self.add_first), (4, self.add_second), (5, self.add_third)):
            c = t - lag
            pl.when((c >= 0) & (c < 16))(lambda step=step, c=c: step(c))


class SmallSum:
    def scratch():
        return [
            pltpu.VMEM((8, 8, 1024), F32),
            pltpu.VMEM((4, 8, 1024), F32),
            pltpu.VMEM((4, 8, 1024), F32),
            pltpu.SemaphoreType.DMA((13,)),
            pltpu.SemaphoreType.DMA((13,)),
        ]

    def __init__(self, scratch):
        self.b1, self.b2, self.b3, self.send, self.recv = scratch
        dp, tensor = lax.axis_index("dp"), lax.axis_index("tensor")
        y, self.zh, core = dp // 4, (dp // 2) % 2, dp % 2
        self.zl, self.x = tensor // 4, tensor % 4
        self.i1 = y * 2 + core
        self.i2 = self.zh * 2 + self.zl
        self.d1, self.d2, self.d3 = [], [], []
        for k in range(1, 8):
            j = (self.i1 + k) % 8
            self.d1.append(((j // 2) * 4 + self.zh * 2 + j % 2, tensor))
        for k in range(1, 4):
            j = (self.i2 + k) % 4
            self.d2.append((y * 4 + (j // 2) * 2 + core, (j % 2) * 4 + self.x))
            self.d3.append((dp, self.zl * 4 + (self.x + k) % 4))

    def devices(self):
        return self.d1 + self.d2 + self.d3

    def copies(self, stage):
        buf, mine, devices, base = ((self.b1, self.i1, self.d1, 0), (self.b2, self.i2, self.d2, 7),
                                    (self.b3, self.x, self.d3, 10))[stage]
        return [rcopy(buf.at[mine], buf.at[mine], self.send.at[base + k], self.recv.at[base + k], device)
                for k, device in enumerate(devices)]

    def start(self, stage):
        for copy in self.copies(stage):
            copy.start()

    def wait(self, stage):
        for copy in self.copies(stage):
            copy.wait()

    def second(self):
        self.wait(0)
        total = self.b1[0]
        for k in range(1, 8):
            total = total + self.b1[k]
        self.b2[self.i2] = total
        self.start(1)

    def third(self):
        self.wait(1)
        wide = self.b2[0] + self.b2[1] + self.b2[2] + self.b2[3]
        narrow = self.b2[self.zl] + self.b2[2 + self.zl]
        row = lax.broadcasted_iota(jnp.int32, (8, 1024), 0)
        self.b3[self.x] = jnp.where(row < 6, wide, narrow)
        self.start(2)

    def result(self):
        self.wait(2)
        wide = self.b3[0] + self.b3[1] + self.b3[2] + self.b3[3]
        row = lax.broadcasted_iota(jnp.int32, (8, 1024), 0)
        return jnp.where(row < 6, wide, self.b3[self.x])


def gelu_parts(u):
    inner = 0.7978845608028654 * (u + 0.044715 * (u * u * u))
    return jnp.tanh(inner)


def swap_pairs(v):
    lane = lax.broadcasted_iota(jnp.int32, v.shape, 1)
    return jnp.where(lane % 32 < 16, pltpu.roll(v, 112, 1), pltpu.roll(v, 16, 1))


def turn(v, cosine, sine):
    return v * cosine + swap_pairs(v) * sine


WIDE = 14
UNITS = ((3, (0, 2)), (3, (2, 4)), (2, (0, 2)), (2, (2, 4)), (1, (0, 4)), (0, (0, 4)))
RS = 10
FEAT, MID = 1792, 1280


def block_kernel(
    tokens, cotangent, seg_row, gain_h, shift_h, b_qkv, b_out_h, b_up_h, b_down_h,
    w_qkv_h, w_out_h, w_up_h, w_down_h,
    pieces, output, input_grad, sums,
    w_in, w_mid, w_sem,
    gain, shift, b_sum,
    normed_t, pre, grad_mid, rows, turned, mid, heads_t, outs_gt, grad_feat,
    cos_t, sin_t, seg_c, seg_r, lse, out_f, q_m, g_m, ds_b, q_2, g_2, mean_row, rstd,
    *scratch,
):
    at = neighbours()
    bias, p_b = grad_feat.at[:, pl.ds(1024, 256)], grad_feat.at[:, pl.ds(1280, 512)]
    s_f, d_f, grad_n = (grad_mid.at[:, pl.ds(a, n)] for a, n in ((0, 512), (512, 512), (1024, 256)))
    act_t = grad_feat
    n1, n2, n3 = len(GradSum.scratch()), len(Gather.scratch()), len(RowSum.scratch())
    small = SmallSum(scratch[n1 + n2 + n3:])

    def unit(cols):
        return (tokens[:, cols].astype(F32) - mean_row[:, 0:1]) * rstd[:, 0:1]

    def own_chunk(c):
        cols = at_rows(c % 8)
        normed = (unit(cols) * gain[0:1, cols] + shift[0:1, cols]).astype(BF)
        return jnp.where(c < 8, normed, cotangent[:, cols])

    grads = GradSum(at, pieces, scratch[:n1])
    gather = Gather(at, own_chunk, scratch[n1:n1 + n2])

    def keep_rows(c, value):
        branch = (c < 4) | (c >= 12)

        @pl.when(branch)
        def _():
            cols = at_rows(jnp.where(c < 4, c, c - 8))
            own = tokens[:, cols].astype(F32) + value + b_sum[0:1, cols]
            output[:, cols] = own.astype(BF)

        @pl.when(jnp.logical_not(branch))
        def _():
            grad_n[at_rows(c - 4, 128), :] = value

    row_sum = RowSum(at, scratch[n1 + n2:n1 + n2 + n3], keep_rows)

    moves = [(w_up_h, w_in.at[:, pl.ds(0, 1024)])]
    moves += [(w_qkv_h.at[k], w_in.at[:, pl.ds(1024 + 256 * k, 256)]) for k in range(3)]
    moves += [(w_down_h, w_mid.at[pl.ds(0, 1024)]), (w_out_h, w_mid.at[pl.ds(1024, 256)])]
    weights = [pltpu.make_async_copy(src, dst, w_sem.at[i]) for i, (src, dst) in enumerate(moves)]

    barrier = pltpu.get_barrier_semaphore()
    greeted = small.devices()
    for device in greeted:
        pl.semaphore_signal(barrier, inc=1, device_id=device, device_id_type=MESH)
    for copy in weights:
        copy.start()

    gain[...] = gain_h[...].astype(F32).reshape(1, 2048)
    shift[...] = shift_h[...].astype(F32).reshape(1, 2048)
    b_sum[...] = (b_out_h[...].astype(F32) + b_down_h[...].astype(F32)).reshape(1, 2048)
    x = tokens[...].astype(F32)
    mean = jnp.mean(x, axis=1, keepdims=True)
    centered = x - mean
    scale = lax.rsqrt(jnp.mean(centered * centered, axis=1, keepdims=True) + EPSILON)
    rstd[...] = jnp.broadcast_to(scale, (128, 128))
    mean_row[...] = jnp.broadcast_to(mean, (128, 128))

    pl.semaphore_wait(barrier, len(greeted))
    for c in range(Gather.AHEAD):
        gather.begin(c)

    seg_f = seg_row[...].astype(F32)
    seg_r[...] = jnp.broadcast_to(seg_f, (8, 1024))
    seg_c[...] = jnp.broadcast_to(seg_f, (128, 1024)).T
    @pl.loop(0, 4)
    def _(b):
        r = at_rows(b)
        i = lax.broadcasted_iota(jnp.int32, (256, 1024), 0) + b * 256
        j = lax.broadcasted_iota(jnp.int32, (256, 1024), 1)
        same = jnp.where((seg_c[r, 0:1] == seg_r[0:1, :]) & (j < i), 1.0, 0.0)
        position = jnp.sum(same, axis=1, keepdims=True)
        lane = lax.broadcasted_iota(jnp.int32, (256, 128), 1) % 64
        power = jnp.exp((lane % 16).astype(F32) * (-2.0 / ROT * 9.210340371976184))
        angle = position * power
        sine = jnp.sin(angle)
        cos_t[r, :] = jnp.where(lane < ROT, jnp.cos(angle), 1.0)
        sin_t[r, :] = jnp.where(lane < ROT // 2, -sine, jnp.where(lane < ROT, sine, 0.0))
        pre[r, 0:1024] = jnp.broadcast_to(b_up_h[...].astype(F32).reshape(1, 1024), (256, 1024))
        for k in range(3):
            cols = slice(1024 + k * 256, 1280 + k * 256)
            pre[r, cols] = jnp.broadcast_to(b_qkv[k:k + 1, :].astype(F32), (256, 256))

    @pl.loop(0, 10)
    def _(i):
        gather.steps(i)

        @pl.when(i == 2)
        def _():
            for copy in weights[:4]:
                copy.wait()

        @pl.when(i >= 2)
        def _():
            c = i - 2

            @pl.loop(0, 2)
            def _(b):
                r = at_rows(b, 512)
                a = gather.all[c % 8, r, :]
                pre[r, :] += dot(a, w_in[at_rows(c), :])
            normed_t[at_rows(c), :] = gather.all[c % 8].T

    def gelu(b):
        r = at_rows(b)
        for k in range(4):
            cols = slice(k * 256, k * 256 + 256)
            u = pre[r, cols]
            a = (u * (0.5 * (1.0 + gelu_parts(u)))).astype(BF)
            mid[r, cols] = a
            act_t[cols, r] = a.T

    pl.loop(0, 2)(gelu)
    gather.steps(10)
    pl.loop(2, 4)(gelu)
    for copy in weights[4:]:
        copy.wait()

    def make_rows(b):
        r = at_rows(b)
        for k in range(3):
            for half in range(2):
                v = pre[r, 1024 + k * 256 + half * 128:1152 + k * 256 + half * 128]
                if k < 2:
                    v = turn(v, cos_t[r, :], sin_t[r, :])
                if k == 0:
                    v = v * HEAD_DIM ** -0.5
                v = v.astype(BF)
                cols = slice(half * 128, half * 128 + 128)
                if k > 0:
                    rows[k - 1, r, cols] = v
                turned[k, cols, r] = v.T

    def attend_bias(qb):
        cols = slice(qb * 256, qb * 256 + 256)
        for kb in range(qb + 1):
            r = slice(kb * 256, kb * 256 + 256)
            keep = seg_c[r, 0:1] == seg_r[0:1, cols]
            if kb == qb:
                i = lax.broadcasted_iota(jnp.int32, (256, 256), 0)
                j = lax.broadcasted_iota(jnp.int32, (256, 256), 1)
                keep = keep & (i <= j)
            bias[r, :] = jnp.where(keep, 0.0, -1e30).astype(BF)

    def head_rows(h, count=64):
        return pl.ds(pl.multiple_of(h * 64, 64), count)

    def two_heads(ref, source, pair, cols):
        ref[...] = jnp.zeros_like(ref)
        for k in range(2):
            hr = head_rows(pair * 2 + k)
            ref[hr, k * 256:k * 256 + 256] = source[hr, cols]

    def both(value):
        return jnp.concatenate([value, value], axis=1)

    def blocks(n):
        return [slice(b, b + 64) for b in range(0, n, 64)]

    def over_rows(op, value):
        return op(value.reshape(8, 8, 512), axis=0)

    def attend(qb, heads):
        cols = slice(qb * 256, qb * 256 + 256)
        n = (qb + 1) * 256
        if heads[0] == 0:
            attend_bias(qb)
        s_f = pre.at[:, pl.ds(1024, 512)]

        @pl.loop(heads[0] // 2, heads[1] // 2)
        def _(pair):
            two_heads(q_m, turned.at[0], pair, cols)
            s_f[0:n, :] = dot(rows[0, 0:n, :], q_m[...])
            most = jnp.full((8, 512), -jnp.inf, F32)
            for r in blocks(n):
                s = s_f[r, :] + both(bias[r, :].astype(F32))
                s_f[r, :] = s
                most = jnp.maximum(most, over_rows(jnp.max, s))
            most = jnp.max(most, axis=0, keepdims=True)
            total = jnp.zeros((8, 512), F32)
            for r in blocks(n):
                e = jnp.exp(s_f[r, :] - most)
                total = total + over_rows(jnp.sum, e)
                ds_b[r, :] = e.astype(BF)
            total = jnp.sum(total, axis=0, keepdims=True)
            share, log_total = 1.0 / total, most + jnp.log(total)
            out = dot(turned[2, head_rows(pair * 2, 128), 0:n], ds_b[0:n, :])
            for k in range(2):
                h, side = pair * 2 + k, slice(k * 256, k * 256 + 256)
                value = out[k * 64:k * 64 + 64, side] * share[:, side]
                out_f[head_rows(h), cols] = value
                heads_t[head_rows(h), cols] = value.astype(BF)
                lse[pl.ds(h, 1), cols] = log_total[:, side]

    def attend_back(qb, heads):
        cols = slice(qb * 256, qb * 256 + 256)
        n = (qb + 1) * 256
        if heads[0] == 0:
            attend_bias(qb)

        @pl.loop(heads[0] // 2, heads[1] // 2)
        def _(pair):
            pair_rows = head_rows(pair * 2, 128)
            two_heads(q_m, turned.at[0], pair, cols)
            two_heads(g_m, outs_gt, pair, cols)
            s_f[0:n, :] = dot(rows[0, 0:n, :], q_m[...])
            d_f[0:n, :] = dot(rows[1, 0:n, :], g_m[...])
            log_total = jnp.concatenate([lse[pl.ds(pair * 2 + k, 1), cols] for k in range(2)], axis=1)
            product = outs_gt[pair_rows, cols].astype(F32) * out_f[pair_rows, cols]
            delta = jnp.concatenate([jnp.sum(product[k * 64:k * 64 + 64], axis=0, keepdims=True)
                                     for k in range(2)], axis=1)
            for r in blocks(n):
                p = jnp.exp(s_f[r, :] + both(bias[r, :].astype(F32)) - log_total)
                p_b[r, :] = p.astype(BF)
                ds_b[r, :] = (p * (d_f[r, :] - delta)).astype(BF)
            q_2[...] = q_m[...].T
            g_2[...] = g_m[...].T
            grad_q = dot(turned[1, pair_rows, 0:n], ds_b[0:n, :])
            for k in range(2):
                pre[pl.ds(pl.multiple_of(qb * 256 + pair * 128 + k * 64, 64), 64), 1024:1280] = grad_q[
                    k * 64:k * 64 + 64, k * 256:k * 256 + 256]
            pre[0:n, 1536:1792] += dot(p_b[0:n, :], g_2[...])
            pre[0:n, 1280:1536] += dot(ds_b[0:n, :], q_2[...])

    @pl.loop(0, 8)
    def _(t):
        grads.steps(t)
        chunk = gather.all[t]
        grads.own[t % 2] = dot(act_t[:, 0:1024], chunk).astype(BF)
        grads.send_piece(t)
        gather.steps(11 + t)

        @pl.when(t == 0)
        def _():
            grad_mid[...] = jnp.zeros_like(grad_mid)

        @pl.loop(0, 2)
        def _(b):
            r = at_rows(b, 512)
            grad_mid[r, :] += dot_nt(gather.all[t, r, :], w_mid[:, at_rows(t)])

        @pl.when(t < 2)
        def _():
            make_rows(2 * t)
            make_rows(2 * t + 1)

        for i, (qb, heads) in enumerate(UNITS):
            pl.when(t == 2 + i)(lambda qb=qb, heads=heads: attend(qb, heads))

    def branch_chunk(t, c):
        row_sum.store(t - RS, dot(mid[...], w_mid[:, at_rows(c)]))
        row_sum.send_chunk(t - RS)

    def normed_chunk(t, c):
        row_sum.store(t - RS, dot_nt(grad_feat[...], w_in[at_rows(c), :]))
        row_sum.send_chunk(t - RS)

    def gelu_back(k):
        @pl.loop(0, 4)
        def _(b):
            r, cols = at_rows(b), at_rows(k)
            u = pre[r, cols]
            th = gelu_parts(u)
            slope = 0.5 * (1.0 + th) + 0.5 * u * (1.0 - th * th) * (
                0.7978845608028654 * (1.0 + 3 * 0.044715 * (u * u)))
            grad_feat[r, cols] = (slope * grad_mid[r, cols]).astype(BF)

    def feature_piece(t):
        @pl.when(t % 2 == 0)
        def _():
            value = dot(normed_t[...], grad_feat[:, at_rows((t - 10) // 2)])
            for k in range(2):
                grads.own[k] = value[k * 1024:k * 1024 + 1024].astype(BF)

        grads.send_piece(t)

    @pl.loop(0, 4)
    def _(b):
        r = at_rows(b)
        mid[r, 1024:1280] = heads_t[:, r].T
        outs_gt[:, r] = grad_mid[r, 1024:1280].astype(BF).T
        pre[r, 1024:1792] = jnp.zeros((256, 768), F32)

    @pl.loop(8, 10)
    def _(t):
        grads.steps(t)
        for j in range(4):
            r = slice(j * 256, j * 256 + 256)
            grads.own[t % 2, r, :] = dot(heads_t[...], gather.all[4 * (t - 8) + j]).astype(BF)
        grads.send_piece(t)

        @pl.when(t == 8)
        def _():
            for k in range(4):
                gelu_back(k)

        pl.when(t == 9)(lambda: attend_back(*UNITS[0]))

    @pl.loop(10, 14)
    def _(t):
        grads.steps(t)
        row_sum.steps(t - RS)
        feature_piece(t)
        branch_chunk(t, t - RS)
        for i, (qb, heads) in enumerate((UNITS[1], (2, (0, 4)), *UNITS[4:])):
            pl.when(t == 10 + i)(lambda qb=qb, heads=heads: attend_back(qb, heads))

    for b in range(4):
        r = slice(b * 256, b * 256 + 256)
        grad_q = pre[r, 1024:1280].T * HEAD_DIM ** -0.5
        for half in range(2):
            a = half * 128
            cosine, sine = cos_t[r, :], -sin_t[r, :]
            grad_feat[r, 1024 + a:1152 + a] = turn(grad_q[:, a:a + 128], cosine, sine).astype(BF)
            grad_feat[r, 1280 + a:1408 + a] = turn(pre[r, 1280 + a:1408 + a], cosine, sine).astype(BF)
        grad_feat[r, 1536:1792] = pre[r, 1536:1792].astype(BF)

    @pl.loop(14, 24)
    def _(t):
        grads.steps(t)
        row_sum.steps(t - RS)
        feature_piece(t)
        pl.when(t < 22)(lambda: normed_chunk(t, t - 14))
        pl.when(t >= 22)(lambda: branch_chunk(t, t - 18))

    def late_steps(t):
        grads.steps(t)
        row_sum.steps(t - RS)

    @pl.loop(24, 27)
    def _(t):
        late_steps(t)
        pl.when(t < 26)(lambda: branch_chunk(t, t - 18))

    def column_sum(value):
        return jnp.sum(value.astype(F32), axis=0, keepdims=True)

    mine = small.i1
    small.b1[mine] = jnp.zeros((8, 1024), F32)
    mean_plain = jnp.zeros((128, 1), F32)
    mean_unit = jnp.zeros((128, 1), F32)
    for c in range(8):
        cols = slice(c * 256, c * 256 + 256)
        row, lanes = c // 4, slice((c % 4) * 256, (c % 4) * 256 + 256)
        g = grad_n[c * 128:c * 128 + 128, :]
        n = unit(cols)
        scaled = g * gain[0:1, cols]
        mean_plain = mean_plain + jnp.sum(scaled, axis=1, keepdims=True)
        mean_unit = mean_unit + jnp.sum(scaled * n, axis=1, keepdims=True)
        small.b1[mine, row:row + 1, lanes] = column_sum(g * n)
        small.b1[mine, 2 + row:3 + row, lanes] = column_sum(g)
        small.b1[mine, 4 + row:5 + row, lanes] = column_sum(cotangent[:, cols])
    for k in range(7):
        row, lanes = 6 + k // 4, slice((k % 4) * 256, (k % 4) * 256 + 256)
        small.b1[mine, row:row + 1, lanes] = column_sum(grad_feat[:, k * 256:k * 256 + 256])
    small.start(0)
    late_steps(27)
    mean_plain = mean_plain / 2048.0
    mean_unit = mean_unit / 2048.0
    for c in range(8):
        cols = slice(c * 256, c * 256 + 256)
        inner = grad_n[c * 128:c * 128 + 128, :] * gain[0:1, cols] - mean_plain - unit(cols) * mean_unit
        input_grad[:, cols] = (cotangent[:, cols].astype(F32) + rstd[:, 0:1] * inner).astype(BF)

    late_steps(28)
    small.second()
    late_steps(29)
    late_steps(30)
    small.third()
    late_steps(31)
    late_steps(32)
    sums[...] = small.result()
    late_steps(33)


def run_block(tokens, segment, ln_gain, ln_bias, w_qkv, b_qkv, w_out, b_out, w_up, b_up, w_down,
              b_down, cotangent):
    vmem = pl.BlockSpec(memory_space=pltpu.VMEM)
    hbm = pl.BlockSpec(memory_space=pl.ANY)
    V = pltpu.VMEM
    scratch = [
        V((2048, FEAT), BF), V((MID, 2048), BF), pltpu.SemaphoreType.DMA((6,)),
        V((1, 2048), F32), V((1, 2048), F32), V((1, 2048), F32),
        V((2048, 1024), BF),
        V((1024, FEAT), F32), V((1024, MID), F32),
        V((2, 1024, 256), BF), V((3, 256, 1024), BF),
        V((1024, MID), BF), V((256, 1024), BF),
        V((256, 1024), BF),
        V((1024, FEAT), BF),
        V((1024, 128), F32), V((1024, 128), F32),
        V((1024, 128), F32), V((8, 1024), F32),
        V((8, 1024), F32),
        V((256, 1024), F32),
        V((256, 512), BF), V((256, 512), BF), V((1024, 512), BF),
        V((512, 256), BF), V((512, 256), BF),
        V((128, 128), F32), V((128, 128), F32),
    ] + GradSum.scratch() + Gather.scratch() + RowSum.scratch() + SmallSum.scratch()
    return pl.pallas_call(
        block_kernel,
        out_shape=(
            jax.ShapeDtypeStruct((NP, 1024, 256), BF),
            jax.ShapeDtypeStruct((128, 2048), BF),
            jax.ShapeDtypeStruct((128, 2048), BF),
            jax.ShapeDtypeStruct((8, 1024), F32),
        ),
        in_specs=[vmem] * 9 + [hbm] * 4,
        out_specs=(hbm, vmem, vmem, vmem),
        scratch_shapes=scratch,
        compiler_params=pltpu.CompilerParams(
            collective_id=0, has_side_effects=True, vmem_limit_bytes=VMEM_LIMIT),
        cost_estimate=pl.CostEstimate(flops=50 * 10**9, bytes_accessed=30 << 20, transcendentals=10**7),
    )(
        tokens, cotangent, segment.reshape(1, 1024), ln_gain, ln_bias, b_qkv, b_out, b_up, b_down,
        w_qkv.transpose(1, 0, 2), w_out, w_up, w_down,
    )


def widen_kernel(qkv_p, out_p, down_p, up_p, output, input_grad, sums,
                 down, out, up, qkv, output_o, input_grad_o, gain_o, shift_o, b_out_o, b_down_o, b_up_o, b_qkv_o):
    for c in range(8):
        cols = slice(c * 256, c * 256 + 256)
        down[:, cols] = down_p[c].astype(F32)
        out[:, cols] = out_p[c].astype(F32)
    for c in range(4):
        up[:, c * 256:c * 256 + 256] = up_p[c, 0].astype(F32)
    qkv[...] = qkv_p[...].astype(F32)
    output_o[...] = output[...]
    input_grad_o[...] = input_grad[...]

    @pl.when(pl.program_id(0) == 0)
    def _():
        gain_o[...] = sums[0:2, :].reshape(2048)
        shift_o[...] = sums[2:4, :].reshape(2048)
        b_out_o[...] = sums[4:6, :].reshape(2048)
        b_down_o[...] = sums[4:6, :].reshape(2048)
        b_up_o[...] = sums[6:7, :].reshape(1024)
        for c in range(3):
            b_qkv_o[c:c + 1, :] = sums[7:8, c * 256:c * 256 + 256]


def widen(pieces, output, input_grad, sums):
    def rows(count, width):
        return pl.BlockSpec((count, width), lambda i: (i, 0))

    def whole(*shape):
        return pl.BlockSpec(shape, lambda i: (0,) * len(shape))

    def shape(*dims, kind=F32):
        return jax.ShapeDtypeStruct(dims, kind)

    down, out, up, qkv, *rest = pl.pallas_call(
        widen_kernel,
        grid=(4,),
        out_shape=(
            shape(1024, 2048), shape(256, 2048), shape(2048, 1024), shape(6144, 256),
            shape(128, 2048, kind=BF), shape(128, 2048, kind=BF),
            shape(2048), shape(2048), shape(2048), shape(2048), shape(1024), shape(3, 256),
        ),
        in_specs=[
            rows(1536, 256),
            pl.BlockSpec((8, 64, 256), lambda i: (3, i, 0)),
            pl.BlockSpec((8, 256, 256), lambda i: (1, i, 0)),
            pl.BlockSpec((4, 1, 512, 256), lambda i: (2, i // 2, i % 2, 0)),
            rows(32, 2048), rows(32, 2048), whole(8, 1024),
        ],
        out_specs=(
            rows(256, 2048), rows(64, 2048), rows(512, 1024), rows(1536, 256),
            rows(32, 2048), rows(32, 2048),
            whole(2048), whole(2048), whole(2048), whole(2048), whole(1024), whole(3, 256),
        ),
        compiler_params=pltpu.CompilerParams(vmem_limit_bytes=VMEM_LIMIT),
    )(
        pieces.reshape(NP * 1024, 256), pieces.reshape(NP * 4, 256, 256), pieces,
        pieces.reshape(NP // 2, 2, 1024, 256), output, input_grad, sums,
    )
    return down, out, up, qkv.reshape(3, 2048, 256).transpose(1, 0, 2), rest


def on_device(*args):
    pieces, output, input_grad, sums = run_block(*args)
    down, out, up, qkv, rest = widen(pieces, output, input_grad, sums)
    output, input_grad, gain, shift, b_out, b_down, b_up, b_qkv = rest
    return output, input_grad, gain, shift, qkv, b_qkv, out, b_out, up, b_up, down, b_down


def solution(mesh):
    placed = (
        P(("dp", "tensor"), None),
        P("dp"),
        P(),
        P(),
        P(None, None, "tensor"),
        P(None, "tensor"),
        P("tensor", None),
        P(),
        P(None, "tensor"),
        P("tensor"),
        P("tensor", None),
        P(),
        P(("dp", "tensor"), None),
    )
    return jax.shard_map(
        on_device,
        mesh=mesh,
        in_specs=placed,
        out_specs=(
            P(("dp", "tensor"), None),
            P(("dp", "tensor"), None),
            P(),
            P(),
            P(None, None, "tensor"),
            P(None, "tensor"),
            P("tensor", None),
            P(),
            P(None, "tensor"),
            P("tensor"),
            P("tensor", None),
            P(),
        ),
        check_vma=False,
    )
```

```python
import jax
import jax.numpy as jnp
from jax import lax
from jax.experimental import pallas as pl
from jax.experimental.pallas import tpu as pltpu
from jax.sharding import PartitionSpec as P

HEAD_DIM = 64
ROT = 32
EPSILON = 1e-05
MESH = pl.DeviceIdType.MESH
BF = jnp.bfloat16
F32 = jnp.float32
NP = 24
VMEM_LIMIT = 64 << 20


def neighbours():
    dp = lax.axis_index("dp")
    tensor = lax.axis_index("tensor")
    y, zh, core = dp // 4, (dp // 2) % 2, dp % 2
    zl, x = tensor // 4, tensor % 4
    yl, yr, yo = (y + 3) % 4, (y + 1) % 4, (y + 2) % 4
    xl, xr, xo = (x + 3) % 4, (x + 1) % 4, (x + 2) % 4
    where = dict(y=y, core=core, zl=zl, x=x, yl=yl, yr=yr, yo=yo, xl=xl, xr=xr, xo=xo)
    where["dev_yl"] = (yl * 4 + zh * 2 + core, tensor)
    where["dev_yr"] = (yr * 4 + zh * 2 + core, tensor)
    where["dev_zh"] = (y * 4 + (1 - zh) * 2 + core, tensor)
    where["dev_core"] = (y * 4 + zh * 2 + 1 - core, tensor)
    where["dev_xl"] = (dp, zl * 4 + xl)
    where["dev_xr"] = (dp, zl * 4 + xr)
    where["dev_zl"] = (dp, (1 - zl) * 4 + x)
    return where


def greet(devices):
    barrier = pltpu.get_barrier_semaphore()
    for device in devices:
        pl.semaphore_signal(barrier, inc=1, device_id=device, device_id_type=MESH)
    pl.semaphore_wait(barrier, len(devices))


def rcopy(src, dst, send, recv, device):
    return pltpu.make_async_remote_copy(
        src_ref=src, dst_ref=dst, send_sem=send, recv_sem=recv, device_id=device, device_id_type=MESH
    )


def rows_at(index, size, count=None):
    return pl.ds(pl.multiple_of(index * size, size), size if count is None else count)


class GradSum:
    def scratch():
        return [
            pltpu.VMEM((2, 1024, 256), BF),
            pltpu.VMEM((2, 512, 256), BF),
            pltpu.VMEM((4, 512, 256), BF),
            pltpu.VMEM((4, 2, 64, 256), BF),
            pltpu.VMEM((6, 2, 128, 256), BF),
            pltpu.VMEM((2, 128, 256), BF),
            pltpu.VMEM((4, 128, 256), BF),
            pltpu.VMEM((3, 128, 256), BF),
            pltpu.SemaphoreType.DMA((11, 8)),
            pltpu.SemaphoreType.DMA((11, 8)),
            pltpu.SemaphoreType.DMA((8,)),
        ]

    def __init__(self, at, out, scratch):
        self.at, self.out = at, out
        (self.own, self.other, self.half, self.r1, self.r2, self.zs, self.zr, self.full,
         self.send, self.recv, self.local) = scratch

    def place(self, p):
        return jnp.where(p < 8, p + 8, jnp.where(p < 10, p - 2, jnp.where(p < 18, p + 6, p - 18)))

    def core_copy(self, p):
        s, at = p % 4, self.at
        return rcopy(self.own.at[p % 2, rows_at(1 - at["core"], 512)], self.other.at[p % 2],
                     self.send.at[0, p % 8], self.recv.at[0, p % 8], at["dev_core"])

    def first_copies(self, p):
        s, at = p % 4, self.at
        top = self.half.at[s, rows_at(at["yo"], 128, 64)]
        low = self.half.at[s, pl.ds(pl.multiple_of(at["yo"] * 128 + 64, 64), 64)]
        return (rcopy(top, self.r1.at[s, 0], self.send.at[1, p % 8], self.recv.at[1, p % 8], at["dev_yr"]),
                rcopy(low, self.r1.at[s, 1], self.send.at[2, p % 8], self.recv.at[2, p % 8], at["dev_yl"]))

    def second_copies(self, p):
        s, at = p % 4, self.at
        return (rcopy(self.half.at[s, rows_at(at["yr"], 128)], self.r2.at[p % 6, 0],
                      self.send.at[3, p % 8], self.recv.at[3, p % 8], at["dev_yr"]),
                rcopy(self.half.at[s, rows_at(at["yl"], 128)], self.r2.at[p % 6, 1],
                      self.send.at[4, p % 8], self.recv.at[4, p % 8], at["dev_yl"]))

    def z_copy(self, p):
        s = p % 4
        return rcopy(self.zs.at[p % 2], self.zr.at[s], self.send.at[5, p % 8], self.recv.at[5, p % 8],
                     self.at["dev_zh"])

    def back_first(self, p):
        s, at = p % 4, self.at
        mine = self.out.at[self.place(p), rows_at(at["core"] * 4 + at["y"], 128)]
        return (rcopy(self.full.at[p % 3], mine, self.send.at[6, p % 8], self.recv.at[6, p % 8], at["dev_yr"]),
                rcopy(self.full.at[p % 3], mine, self.send.at[7, p % 8], self.recv.at[7, p % 8], at["dev_yl"]),
                pltpu.make_async_copy(self.full.at[p % 3], mine, self.local.at[p % 8]))

    def back_second(self, p):
        s, at = p % 4, self.at
        top = self.out.at[self.place(p), rows_at(at["core"] * 4 + at["yl"], 128, 64)]
        low = self.out.at[self.place(p), pl.ds(pl.multiple_of((at["core"] * 4 + at["yr"]) * 128 + 64, 64), 64)]
        return (rcopy(top, top, self.send.at[9, p % 8], self.recv.at[9, p % 8], at["dev_yr"]),
                rcopy(low, low, self.send.at[10, p % 8], self.recv.at[10, p % 8], at["dev_yl"]))

    def back_core(self, p):
        s, at = p % 4, self.at
        mine = self.out.at[self.place(p), rows_at(at["core"], 512)]
        return rcopy(mine, mine, self.send.at[8, p % 8], self.recv.at[8, p % 8], at["dev_core"])

    def send_piece(self, p):
        self.core_copy(p).start()

    def add_core(self, p):
        s = p % 4
        self.core_copy(p).wait()

        @pl.loop(0, 4)
        def _(j):
            rows = rows_at(j, 128)
            mine = self.own[p % 2, pl.ds(pl.multiple_of(self.at["core"] * 512 + j * 128, 128), 128)]
            self.half[s, rows] = (mine.astype(F32) + self.other[p % 2, rows].astype(F32)).astype(BF)

        for copy in self.first_copies(p):
            copy.start()

    def add_first(self, p):
        s, at = p % 4, self.at
        for copy in self.first_copies(p):
            copy.wait()
        top = rows_at(at["yr"], 128, 64)
        low = pl.ds(pl.multiple_of(at["yl"] * 128 + 64, 64), 64)
        self.half[s, top] = (self.half[s, top].astype(F32) + self.r1[s, 0].astype(F32)).astype(BF)
        self.half[s, low] = (self.half[s, low].astype(F32) + self.r1[s, 1].astype(F32)).astype(BF)
        for copy in self.second_copies(p):
            copy.start()

    def add_second(self, p):
        s = p % 4
        for copy in self.second_copies(p):
            copy.wait()
        mine = self.half[s, rows_at(self.at["y"], 128)].astype(F32)
        self.zs[p % 2] = (mine + self.r2[p % 6, 0].astype(F32) + self.r2[p % 6, 1].astype(F32)).astype(BF)
        self.z_copy(p).start()

    def add_z(self, p):
        s = p % 4
        self.z_copy(p).wait()
        self.full[p % 3] = (self.zs[p % 2].astype(F32) + self.zr[s].astype(F32)).astype(BF)
        for copy in self.back_first(p):
            copy.start()

    def forward_y(self, p):
        for copy in self.back_first(p):
            copy.wait()
        for copy in self.back_second(p):
            copy.start()

    def forward_core(self, p):
        for copy in self.back_second(p):
            copy.wait()
        self.back_core(p).start()

    def finish(self, p):
        self.back_core(p).wait()

    def steps(self, t):
        for lag, step in ((1, self.add_core), (2, self.add_first), (4, self.add_second), (5, self.add_z),
                          (7, self.forward_y), (9, self.forward_core), (10, self.finish)):
            p = t - lag
            pl.when((p >= 0) & (p < NP))(lambda step=step, p=p: step(p))


def dot(a, b):
    return lax.dot_general(a, b, (((1,), (0,)), ((), ())), preferred_element_type=F32)


def dot_nt(a, b):
    return lax.dot_general(a, b, (((1,), (1,)), ((), ())), preferred_element_type=F32)


def at_rows(index, size=256):
    return pl.ds(pl.multiple_of(index * size, size), size)


class Gather:
    AHEAD = 2

    def scratch():
        return [
            pltpu.VMEM((8, 1024, 256), BF),
            pltpu.SemaphoreType.DMA((9, 8)),
            pltpu.SemaphoreType.DMA((9, 8)),
        ]

    def __init__(self, at, own, scratch):
        self.at, self.own = at, own
        self.all, self.send, self.recv = scratch

    def copy(self, kind, c, src, dst, device):
        s = c % 8
        return rcopy(src, dst, self.send.at[kind, s], self.recv.at[kind, s], self.at[device])

    def part(self, c, zl, x, begin=0, count=128):
        first = pl.multiple_of((zl * 4 + x) * 128 + begin, 64)
        return self.all.at[c % 8, pl.ds(first, count)]

    def same(self, kind, c, block, device):
        return self.copy(kind, c, block, block, device)

    def first(self, c, wide):
        at = self.at
        mine = self.part(c, at["zl"], at["x"])
        copies = [self.same(0, c, mine, "dev_xr"), self.same(1, c, mine, "dev_xl")]
        return copies if wide else copies + [self.same(2, c, mine, "dev_zl")]

    def ring(self, c):
        at = self.at
        return [self.same(3, c, self.part(c, at["zl"], at["xl"], 0, 64), "dev_xr"),
                self.same(4, c, self.part(c, at["zl"], at["xr"], 64, 64), "dev_xl")]

    def second(self, c, wide):
        at = self.at
        if wide:
            return [self.same(5, c, self.part(c, at["zl"], at["x"]), "dev_zl"),
                    self.same(6, c, self.part(c, at["zl"], at["xl"]), "dev_zl"),
                    self.same(7, c, self.part(c, at["zl"], at["xr"]), "dev_zl")]
        other = self.part(c, 1 - at["zl"], at["x"])
        return [self.same(5, c, other, "dev_xr"), self.same(6, c, other, "dev_xl")]

    def third(self, c, wide):
        at = self.at
        if wide:
            return [self.same(8, c, self.part(c, at["zl"], at["xo"]), "dev_zl")]
        return [self.same(7, c, self.part(c, 1 - at["zl"], at["xl"], 0, 64), "dev_xr"),
                self.same(8, c, self.part(c, 1 - at["zl"], at["xr"], 64, 64), "dev_xl")]

    def begin(self, c):
        def start(wide):
            for copy in self.first(c, wide):
                copy.start()

        self.part(c, self.at["zl"], self.at["x"])[...] = self.own(c)
        self.either(c, start)

    def either(self, c, step):
        wide = (c % 2 == 1) & (c < WIDE)
        pl.when((c >= 0) & (c < 16) & wide)(lambda: step(True))
        pl.when((c >= 0) & (c < 16) & jnp.logical_not(wide))(lambda: step(False))

    def steps(self, c):
        def second(wide):
            for copy in self.first(c, wide):
                copy.wait()
            for copy in self.ring(c) + self.second(c, wide):
                copy.start()

        def third(wide):
            for copy in self.ring(c - 1) if wide else self.ring(c - 1) + self.second(c - 1, wide):
                copy.wait()
            for copy in self.third(c - 1, wide):
                copy.start()

        def last(wide):
            for copy in self.second(c - 2, wide) + self.third(c - 2, wide) if wide else self.third(c - 2, wide):
                copy.wait()

        self.either(c, second)
        pl.when(c + self.AHEAD < 16)(lambda: self.begin(c + self.AHEAD))
        self.either(c - 1, third)
        self.either(c - 2, last)


class RowSum:
    def scratch():
        return [
            pltpu.VMEM((4, 2, 4, 128, 256), BF),
            pltpu.VMEM((6, 2, 2, 64, 256), BF),
            pltpu.VMEM((6, 2, 2, 128, 256), BF),
            pltpu.VMEM((2, 128, 256), BF),
            pltpu.VMEM((4, 128, 256), BF),
            pltpu.VMEM((2, 128, 256), F32),
            pltpu.SemaphoreType.DMA((5, 8)),
            pltpu.SemaphoreType.DMA((5, 8)),
        ]

    def __init__(self, at, scratch, result):
        self.at, self.result = at, result
        self.part, self.r1, self.r2, self.zs, self.zr, self.mine, self.send, self.recv = scratch

    def copy(self, kind, c, src, dst, device):
        s = c % 8
        return rcopy(src, dst, self.send.at[kind, s], self.recv.at[kind, s], device)

    def first(self, c):
        s, at = c % 4, self.at
        return [self.copy(0, c, self.part.at[s, :, at["xo"], pl.ds(0, 64)], self.r1.at[c % 6, 0], at["dev_xr"]),
                self.copy(1, c, self.part.at[s, :, at["xo"], pl.ds(64, 64)], self.r1.at[c % 6, 1], at["dev_xl"])]

    def second(self, c):
        s, at = c % 4, self.at
        return [self.copy(2, c, self.part.at[s, :, at["xr"]], self.r2.at[c % 6, 0], at["dev_xr"]),
                self.copy(3, c, self.part.at[s, :, at["xl"]], self.r2.at[c % 6, 1], at["dev_xl"])]

    def third(self, c):
        s = c % 4
        return [self.copy(4, c, self.zs.at[c % 2], self.zr.at[s], self.at["dev_zl"])]

    def store(self, c, value):
        for k in range(8):
            self.part[c % 4, k // 4, k % 4] = value[k * 128:(k + 1) * 128].astype(BF)

    def send_chunk(self, c):
        for copy in self.first(c):
            copy.start()

    def add_first(self, c):
        s, at = c % 4, self.at
        for copy in self.first(c):
            copy.wait()
        for z in range(2):
            top = self.part[s, z, at["xr"], 0:64].astype(F32) + self.r1[c % 6, 0, z].astype(F32)
            self.part[s, z, at["xr"], 0:64] = top.astype(BF)
            low = self.part[s, z, at["xl"], 64:128].astype(F32) + self.r1[c % 6, 1, z].astype(F32)
            self.part[s, z, at["xl"], 64:128] = low.astype(BF)
        for copy in self.second(c):
            copy.start()

    def add_second(self, c):
        s, at = c % 4, self.at
        for copy in self.second(c):
            copy.wait()

        def total(z):
            own = self.part[s, z, at["x"]].astype(F32)
            return own + self.r2[c % 6, 0, z].astype(F32) + self.r2[c % 6, 1, z].astype(F32)

        self.zs[c % 2] = total(1 - at["zl"]).astype(BF)
        for copy in self.third(c):
            copy.start()
        self.mine[c % 2] = total(at["zl"])

    def add_third(self, c):
        s = c % 4
        for copy in self.third(c):
            copy.wait()
        self.result(c, self.mine[c % 2] + self.zr[s].astype(F32))

    def steps(self, t):
        for lag, step in ((2, self.add_first), (4, self.add_second), (5, self.add_third)):
            c = t - lag
            pl.when((c >= 0) & (c < 16))(lambda step=step, c=c: step(c))


class SmallSum:
    def scratch():
        return [
            pltpu.VMEM((8, 8, 1024), F32),
            pltpu.VMEM((4, 8, 1024), F32),
            pltpu.VMEM((4, 8, 1024), F32),
            pltpu.SemaphoreType.DMA((13,)),
            pltpu.SemaphoreType.DMA((13,)),
        ]

    def __init__(self, scratch):
        self.b1, self.b2, self.b3, self.send, self.recv = scratch
        dp, tensor = lax.axis_index("dp"), lax.axis_index("tensor")
        y, self.zh, core = dp // 4, (dp // 2) % 2, dp % 2
        self.zl, self.x = tensor // 4, tensor % 4
        self.i1 = y * 2 + core
        self.i2 = self.zh * 2 + self.zl
        self.d1, self.d2, self.d3 = [], [], []
        for k in range(1, 8):
            j = (self.i1 + k) % 8
            self.d1.append(((j // 2) * 4 + self.zh * 2 + j % 2, tensor))
        for k in range(1, 4):
            j = (self.i2 + k) % 4
            self.d2.append((y * 4 + (j // 2) * 2 + core, (j % 2) * 4 + self.x))
            self.d3.append((dp, self.zl * 4 + (self.x + k) % 4))

    def devices(self):
        return self.d1 + self.d2 + self.d3

    def copies(self, stage):
        buf, mine, devices, base = ((self.b1, self.i1, self.d1, 0), (self.b2, self.i2, self.d2, 7),
                                    (self.b3, self.x, self.d3, 10))[stage]
        return [rcopy(buf.at[mine], buf.at[mine], self.send.at[base + k], self.recv.at[base + k], device)
                for k, device in enumerate(devices)]

    def start(self, stage):
        for copy in self.copies(stage):
            copy.start()

    def wait(self, stage):
        for copy in self.copies(stage):
            copy.wait()

    def second(self):
        self.wait(0)
        total = self.b1[0]
        for k in range(1, 8):
            total = total + self.b1[k]
        self.b2[self.i2] = total
        self.start(1)

    def third(self):
        self.wait(1)
        wide = self.b2[0] + self.b2[1] + self.b2[2] + self.b2[3]
        narrow = self.b2[self.zl] + self.b2[2 + self.zl]
        row = lax.broadcasted_iota(jnp.int32, (8, 1024), 0)
        self.b3[self.x] = jnp.where(row < 6, wide, narrow)
        self.start(2)

    def result(self):
        self.wait(2)
        wide = self.b3[0] + self.b3[1] + self.b3[2] + self.b3[3]
        row = lax.broadcasted_iota(jnp.int32, (8, 1024), 0)
        return jnp.where(row < 6, wide, self.b3[self.x])


def gelu_parts(u):
    inner = 0.7978845608028654 * (u + 0.044715 * (u * u * u))
    return jnp.tanh(inner)


def swap_pairs(v):
    lane = lax.broadcasted_iota(jnp.int32, v.shape, 1)
    return jnp.where(lane % 32 < 16, pltpu.roll(v, 112, 1), pltpu.roll(v, 16, 1))


def turn(v, cosine, sine):
    return v * cosine + swap_pairs(v) * sine


WIDE = 14
UNITS = ((3, (0, 2)), (3, (2, 4)), (2, (0, 2)), (2, (2, 4)), (1, (0, 4)), (0, (0, 4)))
RS = 10
FEAT, MID = 1792, 1280


def block_kernel(
    seg_row, gain_h, shift_h, b_qkv, b_out_h, b_up_h, b_down_h,
    tokens_h, cotangent_h, w_qkv_h, w_out_h, w_up_h, w_down_h,
    pieces, output_h, input_grad_h, sums,
    tokens, cotangent, output, input_grad, row_sem, w_in, w_mid, w_sem,
    gain, shift, b_sum,
    normed_t, pre, grad_mid, rows, turned, mid, heads_t, outs_gt, grad_feat,
    cos_t, sin_t, seg_c, seg_r, lse, out_f, q_m, g_m, ds_b, q_2, g_2, mean_row, rstd,
    *scratch,
):
    at = neighbours()
    bias, p_b = grad_feat.at[:, pl.ds(1024, 256)], grad_feat.at[:, pl.ds(1280, 512)]
    s_f, d_f, grad_n = (grad_mid.at[:, pl.ds(a, n)] for a, n in ((0, 512), (512, 512), (1024, 256)))
    act_t = grad_feat
    n1, n2, n3 = len(GradSum.scratch()), len(Gather.scratch()), len(RowSum.scratch())
    small = SmallSum(scratch[n1 + n2 + n3:])

    def unit(cols):
        return (tokens[:, cols].astype(F32) - mean_row[:, 0:1]) * rstd[:, 0:1]

    def own_chunk(c):
        cols = at_rows(c % 8)
        normed = (unit(cols) * gain[0:1, cols] + shift[0:1, cols]).astype(BF)
        return jnp.where(c < 8, normed, cotangent[:, cols])

    grads = GradSum(at, pieces, scratch[:n1])
    gather = Gather(at, own_chunk, scratch[n1:n1 + n2])

    def keep_rows(c, value):
        branch = (c < 4) | (c >= 12)

        @pl.when(branch)
        def _():
            cols = at_rows(jnp.where(c < 4, c, c - 8))
            own = tokens[:, cols].astype(F32) + value + b_sum[0:1, cols]
            output[:, cols] = own.astype(BF)

        @pl.when(jnp.logical_not(branch))
        def _():
            grad_n[at_rows(c - 4, 128), :] = value

    row_sum = RowSum(at, scratch[n1 + n2:n1 + n2 + n3], keep_rows)

    moves = [(w_up_h, w_in.at[:, pl.ds(0, 1024)])]
    moves += [(w_qkv_h.at[k], w_in.at[:, pl.ds(1024 + 256 * k, 256)]) for k in range(3)]
    moves += [(w_down_h, w_mid.at[pl.ds(0, 1024)]), (w_out_h, w_mid.at[pl.ds(1024, 256)])]
    weights = [pltpu.make_async_copy(src, dst, w_sem.at[i]) for i, (src, dst) in enumerate(moves)]

    rows_in = [pltpu.make_async_copy(tokens_h, tokens, row_sem.at[0]),
               pltpu.make_async_copy(cotangent_h, cotangent, row_sem.at[1])]
    rows_out = [pltpu.make_async_copy(output, output_h, row_sem.at[2]),
                pltpu.make_async_copy(input_grad, input_grad_h, row_sem.at[3])]
    for copy in rows_in:
        copy.start()

    barrier = pltpu.get_barrier_semaphore()
    greeted = small.devices()
    for device in greeted:
        pl.semaphore_signal(barrier, inc=1, device_id=device, device_id_type=MESH)
    for copy in weights:
        copy.start()

    gain[...] = gain_h[...].astype(F32).reshape(1, 2048)
    shift[...] = shift_h[...].astype(F32).reshape(1, 2048)
    b_sum[...] = (b_out_h[...].astype(F32) + b_down_h[...].astype(F32)).reshape(1, 2048)
    rows_in[0].wait()
    x = tokens[...].astype(F32)
    mean = jnp.mean(x, axis=1, keepdims=True)
    centered = x - mean
    scale = lax.rsqrt(jnp.mean(centered * centered, axis=1, keepdims=True) + EPSILON)
    rstd[...] = jnp.broadcast_to(scale, (128, 128))
    mean_row[...] = jnp.broadcast_to(mean, (128, 128))

    rows_in[1].wait()
    pl.semaphore_wait(barrier, len(greeted))
    for c in range(Gather.AHEAD):
        gather.begin(c)

    seg_f = seg_row[...].astype(F32)
    seg_r[...] = jnp.broadcast_to(seg_f, (8, 1024))
    seg_c[...] = jnp.broadcast_to(seg_f, (128, 1024)).T
    @pl.loop(0, 4)
    def _(b):
        r = at_rows(b)
        i = lax.broadcasted_iota(jnp.int32, (256, 1024), 0) + b * 256
        j = lax.broadcasted_iota(jnp.int32, (256, 1024), 1)
        same = jnp.where((seg_c[r, 0:1] == seg_r[0:1, :]) & (j < i), 1.0, 0.0)
        position = jnp.sum(same, axis=1, keepdims=True)
        lane = lax.broadcasted_iota(jnp.int32, (256, 128), 1) % 64
        power = jnp.exp((lane % 16).astype(F32) * (-2.0 / ROT * 9.210340371976184))
        angle = position * power
        sine = jnp.sin(angle)
        cos_t[r, :] = jnp.where(lane < ROT, jnp.cos(angle), 1.0)
        sin_t[r, :] = jnp.where(lane < ROT // 2, -sine, jnp.where(lane < ROT, sine, 0.0))
        grad_mid[r, :] = jnp.zeros((256, MID), F32)
        pre[r, 0:1024] = jnp.broadcast_to(b_up_h[...].astype(F32).reshape(1, 1024), (256, 1024))
        for k in range(3):
            cols = slice(1024 + k * 256, 1280 + k * 256)
            pre[r, cols] = jnp.broadcast_to(b_qkv[k:k + 1, :].astype(F32), (256, 256))

    @pl.loop(0, 10)
    def _(i):
        gather.steps(i)

        @pl.when(i == 2)
        def _():
            for copy in weights[:4]:
                copy.wait()

        @pl.when(i >= 2)
        def _():
            c = i - 2

            @pl.loop(0, 2)
            def _(b):
                r = at_rows(b, 512)
                a = gather.all[c % 8, r, :]
                pre[r, :] += dot(a, w_in[at_rows(c), :])
            normed_t[at_rows(c), :] = gather.all[c % 8].T

    def gelu(b):
        r = at_rows(b)
        for k in range(4):
            cols = slice(k * 256, k * 256 + 256)
            u = pre[r, cols]
            a = (u * (0.5 * (1.0 + gelu_parts(u)))).astype(BF)
            mid[r, cols] = a
            act_t[cols, r] = a.T

    pl.loop(0, 2)(gelu)
    gather.steps(10)
    pl.loop(2, 4)(gelu)
    for copy in weights[4:]:
        copy.wait()

    def make_rows(b):
        r = at_rows(b)
        for k in range(3):
            for half in range(2):
                v = pre[r, 1024 + k * 256 + half * 128:1152 + k * 256 + half * 128]
                if k < 2:
                    v = turn(v, cos_t[r, :], sin_t[r, :])
                if k == 0:
                    v = v * HEAD_DIM ** -0.5
                v = v.astype(BF)
                cols = slice(half * 128, half * 128 + 128)
                if k > 0:
                    rows[k - 1, r, cols] = v
                turned[k, cols, r] = v.T

    def attend_bias(qb):
        cols = slice(qb * 256, qb * 256 + 256)
        for kb in range(qb + 1):
            r = slice(kb * 256, kb * 256 + 256)
            keep = seg_c[r, 0:1] == seg_r[0:1, cols]
            if kb == qb:
                i = lax.broadcasted_iota(jnp.int32, (256, 256), 0)
                j = lax.broadcasted_iota(jnp.int32, (256, 256), 1)
                keep = keep & (i <= j)
            bias[r, :] = jnp.where(keep, 0.0, -1e30).astype(BF)

    def head_rows(h, count=64):
        return pl.ds(pl.multiple_of(h * 64, 64), count)

    def two_heads(ref, source, pair, cols):
        ref[...] = jnp.zeros_like(ref)
        for k in range(2):
            hr = head_rows(pair * 2 + k)
            ref[hr, k * 256:k * 256 + 256] = source[hr, cols]

    def both(value):
        return jnp.concatenate([value, value], axis=1)

    def blocks(n):
        return [slice(b, b + 64) for b in range(0, n, 64)]

    def over_rows(op, value):
        return op(value.reshape(8, 8, 512), axis=0)

    def attend(qb, heads):
        cols = slice(qb * 256, qb * 256 + 256)
        n = (qb + 1) * 256
        if heads[0] == 0:
            attend_bias(qb)
        s_f = pre.at[:, pl.ds(1024, 512)]

        @pl.loop(heads[0] // 2, heads[1] // 2)
        def _(pair):
            two_heads(q_m, turned.at[0], pair, cols)
            s_f[0:n, :] = dot(rows[0, 0:n, :], q_m[...])
            most = jnp.full((8, 512), -jnp.inf, F32)
            for r in blocks(n):
                s = s_f[r, :] + both(bias[r, :].astype(F32))
                s_f[r, :] = s
                most = jnp.maximum(most, over_rows(jnp.max, s))
            most = jnp.max(most, axis=0, keepdims=True)
            total = jnp.zeros((8, 512), F32)
            for r in blocks(n):
                e = jnp.exp(s_f[r, :] - most)
                total = total + over_rows(jnp.sum, e)
                ds_b[r, :] = e.astype(BF)
            total = jnp.sum(total, axis=0, keepdims=True)
            share, log_total = 1.0 / total, most + jnp.log(total)
            out = dot(turned[2, head_rows(pair * 2, 128), 0:n], ds_b[0:n, :])
            for k in range(2):
                h, side = pair * 2 + k, slice(k * 256, k * 256 + 256)
                value = out[k * 64:k * 64 + 64, side] * share[:, side]
                out_f[head_rows(h), cols] = value
                heads_t[head_rows(h), cols] = value.astype(BF)
                lse[pl.ds(h, 1), cols] = log_total[:, side]

    def attend_back(qb, heads):
        cols = slice(qb * 256, qb * 256 + 256)
        n = (qb + 1) * 256
        if heads[0] == 0:
            attend_bias(qb)

        @pl.loop(heads[0] // 2, heads[1] // 2)
        def _(pair):
            pair_rows = head_rows(pair * 2, 128)
            two_heads(q_m, turned.at[0], pair, cols)
            two_heads(g_m, outs_gt, pair, cols)
            s_f[0:n, :] = dot(rows[0, 0:n, :], q_m[...])
            d_f[0:n, :] = dot(rows[1, 0:n, :], g_m[...])
            log_total = jnp.concatenate([lse[pl.ds(pair * 2 + k, 1), cols] for k in range(2)], axis=1)
            product = outs_gt[pair_rows, cols].astype(F32) * out_f[pair_rows, cols]
            delta = jnp.concatenate([jnp.sum(product[k * 64:k * 64 + 64], axis=0, keepdims=True)
                                     for k in range(2)], axis=1)
            for r in blocks(n):
                p = jnp.exp(s_f[r, :] + both(bias[r, :].astype(F32)) - log_total)
                p_b[r, :] = p.astype(BF)
                ds_b[r, :] = (p * (d_f[r, :] - delta)).astype(BF)
            q_2[...] = q_m[...].T
            g_2[...] = g_m[...].T
            grad_q = dot(turned[1, pair_rows, 0:n], ds_b[0:n, :])
            for k in range(2):
                pre[pl.ds(pl.multiple_of(qb * 256 + pair * 128 + k * 64, 64), 64), 1024:1280] = grad_q[
                    k * 64:k * 64 + 64, k * 256:k * 256 + 256]
            pre[0:n, 1536:1792] += dot(p_b[0:n, :], g_2[...])
            pre[0:n, 1280:1536] += dot(ds_b[0:n, :], q_2[...])

    @pl.loop(0, 8)
    def _(t):
        grads.steps(t)
        chunk = gather.all[t]
        grads.own[t % 2] = dot(act_t[:, 0:1024], chunk).astype(BF)
        grads.send_piece(t)
        gather.steps(11 + t)

        @pl.loop(0, 2)
        def _(b):
            r = at_rows(b, 512)
            grad_mid[r, :] += dot_nt(gather.all[t, r, :], w_mid[:, at_rows(t)])

        @pl.when(t < 2)
        def _():
            make_rows(2 * t)
            make_rows(2 * t + 1)

        for i, (qb, heads) in enumerate(UNITS):
            pl.when(t == 2 + i)(lambda qb=qb, heads=heads: attend(qb, heads))

    def branch_chunk(t, c):
        row_sum.store(t - RS, dot(mid[...], w_mid[:, at_rows(c)]))
        row_sum.send_chunk(t - RS)

    def normed_chunk(t, c):
        row_sum.store(t - RS, dot_nt(grad_feat[...], w_in[at_rows(c), :]))
        row_sum.send_chunk(t - RS)

    def gelu_back(k):
        @pl.loop(0, 4)
        def _(b):
            r, cols = at_rows(b), at_rows(k)
            u = pre[r, cols]
            th = gelu_parts(u)
            slope = 0.5 * (1.0 + th) + 0.5 * u * (1.0 - th * th) * (
                0.7978845608028654 * (1.0 + 3 * 0.044715 * (u * u)))
            grad_feat[r, cols] = (slope * grad_mid[r, cols]).astype(BF)

    def feature_piece(t):
        @pl.when(t % 2 == 0)
        def _():
            value = dot(normed_t[...], grad_feat[:, at_rows((t - 10) // 2)])
            for k in range(2):
                grads.own[k] = value[k * 1024:k * 1024 + 1024].astype(BF)

        grads.send_piece(t)

    @pl.loop(0, 4)
    def _(b):
        r = at_rows(b)
        outs_gt[:, r] = grad_mid[r, 1024:1280].astype(BF).T
        pre[r, 1024:1792] = jnp.zeros((256, 768), F32)

    @pl.loop(8, 10)
    def _(t):
        grads.steps(t)
        for j in range(4):
            r = slice(j * 256, j * 256 + 256)
            grads.own[t % 2, r, :] = dot(heads_t[...], gather.all[4 * (t - 8) + j]).astype(BF)
        grads.send_piece(t)

        @pl.when(t == 8)
        def _():
            for k in range(4):
                gelu_back(k)

        @pl.when(t == 9)
        def _():
            attend_back(*UNITS[0])
            for b in range(4):
                r = slice(b * 256, b * 256 + 256)
                mid[r, 1024:1280] = heads_t[:, r].T


    @pl.loop(10, 14)
    def _(t):
        grads.steps(t)
        row_sum.steps(t - RS)
        feature_piece(t)
        branch_chunk(t, t - RS)
        for i, (qb, heads) in enumerate((UNITS[1], (2, (0, 4)), *UNITS[4:])):
            pl.when(t == 10 + i)(lambda qb=qb, heads=heads: attend_back(qb, heads))

    for b in range(4):
        r = slice(b * 256, b * 256 + 256)
        grad_q = pre[r, 1024:1280].T * HEAD_DIM ** -0.5
        for half in range(2):
            a = half * 128
            cosine, sine = cos_t[r, :], -sin_t[r, :]
            grad_feat[r, 1024 + a:1152 + a] = turn(grad_q[:, a:a + 128], cosine, sine).astype(BF)
            grad_feat[r, 1280 + a:1408 + a] = turn(pre[r, 1280 + a:1408 + a], cosine, sine).astype(BF)
        grad_feat[r, 1536:1792] = pre[r, 1536:1792].astype(BF)

    @pl.loop(14, 24)
    def _(t):
        grads.steps(t)
        row_sum.steps(t - RS)
        feature_piece(t)
        pl.when(t < 22)(lambda: normed_chunk(t, t - 14))
        pl.when(t >= 22)(lambda: branch_chunk(t, t - 18))

    def late_steps(t):
        grads.steps(t)
        row_sum.steps(t - RS)

    @pl.loop(24, 27)
    def _(t):
        late_steps(t)
        pl.when(t < 26)(lambda: branch_chunk(t, t - 18))

    def column_sum(value):
        return jnp.sum(value.astype(F32), axis=0, keepdims=True)

    mine = small.i1
    small.b1[mine] = jnp.zeros((8, 1024), F32)
    mean_plain = jnp.zeros((128, 1), F32)
    mean_unit = jnp.zeros((128, 1), F32)
    for c in range(8):
        cols = slice(c * 256, c * 256 + 256)
        row, lanes = c // 4, slice((c % 4) * 256, (c % 4) * 256 + 256)
        g = grad_n[c * 128:c * 128 + 128, :]
        n = unit(cols)
        scaled = g * gain[0:1, cols]
        mean_plain = mean_plain + jnp.sum(scaled, axis=1, keepdims=True)
        mean_unit = mean_unit + jnp.sum(scaled * n, axis=1, keepdims=True)
        small.b1[mine, row:row + 1, lanes] = column_sum(g * n)
        small.b1[mine, 2 + row:3 + row, lanes] = column_sum(g)
        small.b1[mine, 4 + row:5 + row, lanes] = column_sum(cotangent[:, cols])
    for k in range(7):
        row, lanes = 6 + k // 4, slice((k % 4) * 256, (k % 4) * 256 + 256)
        small.b1[mine, row:row + 1, lanes] = column_sum(grad_feat[:, k * 256:k * 256 + 256])
    small.start(0)
    late_steps(27)
    mean_plain = mean_plain / 2048.0
    mean_unit = mean_unit / 2048.0
    for c in range(8):
        cols = slice(c * 256, c * 256 + 256)
        inner = grad_n[c * 128:c * 128 + 128, :] * gain[0:1, cols] - mean_plain - unit(cols) * mean_unit
        input_grad[:, cols] = (cotangent[:, cols].astype(F32) + rstd[:, 0:1] * inner).astype(BF)

    rows_out[1].start()
    late_steps(28)
    small.second()
    late_steps(29)
    late_steps(30)
    rows_out[0].start()
    small.third()
    late_steps(31)
    late_steps(32)
    sums[...] = small.result()
    for copy in rows_out:
        copy.wait()
    late_steps(33)


def run_block(tokens, segment, ln_gain, ln_bias, w_qkv, b_qkv, w_out, b_out, w_up, b_up, w_down,
              b_down, cotangent):
    vmem = pl.BlockSpec(memory_space=pltpu.VMEM)
    hbm = pl.BlockSpec(memory_space=pl.ANY)
    V = pltpu.VMEM
    scratch = [
        V((128, 2048), BF), V((128, 2048), BF),
        V((128, 2048), BF), V((128, 2048), BF), pltpu.SemaphoreType.DMA((4,)),
        V((2048, FEAT), BF), V((MID, 2048), BF), pltpu.SemaphoreType.DMA((6,)),
        V((1, 2048), F32), V((1, 2048), F32), V((1, 2048), F32),
        V((2048, 1024), BF),
        V((1024, FEAT), F32), V((1024, MID), F32),
        V((2, 1024, 256), BF), V((3, 256, 1024), BF),
        V((1024, MID), BF), V((256, 1024), BF),
        V((256, 1024), BF),
        V((1024, FEAT), BF),
        V((1024, 128), F32), V((1024, 128), F32),
        V((1024, 128), F32), V((8, 1024), F32),
        V((8, 1024), F32),
        V((256, 1024), F32),
        V((256, 512), BF), V((256, 512), BF), V((1024, 512), BF),
        V((512, 256), BF), V((512, 256), BF),
        V((128, 128), F32), V((128, 128), F32),
    ] + GradSum.scratch() + Gather.scratch() + RowSum.scratch() + SmallSum.scratch()
    return pl.pallas_call(
        block_kernel,
        out_shape=(
            jax.ShapeDtypeStruct((NP, 1024, 256), BF),
            jax.ShapeDtypeStruct((128, 2048), BF),
            jax.ShapeDtypeStruct((128, 2048), BF),
            jax.ShapeDtypeStruct((8, 1024), F32),
        ),
        in_specs=[vmem] * 7 + [hbm] * 6,
        out_specs=(hbm, hbm, hbm, vmem),
        scratch_shapes=scratch,
        compiler_params=pltpu.CompilerParams(
            collective_id=0, has_side_effects=True, vmem_limit_bytes=VMEM_LIMIT),
        cost_estimate=pl.CostEstimate(flops=50 * 10**9, bytes_accessed=30 << 20, transcendentals=10**7),
    )(
        segment.reshape(1, 1024), ln_gain, ln_bias, b_qkv, b_out, b_up, b_down,
        tokens, cotangent, w_qkv.transpose(1, 0, 2), w_out, w_up, w_down,
    )


def widen_kernel(qkv_p, out_p, down_p, up_p, output, input_grad, sums,
                 down, out, up, qkv, output_o, input_grad_o, gain_o, shift_o, b_out_o, b_down_o, b_up_o, b_qkv_o):
    for c in range(8):
        cols = slice(c * 256, c * 256 + 256)
        down[:, cols] = down_p[c].astype(F32)
        out[:, cols] = out_p[c].astype(F32)
    for c in range(4):
        up[:, c * 256:c * 256 + 256] = up_p[c, 0].astype(F32)
    qkv[...] = qkv_p[...].astype(F32)
    output_o[...] = output[...]
    input_grad_o[...] = input_grad[...]

    @pl.when(pl.program_id(0) == 0)
    def _():
        gain_o[...] = sums[0:2, :].reshape(2048)
        shift_o[...] = sums[2:4, :].reshape(2048)
        b_out_o[...] = sums[4:6, :].reshape(2048)
        b_down_o[...] = sums[4:6, :].reshape(2048)
        b_up_o[...] = sums[6:7, :].reshape(1024)
        for c in range(3):
            b_qkv_o[c:c + 1, :] = sums[7:8, c * 256:c * 256 + 256]


def widen(pieces, output, input_grad, sums):
    def rows(count, width):
        return pl.BlockSpec((count, width), lambda i: (i, 0))

    def whole(*shape):
        return pl.BlockSpec(shape, lambda i: (0,) * len(shape))

    def shape(*dims, kind=F32):
        return jax.ShapeDtypeStruct(dims, kind)

    down, out, up, qkv, *rest = pl.pallas_call(
        widen_kernel,
        grid=(4,),
        out_shape=(
            shape(1024, 2048), shape(256, 2048), shape(2048, 1024), shape(6144, 256),
            shape(128, 2048, kind=BF), shape(128, 2048, kind=BF),
            shape(2048), shape(2048), shape(2048), shape(2048), shape(1024), shape(3, 256),
        ),
        in_specs=[
            rows(1536, 256),
            pl.BlockSpec((8, 64, 256), lambda i: (3, i, 0)),
            pl.BlockSpec((8, 256, 256), lambda i: (1, i, 0)),
            pl.BlockSpec((4, 1, 512, 256), lambda i: (2, i // 2, i % 2, 0)),
            rows(32, 2048), rows(32, 2048), whole(8, 1024),
        ],
        out_specs=(
            rows(256, 2048), rows(64, 2048), rows(512, 1024), rows(1536, 256),
            rows(32, 2048), rows(32, 2048),
            whole(2048), whole(2048), whole(2048), whole(2048), whole(1024), whole(3, 256),
        ),
        compiler_params=pltpu.CompilerParams(vmem_limit_bytes=VMEM_LIMIT),
    )(
        pieces.reshape(NP * 1024, 256), pieces.reshape(NP * 4, 256, 256), pieces,
        pieces.reshape(NP // 2, 2, 1024, 256), output, input_grad, sums,
    )
    return down, out, up, qkv.reshape(3, 2048, 256).transpose(1, 0, 2), rest


def on_device(*args):
    pieces, output, input_grad, sums = run_block(*args)
    down, out, up, qkv, rest = widen(pieces, output, input_grad, sums)
    output, input_grad, gain, shift, b_out, b_down, b_up, b_qkv = rest
    return output, input_grad, gain, shift, qkv, b_qkv, out, b_out, up, b_up, down, b_down


def solution(mesh):
    placed = (
        P(("dp", "tensor"), None),
        P("dp"),
        P(),
        P(),
        P(None, None, "tensor"),
        P(None, "tensor"),
        P("tensor", None),
        P(),
        P(None, "tensor"),
        P("tensor"),
        P("tensor", None),
        P(),
        P(("dp", "tensor"), None),
    )
    return jax.shard_map(
        on_device,
        mesh=mesh,
        in_specs=placed,
        out_specs=(
            P(("dp", "tensor"), None),
            P(("dp", "tensor"), None),
            P(),
            P(),
            P(None, None, "tensor"),
            P(None, "tensor"),
            P("tensor", None),
            P(),
            P(None, "tensor"),
            P("tensor"),
            P("tensor", None),
            P(),
        ),
        check_vma=False,
    )
```

```python
import jax
import jax.numpy as jnp
from jax import lax
from jax.experimental import pallas as pl
from jax.experimental.pallas import tpu as pltpu
from jax.sharding import PartitionSpec as P

HEAD_DIM = 64
ROT = 32
EPSILON = 1e-05
MESH = pl.DeviceIdType.MESH
BF = jnp.bfloat16
F32 = jnp.float32
NP = 24
VMEM_LIMIT = 64 << 20


def neighbours():
    dp = lax.axis_index("dp")
    tensor = lax.axis_index("tensor")
    y, zh, core = dp // 4, (dp // 2) % 2, dp % 2
    zl, x = tensor // 4, tensor % 4
    yl, yr, yo = (y + 3) % 4, (y + 1) % 4, (y + 2) % 4
    xl, xr, xo = (x + 3) % 4, (x + 1) % 4, (x + 2) % 4
    where = dict(y=y, core=core, zl=zl, x=x, yl=yl, yr=yr, yo=yo, xl=xl, xr=xr, xo=xo)
    where["dev_yl"] = (yl * 4 + zh * 2 + core, tensor)
    where["dev_yr"] = (yr * 4 + zh * 2 + core, tensor)
    where["dev_zh"] = (y * 4 + (1 - zh) * 2 + core, tensor)
    where["dev_core"] = (y * 4 + zh * 2 + 1 - core, tensor)
    where["dev_xl"] = (dp, zl * 4 + xl)
    where["dev_xr"] = (dp, zl * 4 + xr)
    where["dev_zl"] = (dp, (1 - zl) * 4 + x)
    return where


def greet(devices):
    barrier = pltpu.get_barrier_semaphore()
    for device in devices:
        pl.semaphore_signal(barrier, inc=1, device_id=device, device_id_type=MESH)
    pl.semaphore_wait(barrier, len(devices))


def rcopy(src, dst, send, recv, device):
    return pltpu.make_async_remote_copy(
        src_ref=src, dst_ref=dst, send_sem=send, recv_sem=recv, device_id=device, device_id_type=MESH
    )


def rows_at(index, size, count=None):
    return pl.ds(pl.multiple_of(index * size, size), size if count is None else count)


class GradSum:
    def scratch():
        return [
            pltpu.VMEM((2, 1024, 256), BF),
            pltpu.VMEM((2, 512, 256), BF),
            pltpu.VMEM((4, 512, 256), BF),
            pltpu.VMEM((4, 2, 64, 256), BF),
            pltpu.VMEM((6, 2, 128, 256), BF),
            pltpu.VMEM((2, 128, 256), BF),
            pltpu.VMEM((4, 128, 256), BF),
            pltpu.VMEM((3, 128, 256), BF),
            pltpu.SemaphoreType.DMA((11, 8)),
            pltpu.SemaphoreType.DMA((11, 8)),
            pltpu.SemaphoreType.DMA((8,)),
        ]

    def __init__(self, at, out, scratch):
        self.at, self.out = at, out
        (self.own, self.other, self.half, self.r1, self.r2, self.zs, self.zr, self.full,
         self.send, self.recv, self.local) = scratch

    def place(self, p):
        return jnp.where(p < 8, p + 8, jnp.where(p < 10, p - 2, jnp.where(p < 18, p + 6, p - 18)))

    def core_copy(self, p):
        s, at = p % 4, self.at
        return rcopy(self.own.at[p % 2, rows_at(1 - at["core"], 512)], self.other.at[p % 2],
                     self.send.at[0, p % 8], self.recv.at[0, p % 8], at["dev_core"])

    def first_copies(self, p):
        s, at = p % 4, self.at
        top = self.half.at[s, rows_at(at["yo"], 128, 64)]
        low = self.half.at[s, pl.ds(pl.multiple_of(at["yo"] * 128 + 64, 64), 64)]
        return (rcopy(top, self.r1.at[s, 0], self.send.at[1, p % 8], self.recv.at[1, p % 8], at["dev_yr"]),
                rcopy(low, self.r1.at[s, 1], self.send.at[2, p % 8], self.recv.at[2, p % 8], at["dev_yl"]))

    def second_copies(self, p):
        s, at = p % 4, self.at
        return (rcopy(self.half.at[s, rows_at(at["yr"], 128)], self.r2.at[p % 6, 0],
                      self.send.at[3, p % 8], self.recv.at[3, p % 8], at["dev_yr"]),
                rcopy(self.half.at[s, rows_at(at["yl"], 128)], self.r2.at[p % 6, 1],
                      self.send.at[4, p % 8], self.recv.at[4, p % 8], at["dev_yl"]))

    def z_copy(self, p):
        s = p % 4
        return rcopy(self.zs.at[p % 2], self.zr.at[s], self.send.at[5, p % 8], self.recv.at[5, p % 8],
                     self.at["dev_zh"])

    def back_first(self, p):
        s, at = p % 4, self.at
        mine = self.out.at[self.place(p), rows_at(at["core"] * 4 + at["y"], 128)]
        return (rcopy(self.full.at[p % 3], mine, self.send.at[6, p % 8], self.recv.at[6, p % 8], at["dev_yr"]),
                rcopy(self.full.at[p % 3], mine, self.send.at[7, p % 8], self.recv.at[7, p % 8], at["dev_yl"]),
                pltpu.make_async_copy(self.full.at[p % 3], mine, self.local.at[p % 8]))

    def back_second(self, p):
        s, at = p % 4, self.at
        top = self.out.at[self.place(p), rows_at(at["core"] * 4 + at["yl"], 128, 64)]
        low = self.out.at[self.place(p), pl.ds(pl.multiple_of((at["core"] * 4 + at["yr"]) * 128 + 64, 64), 64)]
        return (rcopy(top, top, self.send.at[9, p % 8], self.recv.at[9, p % 8], at["dev_yr"]),
                rcopy(low, low, self.send.at[10, p % 8], self.recv.at[10, p % 8], at["dev_yl"]))

    def back_core(self, p):
        s, at = p % 4, self.at
        mine = self.out.at[self.place(p), rows_at(at["core"], 512)]
        return rcopy(mine, mine, self.send.at[8, p % 8], self.recv.at[8, p % 8], at["dev_core"])

    def send_piece(self, p):
        self.core_copy(p).start()

    def add_core(self, p):
        s = p % 4
        self.core_copy(p).wait()

        @pl.loop(0, 4)
        def _(j):
            rows = rows_at(j, 128)
            mine = self.own[p % 2, pl.ds(pl.multiple_of(self.at["core"] * 512 + j * 128, 128), 128)]
            self.half[s, rows] = (mine.astype(F32) + self.other[p % 2, rows].astype(F32)).astype(BF)

        for copy in self.first_copies(p):
            copy.start()

    def add_first(self, p):
        s, at = p % 4, self.at
        for copy in self.first_copies(p):
            copy.wait()
        top = rows_at(at["yr"], 128, 64)
        low = pl.ds(pl.multiple_of(at["yl"] * 128 + 64, 64), 64)
        self.half[s, top] = (self.half[s, top].astype(F32) + self.r1[s, 0].astype(F32)).astype(BF)
        self.half[s, low] = (self.half[s, low].astype(F32) + self.r1[s, 1].astype(F32)).astype(BF)
        for copy in self.second_copies(p):
            copy.start()

    def add_second(self, p):
        s = p % 4
        for copy in self.second_copies(p):
            copy.wait()
        mine = self.half[s, rows_at(self.at["y"], 128)].astype(F32)
        self.zs[p % 2] = (mine + self.r2[p % 6, 0].astype(F32) + self.r2[p % 6, 1].astype(F32)).astype(BF)
        self.z_copy(p).start()

    def add_z(self, p):
        s = p % 4
        self.z_copy(p).wait()
        self.full[p % 3] = (self.zs[p % 2].astype(F32) + self.zr[s].astype(F32)).astype(BF)
        for copy in self.back_first(p):
            copy.start()

    def forward_y(self, p):
        for copy in self.back_first(p):
            copy.wait()
        for copy in self.back_second(p):
            copy.start()

    def forward_core(self, p):
        for copy in self.back_second(p):
            copy.wait()
        self.back_core(p).start()

    def finish(self, p):
        self.back_core(p).wait()

    def steps(self, t):
        for lag, step in ((1, self.add_core), (2, self.add_first), (4, self.add_second), (5, self.add_z),
                          (7, self.forward_y), (9, self.forward_core), (10, self.finish)):
            p = t - lag
            pl.when((p >= 0) & (p < NP))(lambda step=step, p=p: step(p))


def dot(a, b):
    return lax.dot_general(a, b, (((1,), (0,)), ((), ())), preferred_element_type=F32)


def dot_nt(a, b):
    return lax.dot_general(a, b, (((1,), (1,)), ((), ())), preferred_element_type=F32)


def at_rows(index, size=256):
    return pl.ds(pl.multiple_of(index * size, size), size)


class Gather:
    AHEAD = 2

    def scratch():
        return [
            pltpu.VMEM((8, 1024, 256), BF),
            pltpu.SemaphoreType.DMA((9, 8)),
            pltpu.SemaphoreType.DMA((9, 8)),
        ]

    def __init__(self, at, own, scratch):
        self.at, self.own = at, own
        self.all, self.send, self.recv = scratch

    def copy(self, kind, c, src, dst, device):
        s = c % 8
        return rcopy(src, dst, self.send.at[kind, s], self.recv.at[kind, s], self.at[device])

    def part(self, c, zl, x, begin=0, count=128):
        first = pl.multiple_of((zl * 4 + x) * 128 + begin, 64)
        return self.all.at[c % 8, pl.ds(first, count)]

    def same(self, kind, c, block, device):
        return self.copy(kind, c, block, block, device)

    def first(self, c, wide):
        at = self.at
        mine = self.part(c, at["zl"], at["x"])
        copies = [self.same(0, c, mine, "dev_xr"), self.same(1, c, mine, "dev_xl")]
        return copies if wide else copies + [self.same(2, c, mine, "dev_zl")]

    def ring(self, c):
        at = self.at
        return [self.same(3, c, self.part(c, at["zl"], at["xl"], 0, 64), "dev_xr"),
                self.same(4, c, self.part(c, at["zl"], at["xr"], 64, 64), "dev_xl")]

    def second(self, c, wide):
        at = self.at
        if wide:
            return [self.same(5, c, self.part(c, at["zl"], at["x"]), "dev_zl"),
                    self.same(6, c, self.part(c, at["zl"], at["xl"]), "dev_zl"),
                    self.same(7, c, self.part(c, at["zl"], at["xr"]), "dev_zl")]
        other = self.part(c, 1 - at["zl"], at["x"])
        return [self.same(5, c, other, "dev_xr"), self.same(6, c, other, "dev_xl")]

    def third(self, c, wide):
        at = self.at
        if wide:
            return [self.same(8, c, self.part(c, at["zl"], at["xo"]), "dev_zl")]
        return [self.same(7, c, self.part(c, 1 - at["zl"], at["xl"], 0, 64), "dev_xr"),
                self.same(8, c, self.part(c, 1 - at["zl"], at["xr"], 64, 64), "dev_xl")]

    def begin(self, c):
        def start(wide):
            for copy in self.first(c, wide):
                copy.start()

        self.part(c, self.at["zl"], self.at["x"])[...] = self.own(c)
        self.either(c, start)

    def either(self, c, step):
        wide = (c % 2 == 1) & (c < WIDE)
        pl.when((c >= 0) & (c < 16) & wide)(lambda: step(True))
        pl.when((c >= 0) & (c < 16) & jnp.logical_not(wide))(lambda: step(False))

    def steps(self, c):
        def second(wide):
            for copy in self.first(c, wide):
                copy.wait()
            for copy in self.ring(c) + self.second(c, wide):
                copy.start()

        def third(wide):
            for copy in self.ring(c - 1) if wide else self.ring(c - 1) + self.second(c - 1, wide):
                copy.wait()
            for copy in self.third(c - 1, wide):
                copy.start()

        def last(wide):
            for copy in self.second(c - 2, wide) + self.third(c - 2, wide) if wide else self.third(c - 2, wide):
                copy.wait()

        self.either(c, second)
        pl.when(c + self.AHEAD < 16)(lambda: self.begin(c + self.AHEAD))
        self.either(c - 1, third)
        self.either(c - 2, last)


class RowSum:
    def scratch():
        return [
            pltpu.VMEM((4, 2, 4, 128, 256), BF),
            pltpu.VMEM((6, 2, 2, 64, 256), BF),
            pltpu.VMEM((6, 2, 2, 128, 256), BF),
            pltpu.VMEM((2, 128, 256), BF),
            pltpu.VMEM((4, 128, 256), BF),
            pltpu.VMEM((2, 128, 256), F32),
            pltpu.SemaphoreType.DMA((5, 8)),
            pltpu.SemaphoreType.DMA((5, 8)),
        ]

    def __init__(self, at, scratch, result):
        self.at, self.result = at, result
        self.part, self.r1, self.r2, self.zs, self.zr, self.mine, self.send, self.recv = scratch

    def copy(self, kind, c, src, dst, device):
        s = c % 8
        return rcopy(src, dst, self.send.at[kind, s], self.recv.at[kind, s], device)

    def first(self, c):
        s, at = c % 4, self.at
        return [self.copy(0, c, self.part.at[s, :, at["xo"], pl.ds(0, 64)], self.r1.at[c % 6, 0], at["dev_xr"]),
                self.copy(1, c, self.part.at[s, :, at["xo"], pl.ds(64, 64)], self.r1.at[c % 6, 1], at["dev_xl"])]

    def second(self, c):
        s, at = c % 4, self.at
        return [self.copy(2, c, self.part.at[s, :, at["xr"]], self.r2.at[c % 6, 0], at["dev_xr"]),
                self.copy(3, c, self.part.at[s, :, at["xl"]], self.r2.at[c % 6, 1], at["dev_xl"])]

    def third(self, c):
        s = c % 4
        return [self.copy(4, c, self.zs.at[c % 2], self.zr.at[s], self.at["dev_zl"])]

    def store(self, c, value):
        for k in range(8):
            self.part[c % 4, k // 4, k % 4] = value[k * 128:(k + 1) * 128].astype(BF)

    def send_chunk(self, c):
        for copy in self.first(c):
            copy.start()

    def add_first(self, c):
        s, at = c % 4, self.at
        for copy in self.first(c):
            copy.wait()
        for z in range(2):
            top = self.part[s, z, at["xr"], 0:64].astype(F32) + self.r1[c % 6, 0, z].astype(F32)
            self.part[s, z, at["xr"], 0:64] = top.astype(BF)
            low = self.part[s, z, at["xl"], 64:128].astype(F32) + self.r1[c % 6, 1, z].astype(F32)
            self.part[s, z, at["xl"], 64:128] = low.astype(BF)
        for copy in self.second(c):
            copy.start()

    def add_second(self, c):
        s, at = c % 4, self.at
        for copy in self.second(c):
            copy.wait()

        def total(z):
            own = self.part[s, z, at["x"]].astype(F32)
            return own + self.r2[c % 6, 0, z].astype(F32) + self.r2[c % 6, 1, z].astype(F32)

        self.zs[c % 2] = total(1 - at["zl"]).astype(BF)
        for copy in self.third(c):
            copy.start()
        self.mine[c % 2] = total(at["zl"])

    def add_third(self, c):
        s = c % 4
        for copy in self.third(c):
            copy.wait()
        self.result(c, self.mine[c % 2] + self.zr[s].astype(F32))

    def steps(self, t):
        for lag, step in ((2, self.add_first), (4, self.add_second), (5, self.add_third)):
            c = t - lag
            pl.when((c >= 0) & (c < 16))(lambda step=step, c=c: step(c))


class SmallSum:
    def scratch():
        return [
            pltpu.VMEM((8, 8, 1024), F32),
            pltpu.VMEM((4, 8, 1024), F32),
            pltpu.VMEM((4, 8, 1024), F32),
            pltpu.SemaphoreType.DMA((13,)),
            pltpu.SemaphoreType.DMA((13,)),
        ]

    def __init__(self, scratch):
        self.b1, self.b2, self.b3, self.send, self.recv = scratch
        dp, tensor = lax.axis_index("dp"), lax.axis_index("tensor")
        y, self.zh, core = dp // 4, (dp // 2) % 2, dp % 2
        self.zl, self.x = tensor // 4, tensor % 4
        self.i1 = y * 2 + core
        self.i2 = self.zh * 2 + self.zl
        self.d1, self.d2, self.d3 = [], [], []
        for k in range(1, 8):
            j = (self.i1 + k) % 8
            self.d1.append(((j // 2) * 4 + self.zh * 2 + j % 2, tensor))
        for k in range(1, 4):
            j = (self.i2 + k) % 4
            self.d2.append((y * 4 + (j // 2) * 2 + core, (j % 2) * 4 + self.x))
            self.d3.append((dp, self.zl * 4 + (self.x + k) % 4))

    def devices(self):
        return self.d1 + self.d2 + self.d3

    def copies(self, stage):
        buf, mine, devices, base = ((self.b1, self.i1, self.d1, 0), (self.b2, self.i2, self.d2, 7),
                                    (self.b3, self.x, self.d3, 10))[stage]
        return [rcopy(buf.at[mine], buf.at[mine], self.send.at[base + k], self.recv.at[base + k], device)
                for k, device in enumerate(devices)]

    def start(self, stage):
        for copy in self.copies(stage):
            copy.start()

    def wait(self, stage):
        for copy in self.copies(stage):
            copy.wait()

    def second(self):
        self.wait(0)
        total = self.b1[0]
        for k in range(1, 8):
            total = total + self.b1[k]
        self.b2[self.i2] = total
        self.start(1)

    def third(self):
        self.wait(1)
        wide = self.b2[0] + self.b2[1] + self.b2[2] + self.b2[3]
        narrow = self.b2[self.zl] + self.b2[2 + self.zl]
        row = lax.broadcasted_iota(jnp.int32, (8, 1024), 0)
        self.b3[self.x] = jnp.where(row < 6, wide, narrow)
        self.start(2)

    def result(self):
        self.wait(2)
        wide = self.b3[0] + self.b3[1] + self.b3[2] + self.b3[3]
        row = lax.broadcasted_iota(jnp.int32, (8, 1024), 0)
        return jnp.where(row < 6, wide, self.b3[self.x])


def gelu_parts(u):
    inner = 0.7978845608028654 * (u + 0.044715 * (u * u * u))
    return jnp.tanh(inner)


def swap_pairs(v):
    lane = lax.broadcasted_iota(jnp.int32, v.shape, 1)
    return jnp.where(lane % 32 < 16, pltpu.roll(v, 112, 1), pltpu.roll(v, 16, 1))


def turn(v, cosine, sine):
    return v * cosine + swap_pairs(v) * sine


WIDE = 14
UNITS = ((3, (0, 2)), (3, (2, 4)), (2, (0, 2)), (2, (2, 4)), (1, (0, 4)), (0, (0, 4)))
RS = 10
FEAT, MID = 1792, 1280


def block_kernel(
    seg_row, gain_h, shift_h, b_qkv, b_out_h, b_up_h, b_down_h,
    tokens_h, cotangent_h, w_qkv_h, w_out_h, w_up_h, w_down_h,
    pieces, output_h, input_grad_h, sums,
    tokens, cotangent, output, input_grad, row_sem, w_in, w_mid, w_sem,
    gain, shift, b_sum,
    normed_t, pre, grad_mid, rows, turned, mid, heads_t, outs_gt, grad_feat,
    cos_t, sin_t, seg_c, seg_r, lse, out_f, q_m, g_m, ds_b, q_2, g_2, mean_row, rstd,
    *scratch,
):
    at = neighbours()
    bias, p_b = grad_feat.at[:, pl.ds(1024, 256)], grad_feat.at[:, pl.ds(1280, 512)]
    s_f, d_f, grad_n = (grad_mid.at[:, pl.ds(a, n)] for a, n in ((0, 512), (512, 512), (1024, 256)))
    act_t = grad_feat
    n1, n2, n3 = len(GradSum.scratch()), len(Gather.scratch()), len(RowSum.scratch())
    small = SmallSum(scratch[n1 + n2 + n3:])

    def unit(cols):
        return (tokens[:, cols].astype(F32) - mean_row[:, 0:1]) * rstd[:, 0:1]

    def own_chunk(c):
        cols = at_rows(c % 8)
        normed = (unit(cols) * gain[0:1, cols] + shift[0:1, cols]).astype(BF)
        return jnp.where(c < 8, normed, cotangent[:, cols])

    grads = GradSum(at, pieces, scratch[:n1])
    gather = Gather(at, own_chunk, scratch[n1:n1 + n2])

    def keep_rows(c, value):
        branch = (c < 4) | (c >= 12)

        @pl.when(branch)
        def _():
            cols = at_rows(jnp.where(c < 4, c, c - 8))
            own = tokens[:, cols].astype(F32) + value + b_sum[0:1, cols]
            output[:, cols] = own.astype(BF)

        @pl.when(jnp.logical_not(branch))
        def _():
            grad_n[at_rows(c - 4, 128), :] = value

    row_sum = RowSum(at, scratch[n1 + n2:n1 + n2 + n3], keep_rows)

    moves = [(w_up_h, w_in.at[:, pl.ds(0, 1024)])]
    moves += [(w_qkv_h.at[k], w_in.at[:, pl.ds(1024 + 256 * k, 256)]) for k in range(3)]
    moves += [(w_down_h, w_mid.at[pl.ds(0, 1024)]), (w_out_h, w_mid.at[pl.ds(1024, 256)])]
    weights = [pltpu.make_async_copy(src, dst, w_sem.at[i]) for i, (src, dst) in enumerate(moves)]

    rows_in = [pltpu.make_async_copy(tokens_h, tokens, row_sem.at[0]),
               pltpu.make_async_copy(cotangent_h, cotangent, row_sem.at[1])]
    rows_out = [pltpu.make_async_copy(output, output_h, row_sem.at[2]),
                pltpu.make_async_copy(input_grad, input_grad_h, row_sem.at[3])]
    for copy in rows_in:
        copy.start()

    barrier = pltpu.get_barrier_semaphore()
    greeted = small.devices()
    for device in greeted:
        pl.semaphore_signal(barrier, inc=1, device_id=device, device_id_type=MESH)
    for copy in weights:
        copy.start()

    gain[...] = gain_h[...].astype(F32).reshape(1, 2048)
    shift[...] = shift_h[...].astype(F32).reshape(1, 2048)
    b_sum[...] = (b_out_h[...].astype(F32) + b_down_h[...].astype(F32)).reshape(1, 2048)
    rows_in[0].wait()
    x = tokens[...].astype(F32)
    mean = jnp.mean(x, axis=1, keepdims=True)
    centered = x - mean
    scale = lax.rsqrt(jnp.mean(centered * centered, axis=1, keepdims=True) + EPSILON)
    rstd[...] = jnp.broadcast_to(scale, (128, 128))
    mean_row[...] = jnp.broadcast_to(mean, (128, 128))

    rows_in[1].wait()
    pl.semaphore_wait(barrier, len(greeted))
    for c in range(Gather.AHEAD):
        gather.begin(c)

    seg_f = seg_row[...].astype(F32)
    seg_r[...] = jnp.broadcast_to(seg_f, (8, 1024))
    seg_c[...] = jnp.broadcast_to(seg_f, (128, 1024)).T
    @pl.loop(0, 4)
    def _(b):
        r = at_rows(b)
        i = lax.broadcasted_iota(jnp.int32, (256, 1024), 0) + b * 256
        j = lax.broadcasted_iota(jnp.int32, (256, 1024), 1)
        same = jnp.where((seg_c[r, 0:1] == seg_r[0:1, :]) & (j < i), 1.0, 0.0)
        position = jnp.sum(same, axis=1, keepdims=True)
        lane = lax.broadcasted_iota(jnp.int32, (256, 128), 1) % 64
        power = jnp.exp((lane % 16).astype(F32) * (-2.0 / ROT * 9.210340371976184))
        angle = position * power
        sine = jnp.sin(angle)
        cos_t[r, :] = jnp.where(lane < ROT, jnp.cos(angle), 1.0)
        sin_t[r, :] = jnp.where(lane < ROT // 2, -sine, jnp.where(lane < ROT, sine, 0.0))
        grad_mid[r, :] = jnp.zeros((256, MID), F32)
        pre[r, 0:1024] = jnp.broadcast_to(b_up_h[...].astype(F32).reshape(1, 1024), (256, 1024))
        for k in range(3):
            cols = slice(1024 + k * 256, 1280 + k * 256)
            pre[r, cols] = jnp.broadcast_to(b_qkv[k:k + 1, :].astype(F32), (256, 256))

    @pl.loop(0, 10)
    def _(i):
        gather.steps(i)

        @pl.when(i == 2)
        def _():
            for copy in weights[:4]:
                copy.wait()

        @pl.when(i >= 2)
        def _():
            c = i - 2

            @pl.loop(0, 2)
            def _(b):
                r = at_rows(b, 512)
                a = gather.all[c % 8, r, :]
                pre[r, :] += dot(a, w_in[at_rows(c), :])
            normed_t[at_rows(c), :] = gather.all[c % 8].T

    def gelu(b):
        r = at_rows(b)
        for k in range(4):
            cols = slice(k * 256, k * 256 + 256)
            u = pre[r, cols]
            a = (u * (0.5 * (1.0 + gelu_parts(u)))).astype(BF)
            mid[r, cols] = a
            act_t[cols, r] = a.T

    pl.loop(0, 2)(gelu)
    gather.steps(10)
    pl.loop(2, 4)(gelu)
    for copy in weights[4:]:
        copy.wait()

    def make_rows(b):
        r = at_rows(b)
        for k in range(3):
            for half in range(2):
                v = pre[r, 1024 + k * 256 + half * 128:1152 + k * 256 + half * 128]
                if k < 2:
                    v = turn(v, cos_t[r, :], sin_t[r, :])
                if k == 0:
                    v = v * HEAD_DIM ** -0.5
                v = v.astype(BF)
                cols = slice(half * 128, half * 128 + 128)
                if k > 0:
                    rows[k - 1, r, cols] = v
                turned[k, cols, r] = v.T

    def attend_bias(qb):
        cols = slice(qb * 256, qb * 256 + 256)
        for kb in range(qb + 1):
            r = slice(kb * 256, kb * 256 + 256)
            keep = seg_c[r, 0:1] == seg_r[0:1, cols]
            if kb == qb:
                i = lax.broadcasted_iota(jnp.int32, (256, 256), 0)
                j = lax.broadcasted_iota(jnp.int32, (256, 256), 1)
                keep = keep & (i <= j)
            bias[r, :] = jnp.where(keep, 0.0, -1e30).astype(BF)

    def head_rows(h, count=64):
        return pl.ds(pl.multiple_of(h * 64, 64), count)

    def two_heads(ref, source, pair, cols):
        ref[...] = jnp.zeros_like(ref)
        for k in range(2):
            hr = head_rows(pair * 2 + k)
            ref[hr, k * 256:k * 256 + 256] = source[hr, cols]

    def both(value):
        return jnp.concatenate([value, value], axis=1)

    def blocks(n):
        return [slice(b, b + 64) for b in range(0, n, 64)]

    def over_rows(op, value):
        return op(value.reshape(8, 8, 512), axis=0)

    def attend(qb, heads):
        cols = slice(qb * 256, qb * 256 + 256)
        n = (qb + 1) * 256
        if heads[0] == 0:
            attend_bias(qb)
        s_f = pre.at[:, pl.ds(1024, 512)]

        @pl.loop(heads[0] // 2, heads[1] // 2)
        def _(pair):
            two_heads(q_m, turned.at[0], pair, cols)
            s_f[0:n, :] = dot(rows[0, 0:n, :], q_m[...])
            most = jnp.full((8, 512), -jnp.inf, F32)
            for r in blocks(n):
                s = s_f[r, :] + both(bias[r, :].astype(F32))
                s_f[r, :] = s
                most = jnp.maximum(most, over_rows(jnp.max, s))
            most = jnp.max(most, axis=0, keepdims=True)
            total = jnp.zeros((8, 512), F32)
            for r in blocks(n):
                e = jnp.exp(s_f[r, :] - most)
                total = total + over_rows(jnp.sum, e)
                ds_b[r, :] = e.astype(BF)
            total = jnp.sum(total, axis=0, keepdims=True)
            share, log_total = 1.0 / total, most + jnp.log(total)
            out = dot(turned[2, head_rows(pair * 2, 128), 0:n], ds_b[0:n, :])
            for k in range(2):
                h, side = pair * 2 + k, slice(k * 256, k * 256 + 256)
                value = out[k * 64:k * 64 + 64, side] * share[:, side]
                out_f[head_rows(h), cols] = value
                heads_t[head_rows(h), cols] = value.astype(BF)
                lse[pl.ds(h, 1), cols] = log_total[:, side]

    def attend_back(qb, heads):
        cols = slice(qb * 256, qb * 256 + 256)
        n = (qb + 1) * 256
        if heads[0] == 0:
            attend_bias(qb)

        @pl.loop(heads[0] // 2, heads[1] // 2)
        def _(pair):
            pair_rows = head_rows(pair * 2, 128)
            two_heads(q_m, turned.at[0], pair, cols)
            two_heads(g_m, outs_gt, pair, cols)
            s_f[0:n, :] = dot(rows[0, 0:n, :], q_m[...])
            d_f[0:n, :] = dot(rows[1, 0:n, :], g_m[...])
            log_total = jnp.concatenate([lse[pl.ds(pair * 2 + k, 1), cols] for k in range(2)], axis=1)
            product = outs_gt[pair_rows, cols].astype(F32) * out_f[pair_rows, cols]
            delta = jnp.concatenate([jnp.sum(product[k * 64:k * 64 + 64], axis=0, keepdims=True)
                                     for k in range(2)], axis=1)
            for r in blocks(n):
                p = jnp.exp(s_f[r, :] + both(bias[r, :].astype(F32)) - log_total)
                p_b[r, :] = p.astype(BF)
                ds_b[r, :] = (p * (d_f[r, :] - delta)).astype(BF)
            q_2[...] = q_m[...].T
            g_2[...] = g_m[...].T
            grad_q = dot(turned[1, pair_rows, 0:n], ds_b[0:n, :])
            for k in range(2):
                pre[pl.ds(pl.multiple_of(qb * 256 + pair * 128 + k * 64, 64), 64), 1024:1280] = grad_q[
                    k * 64:k * 64 + 64, k * 256:k * 256 + 256]
            grad_v, grad_k = dot(p_b[0:n, :], g_2[...]), dot(ds_b[0:n, :], q_2[...])
            if (qb, heads) == UNITS[0]:
                pre[:, 1536:1792], pre[:, 1280:1536] = grad_v, grad_k
            else:
                pre[0:n, 1536:1792] += grad_v
                pre[0:n, 1280:1536] += grad_k

    @pl.loop(0, 8)
    def _(t):
        grads.steps(t)
        chunk = gather.all[t]
        grads.own[t % 2] = dot(act_t[:, 0:1024], chunk).astype(BF)
        grads.send_piece(t)
        gather.steps(11 + t)

        @pl.loop(0, 2)
        def _(b):
            r = at_rows(b, 512)
            grad_mid[r, :] += dot_nt(gather.all[t, r, :], w_mid[:, at_rows(t)])

        @pl.when(t < 2)
        def _():
            make_rows(2 * t)
            make_rows(2 * t + 1)

        for i, (qb, heads) in enumerate(UNITS):
            pl.when(t == 2 + i)(lambda qb=qb, heads=heads: attend(qb, heads))

    def branch_chunk(t, c):
        row_sum.store(t - RS, dot(mid[...], w_mid[:, at_rows(c)]))
        row_sum.send_chunk(t - RS)

    def normed_chunk(t, c):
        row_sum.store(t - RS, dot_nt(grad_feat[...], w_in[at_rows(c), :]))
        row_sum.send_chunk(t - RS)

    def gelu_back(k):
        @pl.loop(0, 4)
        def _(b):
            r, cols = at_rows(b), at_rows(k)
            u = pre[r, cols]
            th = gelu_parts(u)
            slope = 0.5 * (1.0 + th) + 0.5 * u * (1.0 - th * th) * (
                0.7978845608028654 * (1.0 + 3 * 0.044715 * (u * u)))
            grad_feat[r, cols] = (slope * grad_mid[r, cols]).astype(BF)

    def feature_piece(t):
        @pl.when(t % 2 == 0)
        def _():
            value = dot(normed_t[...], grad_feat[:, at_rows((t - 10) // 2)])
            for k in range(2):
                grads.own[k] = value[k * 1024:k * 1024 + 1024].astype(BF)

        grads.send_piece(t)

    @pl.loop(0, 4)
    def _(b):
        r = at_rows(b)
        outs_gt[:, r] = grad_mid[r, 1024:1280].astype(BF).T

    @pl.loop(8, 10)
    def _(t):
        grads.steps(t)
        for j in range(4):
            r = slice(j * 256, j * 256 + 256)
            grads.own[t % 2, r, :] = dot(heads_t[...], gather.all[4 * (t - 8) + j]).astype(BF)
        grads.send_piece(t)

        @pl.when(t == 8)
        def _():
            for k in range(4):
                gelu_back(k)

        @pl.when(t == 9)
        def _():
            attend_back(*UNITS[0])
            for b in range(4):
                r = slice(b * 256, b * 256 + 256)
                mid[r, 1024:1280] = heads_t[:, r].T


    @pl.loop(10, 14)
    def _(t):
        grads.steps(t)
        row_sum.steps(t - RS)
        feature_piece(t)
        branch_chunk(t, t - RS)
        for i, (qb, heads) in enumerate((UNITS[1], (2, (0, 4)), *UNITS[4:])):
            pl.when(t == 10 + i)(lambda qb=qb, heads=heads: attend_back(qb, heads))

    for b in range(4):
        r = slice(b * 256, b * 256 + 256)
        grad_q = pre[r, 1024:1280].T * HEAD_DIM ** -0.5
        for half in range(2):
            a = half * 128
            cosine, sine = cos_t[r, :], -sin_t[r, :]
            grad_feat[r, 1024 + a:1152 + a] = turn(grad_q[:, a:a + 128], cosine, sine).astype(BF)
            grad_feat[r, 1280 + a:1408 + a] = turn(pre[r, 1280 + a:1408 + a], cosine, sine).astype(BF)
        grad_feat[r, 1536:1792] = pre[r, 1536:1792].astype(BF)

    @pl.loop(14, 24)
    def _(t):
        grads.steps(t)
        row_sum.steps(t - RS)
        feature_piece(t)
        pl.when(t < 22)(lambda: normed_chunk(t, t - 14))
        pl.when(t >= 22)(lambda: branch_chunk(t, t - 18))

    def late_steps(t):
        grads.steps(t)
        row_sum.steps(t - RS)

    @pl.loop(24, 27)
    def _(t):
        late_steps(t)
        pl.when(t < 26)(lambda: branch_chunk(t, t - 18))

    def column_sum(value):
        return jnp.sum(value.astype(F32), axis=0, keepdims=True)

    mine = small.i1
    small.b1[mine] = jnp.zeros((8, 1024), F32)
    mean_plain = jnp.zeros((128, 1), F32)
    mean_unit = jnp.zeros((128, 1), F32)
    for c in range(8):
        cols = slice(c * 256, c * 256 + 256)
        row, lanes = c // 4, slice((c % 4) * 256, (c % 4) * 256 + 256)
        g = grad_n[c * 128:c * 128 + 128, :]
        n = unit(cols)
        scaled = g * gain[0:1, cols]
        mean_plain = mean_plain + jnp.sum(scaled, axis=1, keepdims=True)
        mean_unit = mean_unit + jnp.sum(scaled * n, axis=1, keepdims=True)
        small.b1[mine, row:row + 1, lanes] = column_sum(g * n)
        small.b1[mine, 2 + row:3 + row, lanes] = column_sum(g)
        small.b1[mine, 4 + row:5 + row, lanes] = column_sum(cotangent[:, cols])
    for k in range(7):
        row, lanes = 6 + k // 4, slice((k % 4) * 256, (k % 4) * 256 + 256)
        small.b1[mine, row:row + 1, lanes] = column_sum(grad_feat[:, k * 256:k * 256 + 256])
    small.start(0)
    late_steps(27)
    mean_plain = mean_plain / 2048.0
    mean_unit = mean_unit / 2048.0
    for c in range(8):
        cols = slice(c * 256, c * 256 + 256)
        inner = grad_n[c * 128:c * 128 + 128, :] * gain[0:1, cols] - mean_plain - unit(cols) * mean_unit
        input_grad[:, cols] = (cotangent[:, cols].astype(F32) + rstd[:, 0:1] * inner).astype(BF)

    rows_out[1].start()
    late_steps(28)
    small.second()
    late_steps(29)
    late_steps(30)
    rows_out[0].start()
    small.third()
    late_steps(31)
    late_steps(32)
    sums[...] = small.result()
    for copy in rows_out:
        copy.wait()
    late_steps(33)


def run_block(tokens, segment, ln_gain, ln_bias, w_qkv, b_qkv, w_out, b_out, w_up, b_up, w_down,
              b_down, cotangent):
    vmem = pl.BlockSpec(memory_space=pltpu.VMEM)
    hbm = pl.BlockSpec(memory_space=pl.ANY)
    V = pltpu.VMEM
    scratch = [
        V((128, 2048), BF), V((128, 2048), BF),
        V((128, 2048), BF), V((128, 2048), BF), pltpu.SemaphoreType.DMA((4,)),
        V((2048, FEAT), BF), V((MID, 2048), BF), pltpu.SemaphoreType.DMA((6,)),
        V((1, 2048), F32), V((1, 2048), F32), V((1, 2048), F32),
        V((2048, 1024), BF),
        V((1024, FEAT), F32), V((1024, MID), F32),
        V((2, 1024, 256), BF), V((3, 256, 1024), BF),
        V((1024, MID), BF), V((256, 1024), BF),
        V((256, 1024), BF),
        V((1024, FEAT), BF),
        V((1024, 128), F32), V((1024, 128), F32),
        V((1024, 128), F32), V((8, 1024), F32),
        V((8, 1024), F32),
        V((256, 1024), F32),
        V((256, 512), BF), V((256, 512), BF), V((1024, 512), BF),
        V((512, 256), BF), V((512, 256), BF),
        V((128, 128), F32), V((128, 128), F32),
    ] + GradSum.scratch() + Gather.scratch() + RowSum.scratch() + SmallSum.scratch()
    return pl.pallas_call(
        block_kernel,
        out_shape=(
            jax.ShapeDtypeStruct((NP, 1024, 256), BF),
            jax.ShapeDtypeStruct((128, 2048), BF),
            jax.ShapeDtypeStruct((128, 2048), BF),
            jax.ShapeDtypeStruct((8, 1024), F32),
        ),
        in_specs=[vmem] * 7 + [hbm] * 6,
        out_specs=(hbm, hbm, hbm, vmem),
        scratch_shapes=scratch,
        compiler_params=pltpu.CompilerParams(
            collective_id=0, has_side_effects=True, vmem_limit_bytes=VMEM_LIMIT),
        cost_estimate=pl.CostEstimate(flops=50 * 10**9, bytes_accessed=30 << 20, transcendentals=10**7),
    )(
        segment.reshape(1, 1024), ln_gain, ln_bias, b_qkv, b_out, b_up, b_down,
        tokens, cotangent, w_qkv.transpose(1, 0, 2), w_out, w_up, w_down,
    )


def widen_kernel(qkv_p, out_p, down_p, up_p, output, input_grad, sums,
                 down, out, up, qkv, output_o, input_grad_o, gain_o, shift_o, b_out_o, b_down_o, b_up_o, b_qkv_o):
    for c in range(8):
        cols = slice(c * 256, c * 256 + 256)
        down[:, cols] = down_p[c].astype(F32)
        out[:, cols] = out_p[c].astype(F32)
    for c in range(4):
        up[:, c * 256:c * 256 + 256] = up_p[c, 0].astype(F32)
    qkv[...] = qkv_p[...].astype(F32)
    output_o[...] = output[...]
    input_grad_o[...] = input_grad[...]

    @pl.when(pl.program_id(0) == 0)
    def _():
        gain_o[...] = sums[0:2, :].reshape(2048)
        shift_o[...] = sums[2:4, :].reshape(2048)
        b_out_o[...] = sums[4:6, :].reshape(2048)
        b_down_o[...] = sums[4:6, :].reshape(2048)
        b_up_o[...] = sums[6:7, :].reshape(1024)
        for c in range(3):
            b_qkv_o[c:c + 1, :] = sums[7:8, c * 256:c * 256 + 256]


def widen(pieces, output, input_grad, sums):
    def rows(count, width):
        return pl.BlockSpec((count, width), lambda i: (i, 0))

    def whole(*shape):
        return pl.BlockSpec(shape, lambda i: (0,) * len(shape))

    def shape(*dims, kind=F32):
        return jax.ShapeDtypeStruct(dims, kind)

    down, out, up, qkv, *rest = pl.pallas_call(
        widen_kernel,
        grid=(4,),
        out_shape=(
            shape(1024, 2048), shape(256, 2048), shape(2048, 1024), shape(6144, 256),
            shape(128, 2048, kind=BF), shape(128, 2048, kind=BF),
            shape(2048), shape(2048), shape(2048), shape(2048), shape(1024), shape(3, 256),
        ),
        in_specs=[
            rows(1536, 256),
            pl.BlockSpec((8, 64, 256), lambda i: (3, i, 0)),
            pl.BlockSpec((8, 256, 256), lambda i: (1, i, 0)),
            pl.BlockSpec((4, 1, 512, 256), lambda i: (2, i // 2, i % 2, 0)),
            rows(32, 2048), rows(32, 2048), whole(8, 1024),
        ],
        out_specs=(
            rows(256, 2048), rows(64, 2048), rows(512, 1024), rows(1536, 256),
            rows(32, 2048), rows(32, 2048),
            whole(2048), whole(2048), whole(2048), whole(2048), whole(1024), whole(3, 256),
        ),
        compiler_params=pltpu.CompilerParams(vmem_limit_bytes=VMEM_LIMIT),
    )(
        pieces.reshape(NP * 1024, 256), pieces.reshape(NP * 4, 256, 256), pieces,
        pieces.reshape(NP // 2, 2, 1024, 256), output, input_grad, sums,
    )
    return down, out, up, qkv.reshape(3, 2048, 256).transpose(1, 0, 2), rest


def on_device(*args):
    pieces, output, input_grad, sums = run_block(*args)
    down, out, up, qkv, rest = widen(pieces, output, input_grad, sums)
    output, input_grad, gain, shift, b_out, b_down, b_up, b_qkv = rest
    return output, input_grad, gain, shift, qkv, b_qkv, out, b_out, up, b_up, down, b_down


def solution(mesh):
    placed = (
        P(("dp", "tensor"), None),
        P("dp"),
        P(),
        P(),
        P(None, None, "tensor"),
        P(None, "tensor"),
        P("tensor", None),
        P(),
        P(None, "tensor"),
        P("tensor"),
        P("tensor", None),
        P(),
        P(("dp", "tensor"), None),
    )
    return jax.shard_map(
        on_device,
        mesh=mesh,
        in_specs=placed,
        out_specs=(
            P(("dp", "tensor"), None),
            P(("dp", "tensor"), None),
            P(),
            P(),
            P(None, None, "tensor"),
            P(None, "tensor"),
            P("tensor", None),
            P(),
            P(None, "tensor"),
            P("tensor"),
            P("tensor", None),
            P(),
        ),
        check_vma=False,
    )
```
